32 devices in a mesh: dp: 8 (over y, x, core), gene: 4 (over z).
Axes of the slice: x: 2, y: 2, z: 4, core: 2. Of those that a mesh axis runs over, the one named last changes fastest.
Arguments:
- gene_counts: bfloat16 [4096, 13500], P('dp', 'gene'), may hold values from -6 to 6
- coords: float32 [2, 4096], P(None, ('dp', 'gene')), may hold values from 0 to 100
- lengths: int32 [8, 2], P('dp'), may hold values from 0 to 512, as said below
- enc_weight: bfloat16 [13500, 1024], P('gene'), may hold values from -0.0546875 to 0.0546875
- dec_weight: bfloat16 [1024, 13500], P(None, 'gene'), may hold values from -0.1875 to 0.1875
- attn_weight: bfloat16 [4096, 1024], P(('dp', 'gene'))
- up_weight: bfloat16 [4096, 1024], P(('dp', 'gene')), may hold values from -0.1875 to 0.1875
- down_weight: bfloat16 [4096, 1024], P(('dp', 'gene')), may hold values from -0.09375 to 0.09375
- ln_gain: bfloat16 [2048], P(('dp', 'gene')), may hold values from 0.5 to 1.5
- ln_bias: bfloat16 [2048], P(('dp', 'gene')), may hold values from -1.5 to 1.5
- logit_grad: bfloat16 [4096, 13500], P('dp', 'gene'), may hold values from -6 to 6
Outputs:
- logits: bfloat16 [4096, 13500], P('dp', 'gene')
- gene_grad: bfloat16 [4096, 13500], P('dp', 'gene')
- enc_grad: float32 [13500, 1024], P('gene', 'dp')
- dec_grad: float32 [1024, 13500], P('dp', 'gene')
- attn_grad: float32 [4096, 1024], P(('dp', 'gene'))
- up_grad: float32 [4096, 1024], P(('dp', 'gene'))
- down_grad: float32 [4096, 1024], P(('dp', 'gene'))
- gain_grad: float32 [2048], P(('dp', 'gene'))
- bias_grad: float32 [1024], P(('dp', 'gene'))
- mid_bias_grad: float32 [1024], P(('dp', 'gene'))
The draws below stay inside these ranges and needn't reach their ends.
Inputs may be any that keep to these rules, and one draw needn't show every extreme that they name: Per group the two lengths and the padding fill 4 * 128 slots; one of the two slides covers the group's slots from below 128 to beyond 3 * 128.
All inputs are finite; a program needn't handle non-finite values.
Results may differ from the reference program's by a relative error of at most 0.03.
Values may be sent and summed in bfloat16 or wider, within the bound.
A program may use at most 192 MiB of HBM per device.

```python
import math
import jax
import jax.numpy as jnp
from jax import lax

D = 1024
FF = 4096
HEADS = 16
HEAD_DIM = 64
GENES = 13500
CELLS_DEV = 128
GROUPS = 8
CELLS = 4096


def draw_lengths(key, part):
    key = jax.random.fold_in(key, 11)
    key_short, key_spare, key_chosen, key_order = jax.random.split(key, 4)
    capacity = 4 * CELLS_DEV
    smaller = jax.random.randint(key_short, (GROUPS,), 0, CELLS_DEV // 2 + 1)
    padding = jax.random.randint(key_spare, (GROUPS,), 0, CELLS_DEV // 2)
    chosen = jax.random.randint(key_chosen, (), 0, GROUPS)
    single = jnp.arange(GROUPS) == chosen
    smaller = jnp.where(single, 0, smaller)
    padding = jnp.where(single, 0, padding)
    larger = capacity - smaller - padding
    flipped = jax.random.randint(key_order, (GROUPS,), 0, 2)
    leading = jnp.where(flipped == 1, larger, smaller)
    trailing = jnp.where(flipped == 1, smaller, larger)
    return jnp.stack([leading, trailing], axis=1).astype(jnp.int32)


def draw_attn_weight(key, part):
    key = jax.random.fold_in(key, 23)
    values = jax.random.normal(key, (4 * D, D), jnp.float32)
    row_index = jnp.arange(4 * D)[:, None]
    spread = jnp.where(row_index < 3 * D, D ** (-0.5), max(1, D // (4 * CELLS_DEV)) ** (-0.5))
    return (values * spread).astype(jnp.bfloat16)


def shard_levels(own_key, shape, cuts, least, largest):
    level, own = 1.0, jax.random.fold_in(own_key, 6)
    for dim, blocks in cuts:
        heights = jnp.exp(jax.random.uniform(jax.random.fold_in(own, dim), (blocks,), jnp.float32, least / len(cuts), largest / len(cuts)))
        level = level * jnp.repeat(heights, shape[dim] // blocks).reshape([-1 if axis == dim else 1 for axis in range(len(shape))])
    return level


def noise(key, shape, deviation, limit, cuts=(), kind=jnp.bfloat16):
    result = deviation * jax.random.normal(key, shape, jnp.float32)
    if cuts:
        result = result * shard_levels(key, shape, cuts, -0.22, 0.18)
    return jnp.clip(result, -limit, limit).astype(kind)


def setup_inputs(seed: int = 0) -> dict:
    keys = jax.random.split(jax.random.key(seed), 12)
    gene_counts = noise(keys[0], (CELLS, GENES), 1.0, 6.0, ((0, 8), (1, 4)))
    coords = jnp.clip(100.0 * jax.random.uniform(keys[1], (2, CELLS), jnp.float32) ** shard_levels(keys[1], (2, CELLS), ((1, 32),), -0.2, 0.2), 0.0, 100.0)
    lengths = draw_lengths(jax.random.fold_in(keys[11], 71), 0)
    enc_weight = noise(keys[3], (GENES, D), GENES ** -0.5, 0.0546875, ((0, 4),))
    dec_weight = noise(keys[4], (D, GENES), D ** -0.5, 0.1875, ((1, 4),))
    attn_weight = draw_attn_weight(jax.random.fold_in(keys[11], 71), 0)
    up_weight = noise(keys[6], (FF, D), D ** -0.5, 0.1875, ((0, 32),))
    down_weight = noise(keys[7], (FF, D), FF ** -0.5, 0.09375, ((0, 32),))
    ln_gain = jnp.clip(1.0 + 0.1 * jax.random.normal(keys[8], (2 * D,), jnp.float32), 0.5, 1.5).astype(jnp.bfloat16)
    ln_bias = noise(keys[9], (2 * D,), 0.3, 1.5, ((0, 32),))
    logit_grad = noise(keys[10], (CELLS, GENES), 1.0, 6.0, ((0, 8), (1, 4)))
    return dict(gene_counts=gene_counts, coords=coords, lengths=lengths, enc_weight=enc_weight, dec_weight=dec_weight, attn_weight=attn_weight, up_weight=up_weight, down_weight=down_weight, ln_gain=ln_gain, ln_bias=ln_bias, logit_grad=logit_grad)


@jax.custom_vjp
def low(v):
    return lax.optimization_barrier(v.astype(jnp.bfloat16)).astype(jnp.float32)

@jax.custom_vjp
def low_back(v):
    return v

def low_keep(v):
    return (low(v), None)

def low_pass(kept, grad):
    return (grad,)

def back_keep(v):
    return (v, None)

def back_low(kept, grad):
    return (low(grad),)
low.defvjp(low_keep, low_pass)
low_back.defvjp(back_keep, back_low)
epsilon = 1e-05

def matmul(left, right):
    return jnp.dot(left, right, precision=lax.Precision.HIGHEST)

def matmul_tr(left, right):
    return lax.dot_general(left, right, (((1,), (1,)), ((), ())), precision=lax.Precision.HIGHEST)

def norm_rows(values, gain, offset):
    center = values - lax.optimization_barrier(jnp.mean(values, axis=-1, keepdims=True))
    spread = lax.optimization_barrier(jnp.mean(center * center, axis=-1, keepdims=True))
    return center * lax.rsqrt(spread + epsilon) * gain + offset

def gelu_tanh(values):
    return jax.nn.gelu(values, approximate=True)

def positions(coords, model_width):
    indices = jnp.arange(model_width // 4).astype(coords.dtype)
    freqs = jnp.exp(indices * (-4.0 * math.log(10000.0) / model_width))
    along_x = coords[0][:, None] * freqs[None, :]
    along_y = coords[1][:, None] * freqs[None, :]
    return jnp.concatenate([jnp.sin(along_x), jnp.cos(along_x), jnp.sin(along_y), jnp.cos(along_y)], axis=1)

def slide_ids(slide_lengths, length_all):
    places = jnp.arange(length_all, dtype=jnp.int32)
    return (places >= slide_lengths[0]).astype(jnp.int32) + (places >= slide_lengths[0] + slide_lengths[1]).astype(jnp.int32)

def forward(cell_rows, enc_w, dec_w, attn_w, up_w, down_w, norm_gains, offsets, posit, slide, live):
    row_total = cell_rows.shape[0]
    score_scale = 1.0 / math.sqrt(HEAD_DIM)
    embedded = low_back(matmul(cell_rows, enc_w))
    stream_in = embedded + posit
    first_normed = low(norm_rows(stream_in, norm_gains[:D], offsets[:D]))
    projected = low(low_back(matmul_tr(first_normed, attn_w[:3 * D])))
    queries = projected[:, :D].reshape(row_total, HEADS, HEAD_DIM)
    keys_all = projected[:, D:2 * D].reshape(row_total, HEADS, HEAD_DIM)
    values_all = projected[:, 2 * D:].reshape(row_total, HEADS, HEAD_DIM)
    scores = low_back(jnp.einsum('qhd,khd->hqk', queries, keys_all, precision=lax.Precision.HIGHEST) * score_scale)
    same_slide = (slide[:, None] == slide[None, :])[None]
    scores = jnp.where(same_slide, scores, -1e+30)
    soft = low(jax.nn.softmax(scores, axis=-1))
    attended = jnp.einsum('hqk,khd->qhd', soft, values_all, precision=lax.Precision.HIGHEST).reshape(row_total, D)
    attended = low(low_back(attended))
    stream_mid = stream_in + low_back(matmul(attended, attn_w[3 * D:]))
    second_normed = low(norm_rows(stream_mid, norm_gains[D:], offsets[D:]))
    hidden_pre = low_back(matmul_tr(second_normed, up_w))
    active = low(gelu_tanh(hidden_pre))
    stream_out = stream_mid + low_back(matmul(active, down_w))
    return matmul(low(stream_out), dec_w) * live[:, None]

def reference(gene_counts, coords, lengths, enc_weight, dec_weight, attn_weight, up_weight, down_weight, ln_gain, ln_bias, logit_grad):
    group_count = lengths.shape[0]
    group_rows = gene_counts.shape[0] // group_count
    counts_all = gene_counts.astype(jnp.float32).reshape(group_count, group_rows, GENES)
    cotangent = logit_grad.astype(jnp.float32).reshape(group_count, group_rows, GENES)
    placed = coords.reshape(2, group_count, group_rows).transpose(1, 0, 2)
    weights = (enc_weight.astype(jnp.float32), dec_weight.astype(jnp.float32), attn_weight.astype(jnp.float32), up_weight.astype(jnp.float32), down_weight.astype(jnp.float32), ln_gain.astype(jnp.float32), ln_bias.astype(jnp.float32))

    def one_group(running, item):
        cell_rows, cot_rows, where_rows, slide_lengths = item
        slide = slide_ids(slide_lengths, group_rows)
        live = (slide < 2).astype(cell_rows.dtype)
        posit = positions(where_rows, D)

        def run(cells_in, enc_w, dec_w, attn_w, up_w, down_w, norm_gains, offsets):
            return forward(cells_in, enc_w, dec_w, attn_w, up_w, down_w, norm_gains, offsets, posit, slide, live)
        outputs, pull = jax.vjp(run, cell_rows, *weights)
        grads = pull(cot_rows)
        running = tuple((acc + new for acc, new in zip(running, grads[1:])))
        return (running, (outputs.astype(jnp.bfloat16), grads[0].astype(jnp.bfloat16)))
    initial = tuple((jnp.zeros_like(weight_item) for weight_item in weights))
    totals, (logit_rows, grad_rows) = lax.scan(one_group, initial, (counts_all, cotangent, placed, lengths))
    logits = logit_rows.reshape(group_count * group_rows, GENES)
    gene_grad = grad_rows.reshape(group_count * group_rows, GENES)
    return (logits, gene_grad, totals[0], totals[1], totals[2], totals[3], totals[4], totals[5], totals[6][:D], totals[6][D:])
```

```python
import functools
import math

import jax
import jax.numpy as jnp
from jax import lax
from jax.experimental import pallas as pl
from jax.experimental.pallas import tpu as pltpu
from jax.sharding import PartitionSpec as P

HEADS = 16
HEAD_DIM = 64


epsilon = 1e-05


def norm_rows(values, gain, offset):
    center = values - jnp.mean(values, axis=-1, keepdims=True)
    spread = jnp.mean(center * center, axis=-1, keepdims=True)
    return center * lax.rsqrt(spread + epsilon) * gain + offset


def gelu_tanh(values):
    return jax.nn.gelu(values, approximate=True)


def positions(coords, model_width):
    indices = jnp.arange(model_width // 4).astype(coords.dtype)
    freqs = jnp.exp(indices * (-4.0 * math.log(10000.0) / model_width))
    along_x = coords[0][:, None] * freqs[None, :]
    along_y = coords[1][:, None] * freqs[None, :]
    return jnp.concatenate(
        [jnp.sin(along_x), jnp.cos(along_x), jnp.sin(along_y), jnp.cos(along_y)], axis=1
    )


def slide_ids(slide_lengths, length_all):
    places = jnp.arange(length_all, dtype=jnp.int32)
    return (places >= slide_lengths[0]).astype(jnp.int32) + (
        places >= slide_lengths[0] + slide_lengths[1]
    ).astype(jnp.int32)


def product(left, right):
    return jnp.dot(left, right, preferred_element_type=jnp.float32)


def contract_rows(left, right):
    return lax.dot_general(
        left, right, (((0,), (0,)), ((), ())), preferred_element_type=jnp.float32
    )


def contract_cols(left, right):
    return lax.dot_general(
        left, right, (((1,), (1,)), ((), ())), preferred_element_type=jnp.float32
    )


def body(
    gene_counts,
    coords,
    lengths,
    enc_weight,
    dec_weight,
    attn_weight,
    up_weight,
    down_weight,
    ln_gain,
    ln_bias,
    logit_grad,
):
    model_width = enc_weight.shape[1]
    group_rows = gene_counts.shape[0]
    own_rows = coords.shape[1]
    gene_index = lax.axis_index("gene")
    score_scale = 1.0 / math.sqrt(HEAD_DIM)
    slide_all = slide_ids(lengths[0], group_rows)
    slide_own = lax.dynamic_slice_in_dim(slide_all, gene_index * own_rows, own_rows)
    live_rows = (slide_all < 2).astype(jnp.bfloat16)[:, None]
    attn_full, up_full, down_full, gain_full, bias_full = (
        lax.all_gather(attn_weight, ("dp", "gene"), axis=0, tiled=True),
        lax.all_gather(up_weight, ("dp", "gene"), axis=0, tiled=True),
        lax.all_gather(down_weight, ("dp", "gene"), axis=0, tiled=True),
        lax.all_gather(ln_gain, ("dp", "gene"), axis=0, tiled=True),
        lax.all_gather(ln_bias, ("dp", "gene"), axis=0, tiled=True),
    )
    norm_gains = gain_full.astype(jnp.float32)
    offsets = bias_full.astype(jnp.float32)
    proj_weight = attn_full[: 3 * model_width]
    out_weight = attn_full[3 * model_width :]
    embedded = lax.psum_scatter(
        product(gene_counts, enc_weight).astype(jnp.bfloat16),
        "gene",
        scatter_dimension=0,
        tiled=True,
    ).astype(jnp.float32)
    stream_in = embedded + positions(coords, model_width)
    first_normed, first_pull = jax.vjp(
        norm_rows, stream_in, norm_gains[:model_width], offsets[:model_width]
    )
    first_low = first_normed.astype(jnp.bfloat16)
    projected = contract_cols(first_low, proj_weight).astype(jnp.bfloat16)
    queries = projected[:, :model_width].reshape(own_rows, HEADS, HEAD_DIM)
    keyval_all = lax.all_gather(projected[:, model_width:], "gene", axis=0, tiled=True)
    keys_all = keyval_all[:, :model_width].reshape(group_rows, HEADS, HEAD_DIM)
    values_all = keyval_all[:, model_width:].reshape(group_rows, HEADS, HEAD_DIM)
    same_slide = (slide_own[:, None] == slide_all[None, :])[None]
    scores = (
        jnp.einsum("qhd,khd->hqk", queries, keys_all, preferred_element_type=jnp.float32)
        * score_scale
    )
    scores = jnp.where(same_slide, scores, -1e30)
    row_max = jnp.max(scores, axis=-1, keepdims=True)
    raised = jnp.exp(scores - row_max)
    soft = raised / jnp.sum(raised, axis=-1, keepdims=True)
    soft_low = soft.astype(jnp.bfloat16)
    attended = jnp.einsum("hqk,khd->qhd", soft_low, values_all, preferred_element_type=jnp.float32)
    attended = attended.reshape(own_rows, model_width).astype(jnp.bfloat16)
    stream_mid = stream_in + product(attended, out_weight)
    second_normed, second_pull = jax.vjp(
        norm_rows, stream_mid, norm_gains[model_width:], offsets[model_width:]
    )
    second_low = second_normed.astype(jnp.bfloat16)
    hidden_pre = contract_cols(second_low, up_full)
    active, gelu_pull = jax.vjp(gelu_tanh, hidden_pre)
    active_low = active.astype(jnp.bfloat16)
    stream_out = stream_mid + product(active_low, down_full)
    cells_low = stream_out.astype(jnp.bfloat16)
    cells_all = lax.all_gather(cells_low, "gene", axis=0, tiled=True)
    logits_full = product(cells_all, dec_weight)
    logits = (logits_full * live_rows.astype(jnp.float32)).astype(jnp.bfloat16)
    masked_grad = logit_grad * live_rows
    grad_out = lax.psum_scatter(
        contract_cols(masked_grad, dec_weight).astype(jnp.bfloat16),
        "gene",
        scatter_dimension=0,
        tiled=True,
    ).astype(jnp.float32)
    dec_part = contract_rows(cells_all, masked_grad)
    grad_branch = grad_out.astype(jnp.bfloat16)
    down_part = contract_rows(active_low, grad_branch)
    grad_active = contract_cols(grad_branch, down_full)
    grad_hidden = gelu_pull(grad_active)[0].astype(jnp.bfloat16)
    up_part = contract_rows(grad_hidden, second_low)
    grad_second = product(grad_hidden, up_full)
    grad_mid_norm, gain_second, bias_second = second_pull(grad_second)
    grad_mid = grad_out + grad_mid_norm
    grad_attn = grad_mid.astype(jnp.bfloat16)
    out_part = contract_rows(attended, grad_attn)
    grad_attended = (
        contract_cols(grad_attn, out_weight).astype(jnp.bfloat16).reshape(own_rows, HEADS, HEAD_DIM)
    )
    grad_soft = jnp.einsum(
        "qhd,khd->hqk", grad_attended, values_all, preferred_element_type=jnp.float32
    )
    grad_scores = soft * (grad_soft - jnp.sum(grad_soft * soft, axis=-1, keepdims=True))
    grad_scores = grad_scores.astype(jnp.bfloat16)
    grad_query = (
        jnp.einsum("hqk,khd->qhd", grad_scores, keys_all, preferred_element_type=jnp.float32)
        * score_scale
    )
    grad_query = grad_query.reshape(own_rows, model_width).astype(jnp.bfloat16)
    grad_keys = (
        jnp.einsum("hqk,qhd->khd", grad_scores, queries, preferred_element_type=jnp.float32)
        * score_scale
    )
    grad_values = jnp.einsum(
        "hqk,qhd->khd", soft_low, grad_attended, preferred_element_type=jnp.float32
    )
    keyval_part = jnp.concatenate(
        [grad_keys.reshape(group_rows, model_width), grad_values.reshape(group_rows, model_width)],
        axis=1,
    )
    grad_keyval = lax.psum_scatter(
        keyval_part.astype(jnp.bfloat16), "gene", scatter_dimension=0, tiled=True
    )
    grad_proj = jnp.concatenate([grad_query, grad_keyval], axis=1)
    proj_part = contract_rows(grad_proj, first_low)
    grad_first = product(grad_proj, proj_weight)
    grad_in_norm, gain_first, bias_first = first_pull(grad_first)
    grad_in = (grad_mid + grad_in_norm).astype(jnp.bfloat16)
    grad_in_all = lax.all_gather(grad_in, "gene", axis=0, tiled=True)
    gene_grad = contract_cols(grad_in_all, enc_weight).astype(jnp.bfloat16)
    enc_part = contract_rows(gene_counts, grad_in_all)
    enc_grad, dec_grad = (
        lax.psum_scatter(enc_part, "dp", scatter_dimension=1, tiled=True),
        lax.psum_scatter(dec_part, "dp", scatter_dimension=0, tiled=True),
    )
    attn_part = jnp.concatenate([proj_part, out_part], axis=0)
    gain_part = jnp.concatenate([gain_first, gain_second], axis=0)
    attn_grad, up_grad, down_grad, gain_grad, bias_grad, mid_bias_grad = (
        lax.psum_scatter(attn_part, ("dp", "gene"), scatter_dimension=0, tiled=True),
        lax.psum_scatter(up_part, ("dp", "gene"), scatter_dimension=0, tiled=True),
        lax.psum_scatter(down_part, ("dp", "gene"), scatter_dimension=0, tiled=True),
        lax.psum_scatter(gain_part, ("dp", "gene"), scatter_dimension=0, tiled=True),
        lax.psum_scatter(bias_first, ("dp", "gene"), scatter_dimension=0, tiled=True),
        lax.psum_scatter(bias_second, ("dp", "gene"), scatter_dimension=0, tiled=True),
    )
    return (
        logits,
        gene_grad,
        enc_grad,
        dec_grad,
        attn_grad,
        up_grad,
        down_grad,
        gain_grad,
        bias_grad,
        mid_bias_grad,
    )


MESH = pl.DeviceIdType.MESH
MIB = 2**20
VMEM = pl.BlockSpec(memory_space=pltpu.VMEM)
SMEM = pl.BlockSpec(memory_space=pltpu.SMEM)
ANY = pl.BlockSpec(memory_space=pl.ANY)
DMA = pltpu.SemaphoreType.DMA


class Place:
    def __init__(self):
        self.dp = dp = lax.axis_index("dp")
        self.z = z = lax.axis_index("gene")
        self.core = dp % 2
        self.chip = dp // 2
        self.inner = z * (3 - z) > 0
        self.outer = z * (3 - z) == 0
        self.pair = (dp, z + 1 - 2 * (z % 2))
        self.middle = (dp, 3 - z)
        self.sibling_dp = dp + 1 - 2 * (dp % 2)
        self.x_dp = dp + 2 - 4 * ((dp // 2) % 2)
        self.y_dp = dp + 4 - 8 * (dp // 4)
        self.xy_dp = self.x_dp + 4 - 8 * (dp // 4)
        self.sibling = (self.sibling_dp, z)
        self.far_dps = (self.x_dp, self.y_dp, self.xy_dp)
        self.far = tuple((d, z) for d in self.far_dps)
        self.line = tuple((dp, (z + k) % 4) for k in (1, 2, 3))

    def meet(self, devices):
        barrier = pltpu.get_barrier_semaphore()
        for device in devices:
            pl.semaphore_signal(barrier, inc=1, device_id=device, device_id_type=MESH)
        pl.semaphore_wait(barrier, len(devices))

    def meet_line(self):
        barrier = pltpu.get_barrier_semaphore()
        pl.semaphore_signal(barrier, inc=1, device_id=self.pair, device_id_type=MESH)

        @pl.when(self.inner)
        def _():
            pl.semaphore_signal(barrier, inc=1, device_id=self.middle, device_id_type=MESH)
            pl.semaphore_wait(barrier, 2)

        @pl.when(self.outer)
        def _():
            pl.semaphore_wait(barrier, 1)


def send(src, dst, send_sem, recv_sem, device):
    return pltpu.make_async_remote_copy(
        src_ref=src,
        dst_ref=dst,
        send_sem=send_sem,
        recv_sem=recv_sem,
        device_id=device,
        device_id_type=MESH,
    )


class LineSum:
    SEMS = 6

    def __init__(self, place, part, inbox, peer, total, sems, view):
        self.place, self.part, self.inbox, self.peer, self.total = place, part, inbox, peer, total
        self.sems, self.view = sems, view

    def up(self, k):
        s, v = self.sems, self.view
        return send(v(self.part, k), v(self.inbox, k), s.at[0, k], s.at[1, k], self.place.pair)

    def across(self, k):
        s, v = self.sems, self.view
        return send(v(self.part, k), v(self.peer, k), s.at[2, k], s.at[3, k], self.place.middle)

    def down(self, k):
        s, v = self.sems, self.view
        return send(v(self.total, k), v(self.total, k), s.at[4, k], s.at[5, k], self.place.pair)

    def push(self, k):
        @pl.when(self.place.outer)
        def _():
            self.up(k).start()

    def meet_up(self, k):
        @pl.when(self.place.inner)
        def _():
            self.up(k).wait_recv()
            mine, other = self.view(self.part, k), self.view(self.inbox, k)
            mine[...] = (mine[...].astype(jnp.float32) + other[...].astype(jnp.float32)).astype(
                jnp.bfloat16
            )
            self.across(k).start()

    def meet_across(self, k):
        @pl.when(self.place.inner)
        def _():
            self.across(k).wait_recv()
            mine, other = self.view(self.part, k), self.view(self.peer, k)
            self.view(self.total, k)[...] = (
                mine[...].astype(jnp.float32) + other[...].astype(jnp.float32)
            ).astype(jnp.bfloat16)
            self.down(k).start()

    def get(self, k):
        @pl.when(self.place.outer)
        def _():
            self.down(k).wait_recv()

    def finish(self, count):
        @pl.when(self.place.outer)
        def _():
            for k in range(count):
                self.up(k).wait_send()

        @pl.when(self.place.inner)
        def _():
            for k in range(count):
                self.across(k).wait_send()
                self.down(k).wait_send()


def chunk(ref, k):
    return ref.at[k]


def columns(ref, k, width):
    return ref.at[:, pl.ds(k * width, width)]


def row_live(lengths, rows):
    index = lax.broadcasted_iota(jnp.int32, (rows, 1), 0)
    return (index < lengths[0, 0] + lengths[0, 1]).astype(jnp.float32)


def encode_kernel(
    coords,
    lengths,
    counts,
    enc,
    grads,
    dec,
    attn,
    up,
    down,
    gain,
    bias,
    stream,
    grad_out,
    weights,
    vectors,
    counts_v,
    enc_v,
    grads_v,
    dec_v,
    work,
    places,
    part_a,
    inbox_a,
    peer_a,
    part_b,
    inbox_b,
    peer_b,
    load_sems,
    sems_a,
    sems_b,
    far_sems,
    side_sems,
    line_sems,
):
    place = Place()
    dp, z = place.dp, place.z
    chunks, rows, lanes = stream.shape
    width = chunks * lanes
    step = width // 4
    loads = [pltpu.make_async_copy(counts, counts_v, load_sems.at[0])]
    for j in range(4):
        loads.append(
            pltpu.make_async_copy(
                columns(enc, j, step), columns(enc_v, j, step), load_sems.at[1 + j]
            )
        )
    loads.append(pltpu.make_async_copy(grads, grads_v, load_sems.at[5]))
    for j in range(4):
        loads.append(
            pltpu.make_async_copy(
                columns(dec, j, step), columns(dec_v, j, step), load_sems.at[6 + j]
            )
        )
    for copy in loads:
        copy.start()
    for i, ref in enumerate((attn, up, down)):
        weights[i, dp] = ref[...]
    place.meet(place.far + (place.sibling,) + place.line)

    tile = vectors.at[dp * 4 + z]
    tile[...] = jnp.zeros_like(tile)
    tile[0:1, 0:64] = gain[...].astype(jnp.float32)
    tile[1:2, 0:64] = bias[...].astype(jnp.float32)
    line_out = [
        send(tile, tile, line_sems.at[0, i], line_sems.at[1, i], device)
        for i, device in enumerate(place.line)
    ]
    for copy in line_out:
        copy.start()

    def block_of(d):
        return weights.at[:, d]

    far_out = [
        send(block_of(dp), block_of(dp), far_sems.at[0, i], far_sems.at[1, i], device)
        for i, device in enumerate(place.far)
    ]
    far_in = [
        send(block_of(d), block_of(d), far_sems.at[0, i], far_sems.at[1, i], device)
        for i, (d, device) in enumerate(zip(place.far_dps, place.far))
    ]
    side_from = (dp,) + place.far_dps
    side = [
        send(block_of(d), block_of(d), side_sems.at[0, i], side_sems.at[1, i], place.sibling)
        for i, d in enumerate(side_from)
    ]
    for copy in far_out:
        copy.start()
    side[0].start()

    def lines(d):
        return vectors.at[pl.ds(d * 4, 4)]

    vec_far = [
        send(lines(dp), lines(dp), far_sems.at[2, i], far_sems.at[3, i], device)
        for i, device in enumerate(place.far)
    ]
    vec_side = [
        send(lines(d), lines(d), side_sems.at[2, i], side_sems.at[3, i], place.sibling)
        for i, d in enumerate(side_from)
    ]

    own_rows = coords.shape[1]
    index = lax.broadcasted_iota(jnp.int32, (1, step), 1).astype(jnp.float32)
    freqs = jnp.exp(index * (-4.0 * math.log(10000.0) / width))
    for axis in range(2):
        along = jnp.broadcast_to(coords[axis : axis + 1, :], (own_rows, own_rows)).T
        angle = along[:, 0:1] * freqs
        places[2 * axis] = jnp.sin(angle)
        places[2 * axis + 1] = jnp.cos(angle)

    sum_a = LineSum(place, part_a, inbox_a, peer_a, stream, sems_a, chunk)
    sum_b = LineSum(place, part_b, inbox_b, peer_b, grad_out, sems_b, chunk)
    live = row_live(lengths, rows)
    own = pl.ds(pl.multiple_of(z * own_rows, own_rows), own_rows)
    per = step // lanes

    def encode(j):
        if j == 0:
            loads[0].wait()
        loads[1 + j].wait()
        work[...] = contract_rows(counts_v[...], enc_v[:, j * step : (j + 1) * step])
        work[own, :] += places[j]
        for k in range(per):
            part_a[j * per + k] = work[:, k * lanes : (k + 1) * lanes].astype(jnp.bfloat16)
            sum_a.push(j * per + k)

    def decode(j):
        if j == 0:
            loads[5].wait()
        loads[6 + j].wait()
        got = contract_rows(grads_v[...], dec_v[:, j * step : (j + 1) * step]) * live
        for k in range(per):
            part_b[j * per + k] = got[:, k * lanes : (k + 1) * lanes].astype(jnp.bfloat16)
            sum_b.push(j * per + k)

    produce = [functools.partial(encode, j) for j in range(4)]
    produce += [functools.partial(decode, j) for j in range(4)]
    ups = [functools.partial(sum_a.meet_up, k) for k in range(8)]
    ups += [functools.partial(sum_b.meet_up, k) for k in range(8)]
    acrosses = [functools.partial(sum_a.meet_across, k) for k in range(8)]
    acrosses += [functools.partial(sum_b.meet_across, k) for k in range(8)]

    def vectors_out():
        for copy in line_out:
            copy.wait_recv()
        for copy in vec_far + vec_side[:1]:
            copy.start()

    def weights_on():
        for i in range(3):
            far_in[i].wait_recv()
            side[1 + i].start()
            vec_far[i].wait_recv()
            vec_side[1 + i].start()

    made = 0
    for k in range(17):
        while made < 8 and made * per < k + per + 2:
            produce[made]()
            made += 1
        if k < 16:
            ups[k]()
        if k == 4:
            vectors_out()
        if k == 13:
            weights_on()
        if k >= 1:
            acrosses[k - 1]()
    for k in range(8):
        sum_a.get(k)
    for k in range(8):
        sum_b.get(k)
    sum_a.finish(8)
    sum_b.finish(8)
    for copy in line_out:
        copy.wait_send()
    for copy in far_out + vec_far:
        copy.wait_send()
    for copy in side + vec_side:
        copy.wait()


def encode_call(coords, lengths, counts, enc, grads, dec, attn, up, down, gain, bias):
    genes, rows = counts.shape
    width = enc.shape[1]
    low, full = jnp.bfloat16, jnp.float32
    block = pltpu.VMEM((width // 128, rows, 128), low)
    return pl.pallas_call(
        encode_kernel,
        out_shape=(
            jax.ShapeDtypeStruct((width // 128, rows, 128), low),
            jax.ShapeDtypeStruct((width // 128, rows, 128), low),
            jax.ShapeDtypeStruct((3, 8) + attn.shape, low),
            jax.ShapeDtypeStruct((32, 8, 128), full),
        ),
        in_specs=[VMEM, SMEM, ANY, ANY, ANY, ANY, VMEM, VMEM, VMEM, VMEM, VMEM],
        out_specs=(VMEM, VMEM, VMEM, VMEM),
        scratch_shapes=[
            pltpu.VMEM((genes, rows), low),
            pltpu.VMEM((genes, width), low),
            pltpu.VMEM((genes, rows), low),
            pltpu.VMEM((genes, width), low),
            pltpu.VMEM((rows, width // 4), full),
            pltpu.VMEM((4, coords.shape[1], width // 4), full),
            block,
            block,
            block,
            block,
            block,
            block,
            DMA((10,)),
            DMA((6, 8)),
            DMA((6, 8)),
            DMA((4, 3)),
            DMA((4, 4)),
            DMA((2, 3)),
        ],
        compiler_params=pltpu.CompilerParams(
            collective_id=0, has_side_effects=True, vmem_limit_bytes=56 * MIB
        ),
        name="encode",
    )(coords, lengths, counts, enc, grads, dec, attn, up, down, gain, bias)


def fast_body(
    gene_counts,
    coords,
    lengths,
    enc_weight,
    dec_weight,
    attn_weight,
    up_weight,
    down_weight,
    ln_gain,
    ln_bias,
    logit_grad,
):
    model_width = enc_weight.shape[1]
    group_rows = gene_counts.shape[0]
    local = model_width // 4
    heads = HEADS // 4
    score_scale = 1.0 / math.sqrt(HEAD_DIM)
    slide = slide_ids(lengths[0], group_rows)
    live = (slide < 2).astype(jnp.bfloat16)[:, None]
    stream_in, grad_out, weights, vectors = encode_call(
        coords,
        lengths,
        gene_counts.T,
        enc_weight,
        logit_grad.T,
        dec_weight.T,
        attn_weight,
        up_weight,
        down_weight,
        ln_gain[None],
        ln_bias[None],
    )
    norm_gains = vectors[:, 0, :64].reshape(2 * model_width)
    offsets = vectors[:, 1, :64].reshape(2 * model_width)
    attn_full, up_full, down_full = [weights[i].reshape(-1, model_width) for i in range(3)]
    proj_weight, out_weight = attn_full[: 3 * local], attn_full[3 * local :]

    def sum_line(part):
        return lax.psum(part.astype(jnp.bfloat16), "gene").astype(jnp.float32)

    stream_in, grad_out = [
        jnp.swapaxes(v, 0, 1).reshape(group_rows, model_width).astype(jnp.float32)
        for v in (stream_in, grad_out)
    ]
    first_normed, first_pull = jax.vjp(
        norm_rows, stream_in, norm_gains[:model_width], offsets[:model_width]
    )
    first_low = first_normed.astype(jnp.bfloat16)
    projected = contract_cols(first_low, proj_weight).astype(jnp.bfloat16)
    queries, keys, values = [
        projected[:, i * local : (i + 1) * local].reshape(group_rows, heads, HEAD_DIM)
        for i in range(3)
    ]
    same_slide = (slide[:, None] == slide[None, :])[None]
    scores = (
        jnp.einsum("qhd,khd->hqk", queries, keys, preferred_element_type=jnp.float32)
        * score_scale
    )
    scores = jnp.where(same_slide, scores, -1e30)
    row_max = jnp.max(scores, axis=-1, keepdims=True)
    raised = jnp.exp(scores - row_max)
    soft = raised / jnp.sum(raised, axis=-1, keepdims=True)
    soft_low = soft.astype(jnp.bfloat16)
    attended = jnp.einsum("hqk,khd->qhd", soft_low, values, preferred_element_type=jnp.float32)
    attended = attended.reshape(group_rows, local).astype(jnp.bfloat16)
    stream_mid = stream_in + sum_line(product(attended, out_weight))
    second_normed, second_pull = jax.vjp(
        norm_rows, stream_mid, norm_gains[model_width:], offsets[model_width:]
    )
    second_low = second_normed.astype(jnp.bfloat16)
    hidden_pre = contract_cols(second_low, up_full)
    active, gelu_pull = jax.vjp(gelu_tanh, hidden_pre)
    active_low = active.astype(jnp.bfloat16)
    stream_out = stream_mid + sum_line(product(active_low, down_full))
    cells = stream_out.astype(jnp.bfloat16) * live
    logits = product(cells, dec_weight).astype(jnp.bfloat16)
    dec_part = contract_rows(cells, logit_grad).astype(jnp.bfloat16)
    dec_grad = lax.psum_scatter(dec_part, "dp", scatter_dimension=0, tiled=True)
    grad_branch = grad_out.astype(jnp.bfloat16)
    down_part = contract_rows(active_low, grad_branch)
    grad_active = contract_cols(grad_branch, down_full)
    grad_hidden = gelu_pull(grad_active)[0].astype(jnp.bfloat16)
    up_part = contract_rows(grad_hidden, second_low)
    grad_second = sum_line(product(grad_hidden, up_full))
    grad_mid_norm, gain_second, bias_second = second_pull(grad_second)
    grad_mid = grad_out + grad_mid_norm
    grad_attn = grad_mid.astype(jnp.bfloat16)
    out_part = contract_rows(attended, grad_attn)
    grad_attended = (
        contract_cols(grad_attn, out_weight)
        .astype(jnp.bfloat16)
        .reshape(group_rows, heads, HEAD_DIM)
    )
    grad_soft = jnp.einsum(
        "qhd,khd->hqk", grad_attended, values, preferred_element_type=jnp.float32
    )
    grad_scores = soft * (grad_soft - jnp.sum(grad_soft * soft, axis=-1, keepdims=True))
    grad_scores = grad_scores.astype(jnp.bfloat16)
    grad_query = (
        jnp.einsum("hqk,khd->qhd", grad_scores, keys, preferred_element_type=jnp.float32)
        * score_scale
    )
    grad_keys = (
        jnp.einsum("hqk,qhd->khd", grad_scores, queries, preferred_element_type=jnp.float32)
        * score_scale
    )
    grad_values = jnp.einsum(
        "hqk,qhd->khd", soft_low, grad_attended, preferred_element_type=jnp.float32
    )
    grad_proj = jnp.concatenate(
        [g.reshape(group_rows, local) for g in (grad_query, grad_keys, grad_values)], axis=1
    ).astype(jnp.bfloat16)
    proj_part = contract_rows(grad_proj, first_low)
    grad_first = sum_line(product(grad_proj, proj_weight))
    grad_in_norm, gain_first, bias_first = first_pull(grad_first)
    grad_in = (grad_mid + grad_in_norm).astype(jnp.bfloat16)
    gene_grad = contract_cols(grad_in, enc_weight).astype(jnp.bfloat16)
    enc_part = contract_rows(gene_counts, grad_in).astype(jnp.bfloat16)
    enc_grad = lax.psum_scatter(enc_part, "dp", scatter_dimension=1, tiled=True)
    layer_part = jnp.stack(
        [
            part.astype(jnp.bfloat16).reshape(8, -1, model_width)
            for part in (jnp.concatenate([proj_part, out_part], axis=0), up_part, down_part)
        ],
        axis=1,
    )
    layer_grad = lax.psum_scatter(layer_part, "dp", scatter_dimension=0, tiled=True)[0]
    small = jnp.concatenate([gain_first, gain_second, bias_first, bias_second])
    small = lax.psum(small, "dp")
    place = lax.axis_index("dp") * 4 + lax.axis_index("gene")
    gain_grad = lax.dynamic_slice_in_dim(small[: 2 * model_width], place * 64, 64)
    bias_grad = lax.dynamic_slice_in_dim(
        small[2 * model_width : 3 * model_width], place * 32, 32
    )
    mid_bias_grad = lax.dynamic_slice_in_dim(small[3 * model_width :], place * 32, 32)
    return (
        logits,
        gene_grad,
        enc_grad.astype(jnp.float32),
        dec_grad.astype(jnp.float32),
        layer_grad[0].astype(jnp.float32),
        layer_grad[1].astype(jnp.float32),
        layer_grad[2].astype(jnp.float32),
        gain_grad,
        bias_grad,
        mid_bias_grad,
    )


def solution(mesh):
    fast = dict(mesh.shape) == {"dp": 8, "gene": 4}
    in_specs = (
        P("dp", "gene"),
        P(None, ("dp", "gene")),
        P("dp", None),
        P("gene", None),
        P(None, "gene"),
        P(("dp", "gene"), None),
        P(("dp", "gene"), None),
        P(("dp", "gene"), None),
        P(("dp", "gene")),
        P(("dp", "gene")),
        P("dp", "gene"),
    )
    out_specs = (
        P("dp", "gene"),
        P("dp", "gene"),
        P("gene", "dp"),
        P("dp", "gene"),
        P(("dp", "gene"), None),
        P(("dp", "gene"), None),
        P(("dp", "gene"), None),
        P(("dp", "gene")),
        P(("dp", "gene")),
        P(("dp", "gene")),
    )
    return jax.shard_map(
        fast_body if fast else body, mesh=mesh, in_specs=in_specs, out_specs=out_specs, check_vma=False)
```

```python
import functools
import math

import jax
import jax.numpy as jnp
from jax import lax
from jax.experimental import pallas as pl
from jax.experimental.pallas import tpu as pltpu
from jax.sharding import PartitionSpec as P

HEADS = 16
HEAD_DIM = 64


epsilon = 1e-05


def norm_rows(values, gain, offset):
    center = values - jnp.mean(values, axis=-1, keepdims=True)
    spread = jnp.mean(center * center, axis=-1, keepdims=True)
    return center * lax.rsqrt(spread + epsilon) * gain + offset


def gelu_tanh(values):
    return jax.nn.gelu(values, approximate=True)


def positions(coords, model_width):
    indices = jnp.arange(model_width // 4).astype(coords.dtype)
    freqs = jnp.exp(indices * (-4.0 * math.log(10000.0) / model_width))
    along_x = coords[0][:, None] * freqs[None, :]
    along_y = coords[1][:, None] * freqs[None, :]
    return jnp.concatenate(
        [jnp.sin(along_x), jnp.cos(along_x), jnp.sin(along_y), jnp.cos(along_y)], axis=1
    )


def slide_ids(slide_lengths, length_all):
    places = jnp.arange(length_all, dtype=jnp.int32)
    return (places >= slide_lengths[0]).astype(jnp.int32) + (
        places >= slide_lengths[0] + slide_lengths[1]
    ).astype(jnp.int32)


def product(left, right):
    return jnp.dot(left, right, preferred_element_type=jnp.float32)


def contract_rows(left, right):
    return lax.dot_general(
        left, right, (((0,), (0,)), ((), ())), preferred_element_type=jnp.float32
    )


def contract_cols(left, right):
    return lax.dot_general(
        left, right, (((1,), (1,)), ((), ())), preferred_element_type=jnp.float32
    )


def body(
    gene_counts,
    coords,
    lengths,
    enc_weight,
    dec_weight,
    attn_weight,
    up_weight,
    down_weight,
    ln_gain,
    ln_bias,
    logit_grad,
):
    model_width = enc_weight.shape[1]
    group_rows = gene_counts.shape[0]
    own_rows = coords.shape[1]
    gene_index = lax.axis_index("gene")
    score_scale = 1.0 / math.sqrt(HEAD_DIM)
    slide_all = slide_ids(lengths[0], group_rows)
    slide_own = lax.dynamic_slice_in_dim(slide_all, gene_index * own_rows, own_rows)
    live_rows = (slide_all < 2).astype(jnp.bfloat16)[:, None]
    attn_full, up_full, down_full, gain_full, bias_full = (
        lax.all_gather(attn_weight, ("dp", "gene"), axis=0, tiled=True),
        lax.all_gather(up_weight, ("dp", "gene"), axis=0, tiled=True),
        lax.all_gather(down_weight, ("dp", "gene"), axis=0, tiled=True),
        lax.all_gather(ln_gain, ("dp", "gene"), axis=0, tiled=True),
        lax.all_gather(ln_bias, ("dp", "gene"), axis=0, tiled=True),
    )
    norm_gains = gain_full.astype(jnp.float32)
    offsets = bias_full.astype(jnp.float32)
    proj_weight = attn_full[: 3 * model_width]
    out_weight = attn_full[3 * model_width :]
    embedded = lax.psum_scatter(
        product(gene_counts, enc_weight).astype(jnp.bfloat16),
        "gene",
        scatter_dimension=0,
        tiled=True,
    ).astype(jnp.float32)
    stream_in = embedded + positions(coords, model_width)
    first_normed, first_pull = jax.vjp(
        norm_rows, stream_in, norm_gains[:model_width], offsets[:model_width]
    )
    first_low = first_normed.astype(jnp.bfloat16)
    projected = contract_cols(first_low, proj_weight).astype(jnp.bfloat16)
    queries = projected[:, :model_width].reshape(own_rows, HEADS, HEAD_DIM)
    keyval_all = lax.all_gather(projected[:, model_width:], "gene", axis=0, tiled=True)
    keys_all = keyval_all[:, :model_width].reshape(group_rows, HEADS, HEAD_DIM)
    values_all = keyval_all[:, model_width:].reshape(group_rows, HEADS, HEAD_DIM)
    same_slide = (slide_own[:, None] == slide_all[None, :])[None]
    scores = (
        jnp.einsum("qhd,khd->hqk", queries, keys_all, preferred_element_type=jnp.float32)
        * score_scale
    )
    scores = jnp.where(same_slide, scores, -1e30)
    row_max = jnp.max(scores, axis=-1, keepdims=True)
    raised = jnp.exp(scores - row_max)
    soft = raised / jnp.sum(raised, axis=-1, keepdims=True)
    soft_low = soft.astype(jnp.bfloat16)
    attended = jnp.einsum("hqk,khd->qhd", soft_low, values_all, preferred_element_type=jnp.float32)
    attended = attended.reshape(own_rows, model_width).astype(jnp.bfloat16)
    stream_mid = stream_in + product(attended, out_weight)
    second_normed, second_pull = jax.vjp(
        norm_rows, stream_mid, norm_gains[model_width:], offsets[model_width:]
    )
    second_low = second_normed.astype(jnp.bfloat16)
    hidden_pre = contract_cols(second_low, up_full)
    active, gelu_pull = jax.vjp(gelu_tanh, hidden_pre)
    active_low = active.astype(jnp.bfloat16)
    stream_out = stream_mid + product(active_low, down_full)
    cells_low = stream_out.astype(jnp.bfloat16)
    cells_all = lax.all_gather(cells_low, "gene", axis=0, tiled=True)
    logits_full = product(cells_all, dec_weight)
    logits = (logits_full * live_rows.astype(jnp.float32)).astype(jnp.bfloat16)
    masked_grad = logit_grad * live_rows
    grad_out = lax.psum_scatter(
        contract_cols(masked_grad, dec_weight).astype(jnp.bfloat16),
        "gene",
        scatter_dimension=0,
        tiled=True,
    ).astype(jnp.float32)
    dec_part = contract_rows(cells_all, masked_grad)
    grad_branch = grad_out.astype(jnp.bfloat16)
    down_part = contract_rows(active_low, grad_branch)
    grad_active = contract_cols(grad_branch, down_full)
    grad_hidden = gelu_pull(grad_active)[0].astype(jnp.bfloat16)
    up_part = contract_rows(grad_hidden, second_low)
    grad_second = product(grad_hidden, up_full)
    grad_mid_norm, gain_second, bias_second = second_pull(grad_second)
    grad_mid = grad_out + grad_mid_norm
    grad_attn = grad_mid.astype(jnp.bfloat16)
    out_part = contract_rows(attended, grad_attn)
    grad_attended = (
        contract_cols(grad_attn, out_weight).astype(jnp.bfloat16).reshape(own_rows, HEADS, HEAD_DIM)
    )
    grad_soft = jnp.einsum(
        "qhd,khd->hqk", grad_attended, values_all, preferred_element_type=jnp.float32
    )
    grad_scores = soft * (grad_soft - jnp.sum(grad_soft * soft, axis=-1, keepdims=True))
    grad_scores = grad_scores.astype(jnp.bfloat16)
    grad_query = (
        jnp.einsum("hqk,khd->qhd", grad_scores, keys_all, preferred_element_type=jnp.float32)
        * score_scale
    )
    grad_query = grad_query.reshape(own_rows, model_width).astype(jnp.bfloat16)
    grad_keys = (
        jnp.einsum("hqk,qhd->khd", grad_scores, queries, preferred_element_type=jnp.float32)
        * score_scale
    )
    grad_values = jnp.einsum(
        "hqk,qhd->khd", soft_low, grad_attended, preferred_element_type=jnp.float32
    )
    keyval_part = jnp.concatenate(
        [grad_keys.reshape(group_rows, model_width), grad_values.reshape(group_rows, model_width)],
        axis=1,
    )
    grad_keyval = lax.psum_scatter(
        keyval_part.astype(jnp.bfloat16), "gene", scatter_dimension=0, tiled=True
    )
    grad_proj = jnp.concatenate([grad_query, grad_keyval], axis=1)
    proj_part = contract_rows(grad_proj, first_low)
    grad_first = product(grad_proj, proj_weight)
    grad_in_norm, gain_first, bias_first = first_pull(grad_first)
    grad_in = (grad_mid + grad_in_norm).astype(jnp.bfloat16)
    grad_in_all = lax.all_gather(grad_in, "gene", axis=0, tiled=True)
    gene_grad = contract_cols(grad_in_all, enc_weight).astype(jnp.bfloat16)
    enc_part = contract_rows(gene_counts, grad_in_all)
    enc_grad, dec_grad = (
        lax.psum_scatter(enc_part, "dp", scatter_dimension=1, tiled=True),
        lax.psum_scatter(dec_part, "dp", scatter_dimension=0, tiled=True),
    )
    attn_part = jnp.concatenate([proj_part, out_part], axis=0)
    gain_part = jnp.concatenate([gain_first, gain_second], axis=0)
    attn_grad, up_grad, down_grad, gain_grad, bias_grad, mid_bias_grad = (
        lax.psum_scatter(attn_part, ("dp", "gene"), scatter_dimension=0, tiled=True),
        lax.psum_scatter(up_part, ("dp", "gene"), scatter_dimension=0, tiled=True),
        lax.psum_scatter(down_part, ("dp", "gene"), scatter_dimension=0, tiled=True),
        lax.psum_scatter(gain_part, ("dp", "gene"), scatter_dimension=0, tiled=True),
        lax.psum_scatter(bias_first, ("dp", "gene"), scatter_dimension=0, tiled=True),
        lax.psum_scatter(bias_second, ("dp", "gene"), scatter_dimension=0, tiled=True),
    )
    return (
        logits,
        gene_grad,
        enc_grad,
        dec_grad,
        attn_grad,
        up_grad,
        down_grad,
        gain_grad,
        bias_grad,
        mid_bias_grad,
    )


MESH = pl.DeviceIdType.MESH
MIB = 2**20
VMEM = pl.BlockSpec(memory_space=pltpu.VMEM)
SMEM = pl.BlockSpec(memory_space=pltpu.SMEM)
ANY = pl.BlockSpec(memory_space=pl.ANY)
DMA = pltpu.SemaphoreType.DMA


class Place:
    def __init__(self):
        self.dp = dp = lax.axis_index("dp")
        self.z = z = lax.axis_index("gene")
        self.core = dp % 2
        self.chip = dp // 2
        self.inner = z * (3 - z) > 0
        self.outer = z * (3 - z) == 0
        self.pair = (dp, z + 1 - 2 * (z % 2))
        self.middle = (dp, 3 - z)
        self.sibling_dp = dp + 1 - 2 * (dp % 2)
        self.x_dp = dp + 2 - 4 * ((dp // 2) % 2)
        self.y_dp = dp + 4 - 8 * (dp // 4)
        self.xy_dp = self.x_dp + 4 - 8 * (dp // 4)
        self.sibling = (self.sibling_dp, z)
        self.far_dps = (self.x_dp, self.y_dp, self.xy_dp)
        self.far = tuple((d, z) for d in self.far_dps)
        self.line = tuple((dp, (z + k) % 4) for k in (1, 2, 3))

    def near(self):
        return self.line

    def meet(self, devices):
        barrier = pltpu.get_barrier_semaphore()
        for device in devices:
            pl.semaphore_signal(barrier, inc=1, device_id=device, device_id_type=MESH)
        pl.semaphore_wait(barrier, len(devices))

    def meet_line(self):
        barrier = pltpu.get_barrier_semaphore()
        pl.semaphore_signal(barrier, inc=1, device_id=self.pair, device_id_type=MESH)

        @pl.when(self.inner)
        def _():
            pl.semaphore_signal(barrier, inc=1, device_id=self.middle, device_id_type=MESH)
            pl.semaphore_wait(barrier, 2)

        @pl.when(self.outer)
        def _():
            pl.semaphore_wait(barrier, 1)


def send(src, dst, send_sem, recv_sem, device):
    return pltpu.make_async_remote_copy(
        src_ref=src,
        dst_ref=dst,
        send_sem=send_sem,
        recv_sem=recv_sem,
        device_id=device,
        device_id_type=MESH,
    )


class LineSum:
    SEMS = 6

    def __init__(self, place, part, inbox, peer, total, sems, view):
        self.place, self.part, self.inbox, self.peer, self.total = place, part, inbox, peer, total
        self.sems, self.view = sems, view

    def up(self, k):
        s, v = self.sems, self.view
        return send(v(self.part, k), v(self.inbox, k), s.at[0, k], s.at[1, k], self.place.pair)

    def across(self, k):
        s, v = self.sems, self.view
        return send(v(self.part, k), v(self.peer, k), s.at[2, k], s.at[3, k], self.place.middle)

    def down(self, k):
        s, v = self.sems, self.view
        return send(v(self.total, k), v(self.total, k), s.at[4, k], s.at[5, k], self.place.pair)

    def push(self, k):
        @pl.when(self.place.outer)
        def _():
            self.up(k).start()

    def meet_up(self, k):
        @pl.when(self.place.inner)
        def _():
            self.up(k).wait_recv()
            mine, other = self.view(self.part, k), self.view(self.inbox, k)
            mine[...] = (mine[...].astype(jnp.float32) + other[...].astype(jnp.float32)).astype(
                jnp.bfloat16
            )
            self.across(k).start()

    def meet_across(self, k):
        @pl.when(self.place.inner)
        def _():
            self.across(k).wait_recv()
            mine, other = self.view(self.part, k), self.view(self.peer, k)
            self.view(self.total, k)[...] = (
                mine[...].astype(jnp.float32) + other[...].astype(jnp.float32)
            ).astype(jnp.bfloat16)
            self.down(k).start()

    def get(self, k):
        @pl.when(self.place.outer)
        def _():
            self.down(k).wait_recv()

    def finish(self, count):
        @pl.when(self.place.outer)
        def _():
            for k in range(count):
                self.up(k).wait_send()

        @pl.when(self.place.inner)
        def _():
            for k in range(count):
                self.across(k).wait_send()
                self.down(k).wait_send()


def chunk(ref, k):
    return ref.at[k]


def columns(ref, k, width):
    return ref.at[:, pl.ds(k * width, width)]


def row_live(lengths, rows):
    index = lax.broadcasted_iota(jnp.int32, (rows, 1), 0)
    return (index < lengths[0, 0] + lengths[0, 1]).astype(jnp.float32)


def encode_kernel(
    coords,
    lengths,
    counts,
    enc,
    grads,
    dec,
    attn,
    up,
    down,
    gain,
    bias,
    stream,
    grad_out,
    weights,
    vectors,
    counts_side,
    grads_side,
    counts_v,
    enc_v,
    grads_v,
    dec_v,
    work,
    places,
    part_a,
    inbox_a,
    peer_a,
    part_b,
    inbox_b,
    peer_b,
    load_sems,
    sems_a,
    sems_b,
    far_sems,
    side_sems,
    line_sems,
    pair_sems,
):
    place = Place()
    dp, z = place.dp, place.z
    chunks, rows, lanes = stream.shape
    width = chunks * lanes
    step = width // 4
    loads = [pltpu.make_async_copy(counts, counts_v, load_sems.at[0])]
    for j in range(4):
        loads.append(
            pltpu.make_async_copy(
                columns(enc, j, step), columns(enc_v, j, step), load_sems.at[1 + j]
            )
        )
    loads.append(pltpu.make_async_copy(grads, grads_v, load_sems.at[5]))
    for j in range(4):
        loads.append(
            pltpu.make_async_copy(
                columns(dec, j, step), columns(dec_v, j, step), load_sems.at[6 + j]
            )
        )
    for copy in loads:
        copy.start()
    for i, ref in enumerate((attn, up, down)):
        weights[i, dp] = ref[...]
    place.meet(place.far + (place.sibling,) + place.line)

    tile = vectors.at[dp * 4 + z]
    tile[...] = jnp.zeros_like(tile)
    tile[0:1, 0:64] = gain[...].astype(jnp.float32)
    tile[1:2, 0:64] = bias[...].astype(jnp.float32)
    line_out = [
        send(tile, tile, line_sems.at[0, i], line_sems.at[1, i], device)
        for i, device in enumerate(place.line)
    ]
    for copy in line_out:
        copy.start()

    def block_of(d):
        return weights.at[:, d]

    far_out = [
        send(block_of(dp), block_of(dp), far_sems.at[0, i], far_sems.at[1, i], device)
        for i, device in enumerate(place.far)
    ]
    far_in = [
        send(block_of(d), block_of(d), far_sems.at[0, i], far_sems.at[1, i], device)
        for i, (d, device) in enumerate(zip(place.far_dps, place.far))
    ]
    side_from = (dp,) + place.far_dps
    side = [
        send(block_of(d), block_of(d), side_sems.at[0, i], side_sems.at[1, i], place.sibling)
        for i, d in enumerate(side_from)
    ]
    for copy in far_out:
        copy.start()
    side[0].start()

    def lines(d):
        return vectors.at[pl.ds(d * 4, 4)]

    vec_far = [
        send(lines(dp), lines(dp), far_sems.at[2, i], far_sems.at[3, i], device)
        for i, device in enumerate(place.far)
    ]
    vec_side = [
        send(lines(d), lines(d), side_sems.at[2, i], side_sems.at[3, i], place.sibling)
        for i, d in enumerate(side_from)
    ]

    pair_out = [
        send(src, dst, pair_sems.at[0, i], pair_sems.at[1, i], place.sibling)
        for i, (src, dst) in enumerate(((counts_v, counts_side), (grads_v, grads_side)))
    ]

    own_rows = coords.shape[1]
    index = lax.broadcasted_iota(jnp.int32, (1, step), 1).astype(jnp.float32)
    freqs = jnp.exp(index * (-4.0 * math.log(10000.0) / width))
    for axis in range(2):
        along = jnp.broadcast_to(coords[axis : axis + 1, :], (own_rows, own_rows)).T
        angle = along[:, 0:1] * freqs
        places[2 * axis] = jnp.sin(angle)
        places[2 * axis + 1] = jnp.cos(angle)

    sum_a = LineSum(place, part_a, inbox_a, peer_a, stream, sems_a, chunk)
    sum_b = LineSum(place, part_b, inbox_b, peer_b, grad_out, sems_b, chunk)
    live = row_live(lengths, rows)
    own = pl.ds(pl.multiple_of(z * own_rows, own_rows), own_rows)
    per = step // lanes

    def encode(j):
        if j == 0:
            loads[0].wait()
            pair_out[0].start()
        loads[1 + j].wait()
        work[...] = contract_rows(counts_v[...], enc_v[:, j * step : (j + 1) * step])
        work[own, :] += places[j]
        for k in range(per):
            part_a[j * per + k] = work[:, k * lanes : (k + 1) * lanes].astype(jnp.bfloat16)
            sum_a.push(j * per + k)

    def decode(j):
        if j == 0:
            loads[5].wait()
            pair_out[1].start()
        loads[6 + j].wait()
        got = contract_rows(grads_v[...], dec_v[:, j * step : (j + 1) * step]) * live
        for k in range(per):
            part_b[j * per + k] = got[:, k * lanes : (k + 1) * lanes].astype(jnp.bfloat16)
            sum_b.push(j * per + k)

    produce = [functools.partial(encode, j) for j in range(4)]
    produce += [functools.partial(decode, j) for j in range(4)]
    ups = [functools.partial(sum_a.meet_up, k) for k in range(8)]
    ups += [functools.partial(sum_b.meet_up, k) for k in range(8)]
    acrosses = [functools.partial(sum_a.meet_across, k) for k in range(8)]
    acrosses += [functools.partial(sum_b.meet_across, k) for k in range(8)]

    def vectors_out():
        for copy in line_out:
            copy.wait_recv()
        for copy in vec_far + vec_side[:1]:
            copy.start()

    def weights_on():
        for i in range(3):
            far_in[i].wait_recv()
            side[1 + i].start()
            vec_far[i].wait_recv()
            vec_side[1 + i].start()

    made = 0
    for k in range(17):
        while made < 8 and made * per < k + per + 2:
            produce[made]()
            made += 1
        if k < 16:
            ups[k]()
        if k == 4:
            vectors_out()
        if k == 13:
            weights_on()
        if k >= 1:
            acrosses[k - 1]()
    for k in range(8):
        sum_a.get(k)
    for k in range(8):
        sum_b.get(k)
    sum_a.finish(8)
    sum_b.finish(8)
    for copy in line_out:
        copy.wait_send()
    for copy in far_out + vec_far:
        copy.wait_send()
    for copy in side + vec_side + pair_out:
        copy.wait()


def encode_call(coords, lengths, counts, enc, grads, dec, attn, up, down, gain, bias):
    genes, rows = counts.shape
    width = enc.shape[1]
    low, full = jnp.bfloat16, jnp.float32
    block = pltpu.VMEM((width // 128, rows, 128), low)
    return pl.pallas_call(
        encode_kernel,
        out_shape=(
            jax.ShapeDtypeStruct((width // 128, rows, 128), low),
            jax.ShapeDtypeStruct((width // 128, rows, 128), low),
            jax.ShapeDtypeStruct((3, 8) + attn.shape, low),
            jax.ShapeDtypeStruct((32, 8, 128), full),
            jax.ShapeDtypeStruct(counts.shape, low),
            jax.ShapeDtypeStruct(grads.shape, low),
        ),
        in_specs=[VMEM, SMEM, ANY, ANY, ANY, ANY, VMEM, VMEM, VMEM, VMEM, VMEM],
        out_specs=(VMEM, VMEM, VMEM, VMEM, ANY, ANY),
        scratch_shapes=[
            pltpu.VMEM((genes, rows), low),
            pltpu.VMEM((genes, width), low),
            pltpu.VMEM((genes, rows), low),
            pltpu.VMEM((genes, width), low),
            pltpu.VMEM((rows, width // 4), full),
            pltpu.VMEM((4, coords.shape[1], width // 4), full),
            block,
            block,
            block,
            block,
            block,
            block,
            DMA((10,)),
            DMA((6, 8)),
            DMA((6, 8)),
            DMA((4, 3)),
            DMA((4, 4)),
            DMA((2, 3)),
            DMA((2, 2)),
        ],
        compiler_params=pltpu.CompilerParams(
            collective_id=0, has_side_effects=True, vmem_limit_bytes=56 * MIB
        ),
        name="encode",
    )(coords, lengths, counts, enc, grads, dec, attn, up, down, gain, bias)


def exact(value):
    return value.astype(jnp.float32)


def low(value):
    return value.astype(jnp.bfloat16)


def rows_of(ref, k):
    return ref.at[pl.ds(k * 64, 64)]


def normalize(values):
    center = values - jnp.mean(values, axis=-1, keepdims=True)
    spread = jnp.mean(center * center, axis=-1, keepdims=True)
    scale = lax.rsqrt(spread + epsilon)
    return center * scale, scale


def norm_back(grad, gain, normed, scale):
    lifted = grad * gain
    return scale * (
        lifted
        - jnp.mean(lifted, axis=-1, keepdims=True)
        - normed * jnp.mean(lifted * normed, axis=-1, keepdims=True)
    )


def gelu_both(u):
    curve, factor = 0.044715, math.sqrt(2.0 / math.pi)
    square = u * u
    bent = jnp.tanh(factor * (u + curve * u * square))
    half = 0.5 * (1.0 + bent)
    slope = half + 0.5 * u * (1.0 - bent * bent) * (factor * (1.0 + 3.0 * curve * square))
    return u * half, slope


def layer_kernel(
    lengths,
    vectors,
    stream,
    branch,
    weights,
    cells,
    grad_in,
    grads,
    sums,
    qkv,
    key_masked,
    value_masked,
    soft,
    key_sum,
    value_sum,
    grad_mid,
    gains,
    offsets,
    part_m,
    part_o,
    part_s,
    part_f,
    inbox_m,
    inbox_o,
    inbox_s,
    inbox_f,
    peer_m,
    peer_o,
    peer_s,
    peer_f,
    total_m,
    total_o,
    total_s,
    total_f,
    active,
    hidden,
    second,
    branch_rows,
    cat,
    first,
    outgoing,
    arriving,
    line_sems,
    side_sems,
    far_sems,
):
    place = Place()
    width, group = cells.shape[2], cells.shape[1]
    local = width // 4
    span = 128
    parts = group // span
    lane = lax.broadcasted_iota(jnp.int32, (1, span), 1)
    head_lanes = [low((lane // HEAD_DIM == h).astype(jnp.float32)) for h in range(2)]
    head_exact = [exact(h) for h in head_lanes]
    first_end, second_end = lengths[0, 0], lengths[0, 0] + lengths[0, 1]

    def slide_of(index):
        return (index >= first_end).astype(jnp.int32) + (index >= second_end).astype(jnp.int32)

    def rows(r):
        return slice(r * span, (r + 1) * span)

    def row_index(r):
        return lax.broadcasted_iota(jnp.int32, (span, 1), 0) + r * span

    def gathered(ref, r):
        return jnp.concatenate([ref[k, rows(r), :] for k in range(width // span)], axis=1)

    def matrix(i, start, stop):
        return weights[i, start:stop].reshape((stop - start) * span, width)

    def side_copy(ref, i):
        return send(ref.at[0], ref.at[1], side_sems.at[0, i], side_sems.at[1, i], place.sibling)

    def side_rows(ref, r, i):
        block = pl.ds(r * span, span)
        return send(
            ref.at[0, block],
            ref.at[1, block],
            side_sems.at[0, i],
            side_sems.at[1, i],
            place.sibling,
        )

    side_active, side_hidden = side_copy(active, 0), side_copy(hidden, 1)
    side_second, side_branch = side_copy(second, 2), side_copy(branch_rows, 3)
    side_cat = side_copy(cat, 4)
    side_first, side_attn = side_copy(first.at[0], 5), side_copy(first.at[1], 6)
    side_cells = [side_rows(cells, r, 7 + r) for r in range(parts)]
    side_in = [side_rows(grad_in, r, 7 + parts + r) for r in range(parts)]

    def line_sum(i, part, inbox, peer, total):
        return LineSum(place, part, inbox, peer, total, line_sems.at[i], rows_of)

    sum_m = line_sum(0, part_m, inbox_m, peer_m, total_m)
    sum_o = line_sum(1, part_o, inbox_o, peer_o, total_o)
    sum_s = line_sum(2, part_s, inbox_s, peer_s, total_s)
    sum_f = line_sum(3, part_f, inbox_f, peer_f, total_f)

    place.meet(place.far + (place.sibling,) + place.near())

    for k in range(2 * width // span):
        for ref, row in ((gains, 0), (offsets, 1)):
            ref[0:1, k * span : (k + 1) * span] = jnp.concatenate(
                [vectors[2 * k + i, row : row + 1, 0:64] for i in range(2)], axis=1
            )
    gain_a, gain_b = gains[0:1, :width], gains[0:1, width:]
    offset_a, offset_b = offsets[0:1, :width], offsets[0:1, width:]
    sums[...] = jnp.zeros_like(sums)
    key_sum[...] = jnp.zeros_like(key_sum)
    value_sum[...] = jnp.zeros_like(value_sum)

    def project(r):
        normed, _ = normalize(exact(gathered(stream, r)))
        value = low(normed * gain_a + offset_a)
        first[0, 0, rows(r), :] = value
        qkv[rows(r), :] = low(contract_cols(value, matrix(0, 0, 6)))
        for p in range(2):
            for ref, at in ((key_masked, local), (value_masked, 2 * local)):
                block = qkv[rows(r), at + p * span : at + (p + 1) * span]
                for h in range(2):
                    ref[p, h * group + r * span : h * group + (r + 1) * span, :] = (
                        block * head_lanes[h]
                    )

    def attend(r):
        same = slide_of(row_index(r)) == slide_of(
            lax.broadcasted_iota(jnp.int32, (1, group), 1)
        )
        for p in range(2):
            query = qkv[rows(r), p * span : (p + 1) * span]
            scores = contract_cols(query, key_masked[p]) * (1.0 / math.sqrt(HEAD_DIM))
            for h in range(2):
                own = jnp.where(same, scores[:, h * group : (h + 1) * group], -1e30)
                raised = jnp.exp(own - jnp.max(own, axis=-1, keepdims=True))
                soft[p, rows(r), h * group : (h + 1) * group] = raised / jnp.sum(
                    raised, axis=-1, keepdims=True
                )
            cat[0, rows(r), 3 * local + p * span : 3 * local + (p + 1) * span] = low(
                product(low(soft[p, rows(r), :]), value_masked[p])
            )
        part_m[rows(r), :] = low(product(cat[0, rows(r), 3 * local :], matrix(0, 6, 8)))
        push(sum_m, r)

    def middle(r):
        return exact(gathered(stream, r)) + exact(total_m[rows(r), :])

    def feed(r):
        get(sum_m, r)
        normed, _ = normalize(middle(r))
        value = low(normed * gain_b + offset_b)
        second[0, rows(r), :] = value
        act, slope = gelu_both(contract_cols(value, matrix(1, 0, 8)))
        active[0, rows(r), :] = low(act)
        grad = gathered(branch, r)
        branch_rows[0, rows(r), :] = grad
        back = low(contract_cols(grad, matrix(2, 0, 8)) * slope)
        hidden[0, rows(r), :] = back
        part_s[rows(r), :] = low(product(back, matrix(1, 0, 8)))
        push(sum_s, r)
        part_o[rows(r), :] = low(product(active[0, rows(r), :], matrix(2, 0, 8)))

    def attend_back(r):
        get(sum_s, r)
        normed, scale = normalize(middle(r))
        grad = exact(total_s[rows(r), :])
        sums[1:2, :] += jnp.sum(grad * normed, axis=0, keepdims=True)
        sums[3:4, :] += jnp.sum(grad, axis=0, keepdims=True)
        mid = exact(branch_rows[0, rows(r), :]) + norm_back(grad, gain_b, normed, scale)
        grad_mid[rows(r), :] = mid
        first[1, 0, rows(r), :] = low(mid)
        spread = low(contract_cols(low(mid), matrix(0, 6, 8)))
        for p in range(2):
            out = spread[:, p * span : (p + 1) * span]
            slopes = contract_cols(out, value_masked[p])
            marks = []
            for h in range(2):
                block = soft[p, rows(r), h * group : (h + 1) * group]
                slope = slopes[:, h * group : (h + 1) * group]
                inner = jnp.sum(slope * block, axis=-1, keepdims=True)
                marks.append(low(block * (slope - inner)))
            scale_q = 1.0 / math.sqrt(HEAD_DIM)
            cat[0, rows(r), p * span : (p + 1) * span] = low(
                product(jnp.concatenate(marks, axis=1), key_masked[p]) * scale_q
            )
            query = qkv[rows(r), p * span : (p + 1) * span]
            at = slice(p * span, (p + 1) * span)
            key_sum[:, at] += contract_rows(
                jnp.concatenate(marks, axis=0),
                jnp.concatenate([query * lanes for lanes in head_lanes], axis=0),
            )
            value_sum[:, at] += contract_rows(
                jnp.concatenate(
                    [low(soft[p, rows(r), h * group : (h + 1) * group]) for h in range(2)], axis=0
                ),
                jnp.concatenate([out * lanes for lanes in head_lanes], axis=0),
            )

    def project_back(r):
        if r == 0:
            cat[0, :, local : 2 * local] = low(key_sum[...] * (1.0 / math.sqrt(HEAD_DIM)))
            cat[0, :, 2 * local : 3 * local] = low(value_sum[...])
        part_f[rows(r), :] = low(product(cat[0, rows(r), : 3 * local], matrix(0, 0, 6)))
        push(sum_f, r)

    def finish_in(r):
        get(sum_f, r)
        normed, scale = normalize(exact(gathered(stream, r)))
        grad = exact(total_f[rows(r), :])
        sums[0:1, :] += jnp.sum(grad * normed, axis=0, keepdims=True)
        sums[2:3, :] += jnp.sum(grad, axis=0, keepdims=True)
        grad_in[0, rows(r), :] = low(grad_mid[rows(r), :] + norm_back(grad, gain_a, normed, scale))
        side_in[r].start()

    def finish_out(r):
        get(sum_o, r)
        live = (row_index(r) < second_end).astype(jnp.float32)
        cells[0, rows(r), :] = low((middle(r) + exact(total_o[rows(r), :])) * live)
        side_cells[r].start()

    def push(total, r):
        total.push(2 * r)
        total.push(2 * r + 1)

    def get(total, r):
        total.get(2 * r)
        total.get(2 * r + 1)

    chips = tuple(d // 2 for d in place.far_dps) + (place.chip,)

    def lanes_of(ref, slot, chip):
        start = pl.multiple_of((chip * 2 + place.core) * span, span)
        return ref[slot, :, pl.ds(start, span)]

    def far_copy(i, q):
        return send(
            outgoing.at[i, q],
            arriving.at[i, q],
            far_sems.at[0, i, q],
            far_sems.at[1, i, q],
            place.far[q],
        )

    def keep(i, q, value):
        if q == 3:
            grads[i] = value
        else:
            outgoing[i, q] = low(value)
            far_copy(i, q).start()

    def weight_grad(i, left, right, half):
        pair = chips[2 * half : 2 * half + 2]
        got = sum(
            contract_rows(
                jnp.concatenate([lanes_of(left, slot, chip) for chip in pair], axis=1),
                right[slot],
            )
            for slot in range(2)
        )
        for k in range(2):
            keep(i, 2 * half + k, got[k * span : (k + 1) * span])

    def attn_grad(q):
        kind = chips[q] // 3
        keep(
            0,
            q,
            sum(
                contract_rows(lanes_of(cat, slot, chips[q]), first[kind, slot]) for slot in range(2)
            ),
        )

    def run(text):
        for word in text.split():
            name, rest = word[0], word[1:]
            if name in "ux":
                total = dict(m=sum_m, o=sum_o, s=sum_s, f=sum_f)[rest[0]]
                for k in rest[1:]:
                    (total.meet_up if name == "u" else total.meet_across)(int(k))
            else:
                for k in rest:
                    steps[name](int(k))

    def start_feed_sides(_):
        for copy in (side_hidden, side_second, side_active, side_branch):
            copy.start()

    def start_attn_sides(_):
        side_cat.start()
        side_attn.start()

    def up_grad(half):
        if half == 0:
            side_hidden.wait_recv()
            side_second.wait_recv()
        weight_grad(1, hidden, second, half)

    def down_grad(half):
        if half == 0:
            side_active.wait_recv()
            side_branch.wait_recv()
        weight_grad(2, active, branch_rows, half)

    def attn_grads(half):
        if half == 0:
            side_first.wait_recv()
            side_attn.wait_recv()
            side_cat.wait_recv()
        attn_grad(2 * half)
        attn_grad(2 * half + 1)

    steps = dict(
        A=project,
        B=attend,
        C=feed,
        D=attend_back,
        G=project_back,
        E=finish_in,
        F=finish_out,
        P=lambda r: push(sum_o, r),
        S=start_feed_sides,
        T=start_attn_sides,
        H=up_grad,
        L=down_grad,
        K=attn_grads,
    )
    run("A0123")
    side_first.start()
    for stage in SCHEDULE:
        run(stage)
    for i in (2, 1, 0):
        for q in range(3):
            far_copy(i, q).wait_recv()
        grads[i] = grads[i] + sum(exact(arriving[i, q]) for q in range(3))
    for total in (sum_m, sum_o, sum_s, sum_f):
        total.finish(8)
    for i in range(3):
        for q in range(3):
            far_copy(i, q).wait_send()
    for copy in side_cells + side_in:
        copy.wait()
    for copy in (
        side_active,
        side_hidden,
        side_second,
        side_branch,
        side_cat,
        side_first,
        side_attn,
    ):
        copy.wait_send()


SCHEDULE = (
    "B01 um01 B2 xm0 um2 xm1 B3 um3 xm23 C0",
    "um45 xm4 C1 xm5 um67 xm6 C2 xm7 us01 xs0",
    "C3 S0 P01 xs1 us23 xs2 D0 xs3 us45 xs4 D1 xs5 us67 xs67",
    "H01 uo01 D2 xo0 uo2 xo1 D3 uo3 xo23",
    "G0123 T0 P23 L01 F01",
    "uf01 xf0 uf2 xf1 E0 uf3 xf2 uf4 xf3 E1 K0 uf5 xf4 uf6 xf5 E2 uf7 xf67 K1",
    "E3 uo45 xo4 uo6 xo5 F2 uo7 xo67 F3",
)


def layer_call(lengths, vectors, stream, branch, weights):
    chunks, group, lanes = stream.shape
    width = chunks * lanes
    half, full = jnp.bfloat16, jnp.float32
    plain = pltpu.VMEM((group, width), half)
    double = pltpu.VMEM((2, group, width), half)
    return pl.pallas_call(
        layer_kernel,
        out_shape=(
            jax.ShapeDtypeStruct((2, group, width), half),
            jax.ShapeDtypeStruct((2, group, width), half),
            jax.ShapeDtypeStruct((3, 128, width), full),
            jax.ShapeDtypeStruct((8, width), full),
        ),
        in_specs=[SMEM, VMEM, VMEM, VMEM, VMEM],
        out_specs=(VMEM, VMEM, VMEM, VMEM),
        scratch_shapes=[
            pltpu.VMEM((group, 3 * width // 4), half),
            pltpu.VMEM((2, 2 * group, 128), half),
            pltpu.VMEM((2, 2 * group, 128), half),
            pltpu.VMEM((2, group, 2 * group), full),
            pltpu.VMEM((group, width // 4), full),
            pltpu.VMEM((group, width // 4), full),
            pltpu.VMEM((group, width), full),
            pltpu.VMEM((1, 2 * width), full),
            pltpu.VMEM((1, 2 * width), full),
        ]
        + [plain] * 16
        + [double] * 5
        + [
            pltpu.VMEM((2, 2, group, width), half),
            pltpu.VMEM((3, 3, 128, width), half),
            pltpu.VMEM((3, 3, 128, width), half),
            DMA((4, 6, 8)),
            DMA((2, 15)),
            DMA((2, 3, 3)),
        ],
        compiler_params=pltpu.CompilerParams(
            collective_id=1, has_side_effects=True, vmem_limit_bytes=60 * MIB
        ),
        name="layer",
    )(lengths, vectors, stream, branch, weights)


def genes_kernel(
    counts,
    counts_side,
    slopes,
    slopes_side,
    enc,
    dec,
    cells,
    grad_in,
    sums,
    logits,
    gene_grad,
    enc_grad,
    dec_grad,
    small,
    counts_v,
    slopes_v,
    enc_v,
    dec_v,
    outgoing,
    arriving,
    sums_side,
    sums_chip,
    sums_far,
    load_sems,
    far_sems,
    sum_sems,
):
    place = Place()
    genes = counts.shape[0]
    span = 128
    bounds = [min(i * GENE_STEP, genes) for i in range(-(-genes // GENE_STEP) + 1)]
    pieces = list(zip(bounds[:-1], bounds[1:]))
    loads = [
        pltpu.make_async_copy(src, dst, load_sems.at[i])
        for i, (src, dst) in enumerate(
            (
                (slopes, slopes_v.at[0]),
                (slopes_side, slopes_v.at[1]),
                (counts, counts_v.at[0]),
                (counts_side, counts_v.at[1]),
                (dec, dec_v),
                (enc, enc_v),
            )
        )
    ]
    for copy in loads:
        copy.start()
    place.meet(place.far + (place.sibling,))
    tail = outgoing.shape[2] - GENE_TAIL
    for i in range(2):
        for q in range(3):
            outgoing[i, q, tail:, :] = jnp.zeros((GENE_TAIL, span), jnp.bfloat16)

    side = send(sums, sums_side, sum_sems.at[0, 0], sum_sems.at[1, 0], place.sibling)
    side.start()
    far_sums = [
        send(sums_chip, sums_far.at[q], sum_sems.at[0, 1 + q], sum_sems.at[1, 1 + q], device)
        for q, device in enumerate(place.far)
    ]
    chips = tuple(d // 2 for d in place.far_dps) + (place.chip,)

    def far_copy(i, q, k):
        block = pl.ds(k * GENE_STEP, min(GENE_STEP, outgoing.shape[2] - k * GENE_STEP))
        return send(
            outgoing.at[i, q, block],
            arriving.at[i, q, block],
            far_sems.at[0, i, q, k],
            far_sems.at[1, i, q, k],
            place.far[q],
        )

    def columns_of(ref, slot, pair):
        return jnp.concatenate(
            [
                ref[slot, :, pl.ds(pl.multiple_of((chip * 2 + place.core) * span, span), span)]
                for chip in pair
            ],
            axis=1,
        )

    def reduce_part(i, left, right, result, half):
        rights = [columns_of(right, slot, chips[2 * half : 2 * half + 2]) for slot in range(2)]
        for k, (start, stop) in enumerate(pieces):
            got = sum(product(left[slot, start:stop, :], rights[slot]) for slot in range(2))
            for n in range(2):
                q, value = 2 * half + n, got[:, n * span : (n + 1) * span]
                if q == 3:
                    result[start:stop, :] = value
                else:
                    outgoing[i, q, start:stop, :] = low(value)
                    far_copy(i, q, k).start()

    def reduce_end(i, result):
        for k, (start, stop) in enumerate(pieces):
            for q in range(3):
                far_copy(i, q, k).wait_recv()
            result[start:stop, :] = result[start:stop, :] + sum(
                exact(arriving[i, q, start:stop, :]) for q in range(3)
            )

    loads[0].wait()
    loads[1].wait()
    reduce_part(0, slopes_v, cells, dec_grad, 0)
    reduce_part(0, slopes_v, cells, dec_grad, 1)
    side.wait()
    sums_chip[...] = sums[...] + sums_side[...]
    for copy in far_sums:
        copy.start()
    loads[2].wait()
    loads[3].wait()
    reduce_part(1, counts_v, grad_in, enc_grad, 0)
    reduce_part(1, counts_v, grad_in, enc_grad, 1)
    loads[4].wait()
    for start, stop in pieces:
        logits[start:stop, :] = low(contract_cols(dec_v[start:stop, :], cells[0]))
    loads[5].wait()
    for start, stop in pieces:
        gene_grad[start:stop, :] = low(contract_cols(enc_v[start:stop, :], grad_in[0]))
    for copy in far_sums:
        copy.wait_recv()
    small[...] = sums_chip[...] + (sums_far[0] + sums_far[1] + sums_far[2])
    reduce_end(0, dec_grad)
    reduce_end(1, enc_grad)
    for i in range(2):
        for q in range(3):
            for k in range(len(pieces)):
                far_copy(i, q, k).wait_send()
    for copy in far_sums:
        copy.wait_send()


GENE_STEP = 848
GENE_TAIL = 16


def genes_call(counts, counts_side, slopes, slopes_side, enc, dec, cells, grad_in, sums):
    genes, group = counts.shape
    width = enc.shape[1]
    padded = -(-genes // 16) * 16
    steps = -(-genes // GENE_STEP)
    half, full = jnp.bfloat16, jnp.float32
    return pl.pallas_call(
        genes_kernel,
        out_shape=(
            jax.ShapeDtypeStruct((genes, group), half),
            jax.ShapeDtypeStruct((genes, group), half),
            jax.ShapeDtypeStruct((genes, 128), full),
            jax.ShapeDtypeStruct((genes, 128), full),
            jax.ShapeDtypeStruct(sums.shape, full),
        ),
        in_specs=[ANY] * 6 + [VMEM] * 3,
        out_specs=(VMEM,) * 5,
        scratch_shapes=[
            pltpu.VMEM((2, genes, group), half),
            pltpu.VMEM((2, genes, group), half),
            pltpu.VMEM((genes, width), half),
            pltpu.VMEM((genes, width), half),
            pltpu.VMEM((2, 3, padded, 128), half),
            pltpu.VMEM((2, 3, padded, 128), half),
            pltpu.VMEM(sums.shape, full),
            pltpu.VMEM(sums.shape, full),
            pltpu.VMEM((3,) + sums.shape, full),
            DMA((6,)),
            DMA((2, 2, 3, steps)),
            DMA((2, 4)),
        ],
        compiler_params=pltpu.CompilerParams(
            collective_id=2, has_side_effects=True, vmem_limit_bytes=60 * MIB
        ),
        name="genes",
    )(counts, counts_side, slopes, slopes_side, enc, dec, cells, grad_in, sums)


def fast_body(
    gene_counts,
    coords,
    lengths,
    enc_weight,
    dec_weight,
    attn_weight,
    up_weight,
    down_weight,
    ln_gain,
    ln_bias,
    logit_grad,
):
    model_width = enc_weight.shape[1]
    counts, slopes, dec = gene_counts.T, logit_grad.T, dec_weight.T
    stream_in, grad_out, weights, vectors, counts_side, slopes_side = encode_call(
        coords,
        lengths,
        counts,
        enc_weight,
        slopes,
        dec,
        attn_weight,
        up_weight,
        down_weight,
        ln_gain[None],
        ln_bias[None],
    )
    cells, grad_in, layer_grad, sums = layer_call(lengths, vectors, stream_in, grad_out, weights)
    logits, gene_grad, enc_grad, dec_grad, small = genes_call(
        counts, counts_side, slopes, slopes_side, enc_weight, dec, cells, grad_in, sums
    )
    small = small[:4].reshape(-1)
    place = lax.axis_index("dp") * 4 + lax.axis_index("gene")
    gain_grad = lax.dynamic_slice_in_dim(small[: 2 * model_width], place * 64, 64)
    bias_grad = lax.dynamic_slice_in_dim(
        small[2 * model_width : 3 * model_width], place * 32, 32
    )
    mid_bias_grad = lax.dynamic_slice_in_dim(small[3 * model_width :], place * 32, 32)
    return (
        logits.T,
        gene_grad.T,
        enc_grad,
        dec_grad.T,
        layer_grad[0],
        layer_grad[1],
        layer_grad[2],
        gain_grad,
        bias_grad,
        mid_bias_grad,
    )


def solution(mesh):
    fast = dict(mesh.shape) == {"dp": 8, "gene": 4}
    in_specs = (
        P("dp", "gene"),
        P(None, ("dp", "gene")),
        P("dp", None),
        P("gene", None),
        P(None, "gene"),
        P(("dp", "gene"), None),
        P(("dp", "gene"), None),
        P(("dp", "gene"), None),
        P(("dp", "gene")),
        P(("dp", "gene")),
        P("dp", "gene"),
    )
    out_specs = (
        P("dp", "gene"),
        P("dp", "gene"),
        P("gene", "dp"),
        P("dp", "gene"),
        P(("dp", "gene"), None),
        P(("dp", "gene"), None),
        P(("dp", "gene"), None),
        P(("dp", "gene")),
        P(("dp", "gene")),
        P(("dp", "gene")),
    )
    return jax.shard_map(
        fast_body if fast else body, mesh=mesh, in_specs=in_specs, out_specs=out_specs, check_vma=False)
```

```python
import functools
import math

import jax
import jax.numpy as jnp
from jax import lax
from jax.experimental import pallas as pl
from jax.experimental.pallas import tpu as pltpu
from jax.sharding import PartitionSpec as P

HEADS = 16
HEAD_DIM = 64


epsilon = 1e-05


def norm_rows(values, gain, offset):
    center = values - jnp.mean(values, axis=-1, keepdims=True)
    spread = jnp.mean(center * center, axis=-1, keepdims=True)
    return center * lax.rsqrt(spread + epsilon) * gain + offset


def gelu_tanh(values):
    return jax.nn.gelu(values, approximate=True)


def positions(coords, model_width):
    indices = jnp.arange(model_width // 4).astype(coords.dtype)
    freqs = jnp.exp(indices * (-4.0 * math.log(10000.0) / model_width))
    along_x = coords[0][:, None] * freqs[None, :]
    along_y = coords[1][:, None] * freqs[None, :]
    return jnp.concatenate(
        [jnp.sin(along_x), jnp.cos(along_x), jnp.sin(along_y), jnp.cos(along_y)], axis=1
    )


def slide_ids(slide_lengths, length_all):
    places = jnp.arange(length_all, dtype=jnp.int32)
    return (places >= slide_lengths[0]).astype(jnp.int32) + (
        places >= slide_lengths[0] + slide_lengths[1]
    ).astype(jnp.int32)


def product(left, right):
    return jnp.dot(left, right, preferred_element_type=jnp.float32)


def contract_rows(left, right):
    return lax.dot_general(
        left, right, (((0,), (0,)), ((), ())), preferred_element_type=jnp.float32
    )


def contract_cols(left, right):
    return lax.dot_general(
        left, right, (((1,), (1,)), ((), ())), preferred_element_type=jnp.float32
    )


def body(
    gene_counts,
    coords,
    lengths,
    enc_weight,
    dec_weight,
    attn_weight,
    up_weight,
    down_weight,
    ln_gain,
    ln_bias,
    logit_grad,
):
    model_width = enc_weight.shape[1]
    group_rows = gene_counts.shape[0]
    own_rows = coords.shape[1]
    gene_index = lax.axis_index("gene")
    score_scale = 1.0 / math.sqrt(HEAD_DIM)
    slide_all = slide_ids(lengths[0], group_rows)
    slide_own = lax.dynamic_slice_in_dim(slide_all, gene_index * own_rows, own_rows)
    live_rows = (slide_all < 2).astype(jnp.bfloat16)[:, None]
    attn_full, up_full, down_full, gain_full, bias_full = (
        lax.all_gather(attn_weight, ("dp", "gene"), axis=0, tiled=True),
        lax.all_gather(up_weight, ("dp", "gene"), axis=0, tiled=True),
        lax.all_gather(down_weight, ("dp", "gene"), axis=0, tiled=True),
        lax.all_gather(ln_gain, ("dp", "gene"), axis=0, tiled=True),
        lax.all_gather(ln_bias, ("dp", "gene"), axis=0, tiled=True),
    )
    norm_gains = gain_full.astype(jnp.float32)
    offsets = bias_full.astype(jnp.float32)
    proj_weight = attn_full[: 3 * model_width]
    out_weight = attn_full[3 * model_width :]
    embedded = lax.psum_scatter(
        product(gene_counts, enc_weight).astype(jnp.bfloat16),
        "gene",
        scatter_dimension=0,
        tiled=True,
    ).astype(jnp.float32)
    stream_in = embedded + positions(coords, model_width)
    first_normed, first_pull = jax.vjp(
        norm_rows, stream_in, norm_gains[:model_width], offsets[:model_width]
    )
    first_low = first_normed.astype(jnp.bfloat16)
    projected = contract_cols(first_low, proj_weight).astype(jnp.bfloat16)
    queries = projected[:, :model_width].reshape(own_rows, HEADS, HEAD_DIM)
    keyval_all = lax.all_gather(projected[:, model_width:], "gene", axis=0, tiled=True)
    keys_all = keyval_all[:, :model_width].reshape(group_rows, HEADS, HEAD_DIM)
    values_all = keyval_all[:, model_width:].reshape(group_rows, HEADS, HEAD_DIM)
    same_slide = (slide_own[:, None] == slide_all[None, :])[None]
    scores = (
        jnp.einsum("qhd,khd->hqk", queries, keys_all, preferred_element_type=jnp.float32)
        * score_scale
    )
    scores = jnp.where(same_slide, scores, -1e30)
    row_max = jnp.max(scores, axis=-1, keepdims=True)
    raised = jnp.exp(scores - row_max)
    soft = raised / jnp.sum(raised, axis=-1, keepdims=True)
    soft_low = soft.astype(jnp.bfloat16)
    attended = jnp.einsum("hqk,khd->qhd", soft_low, values_all, preferred_element_type=jnp.float32)
    attended = attended.reshape(own_rows, model_width).astype(jnp.bfloat16)
    stream_mid = stream_in + product(attended, out_weight)
    second_normed, second_pull = jax.vjp(
        norm_rows, stream_mid, norm_gains[model_width:], offsets[model_width:]
    )
    second_low = second_normed.astype(jnp.bfloat16)
    hidden_pre = contract_cols(second_low, up_full)
    active, gelu_pull = jax.vjp(gelu_tanh, hidden_pre)
    active_low = active.astype(jnp.bfloat16)
    stream_out = stream_mid + product(active_low, down_full)
    cells_low = stream_out.astype(jnp.bfloat16)
    cells_all = lax.all_gather(cells_low, "gene", axis=0, tiled=True)
    logits_full = product(cells_all, dec_weight)
    logits = (logits_full * live_rows.astype(jnp.float32)).astype(jnp.bfloat16)
    masked_grad = logit_grad * live_rows
    grad_out = lax.psum_scatter(
        contract_cols(masked_grad, dec_weight).astype(jnp.bfloat16),
        "gene",
        scatter_dimension=0,
        tiled=True,
    ).astype(jnp.float32)
    dec_part = contract_rows(cells_all, masked_grad)
    grad_branch = grad_out.astype(jnp.bfloat16)
    down_part = contract_rows(active_low, grad_branch)
    grad_active = contract_cols(grad_branch, down_full)
    grad_hidden = gelu_pull(grad_active)[0].astype(jnp.bfloat16)
    up_part = contract_rows(grad_hidden, second_low)
    grad_second = product(grad_hidden, up_full)
    grad_mid_norm, gain_second, bias_second = second_pull(grad_second)
    grad_mid = grad_out + grad_mid_norm
    grad_attn = grad_mid.astype(jnp.bfloat16)
    out_part = contract_rows(attended, grad_attn)
    grad_attended = (
        contract_cols(grad_attn, out_weight).astype(jnp.bfloat16).reshape(own_rows, HEADS, HEAD_DIM)
    )
    grad_soft = jnp.einsum(
        "qhd,khd->hqk", grad_attended, values_all, preferred_element_type=jnp.float32
    )
    grad_scores = soft * (grad_soft - jnp.sum(grad_soft * soft, axis=-1, keepdims=True))
    grad_scores = grad_scores.astype(jnp.bfloat16)
    grad_query = (
        jnp.einsum("hqk,khd->qhd", grad_scores, keys_all, preferred_element_type=jnp.float32)
        * score_scale
    )
    grad_query = grad_query.reshape(own_rows, model_width).astype(jnp.bfloat16)
    grad_keys = (
        jnp.einsum("hqk,qhd->khd", grad_scores, queries, preferred_element_type=jnp.float32)
        * score_scale
    )
    grad_values = jnp.einsum(
        "hqk,qhd->khd", soft_low, grad_attended, preferred_element_type=jnp.float32
    )
    keyval_part = jnp.concatenate(
        [grad_keys.reshape(group_rows, model_width), grad_values.reshape(group_rows, model_width)],
        axis=1,
    )
    grad_keyval = lax.psum_scatter(
        keyval_part.astype(jnp.bfloat16), "gene", scatter_dimension=0, tiled=True
    )
    grad_proj = jnp.concatenate([grad_query, grad_keyval], axis=1)
    proj_part = contract_rows(grad_proj, first_low)
    grad_first = product(grad_proj, proj_weight)
    grad_in_norm, gain_first, bias_first = first_pull(grad_first)
    grad_in = (grad_mid + grad_in_norm).astype(jnp.bfloat16)
    grad_in_all = lax.all_gather(grad_in, "gene", axis=0, tiled=True)
    gene_grad = contract_cols(grad_in_all, enc_weight).astype(jnp.bfloat16)
    enc_part = contract_rows(gene_counts, grad_in_all)
    enc_grad, dec_grad = (
        lax.psum_scatter(enc_part, "dp", scatter_dimension=1, tiled=True),
        lax.psum_scatter(dec_part, "dp", scatter_dimension=0, tiled=True),
    )
    attn_part = jnp.concatenate([proj_part, out_part], axis=0)
    gain_part = jnp.concatenate([gain_first, gain_second], axis=0)
    attn_grad, up_grad, down_grad, gain_grad, bias_grad, mid_bias_grad = (
        lax.psum_scatter(attn_part, ("dp", "gene"), scatter_dimension=0, tiled=True),
        lax.psum_scatter(up_part, ("dp", "gene"), scatter_dimension=0, tiled=True),
        lax.psum_scatter(down_part, ("dp", "gene"), scatter_dimension=0, tiled=True),
        lax.psum_scatter(gain_part, ("dp", "gene"), scatter_dimension=0, tiled=True),
        lax.psum_scatter(bias_first, ("dp", "gene"), scatter_dimension=0, tiled=True),
        lax.psum_scatter(bias_second, ("dp", "gene"), scatter_dimension=0, tiled=True),
    )
    return (
        logits,
        gene_grad,
        enc_grad,
        dec_grad,
        attn_grad,
        up_grad,
        down_grad,
        gain_grad,
        bias_grad,
        mid_bias_grad,
    )


MESH = pl.DeviceIdType.MESH
MIB = 2**20
VMEM = pl.BlockSpec(memory_space=pltpu.VMEM)
SMEM = pl.BlockSpec(memory_space=pltpu.SMEM)
ANY = pl.BlockSpec(memory_space=pl.ANY)
DMA = pltpu.SemaphoreType.DMA


class Place:
    def __init__(self):
        self.dp = dp = lax.axis_index("dp")
        self.z = z = lax.axis_index("gene")
        self.core = dp % 2
        self.chip = dp // 2
        self.inner = z * (3 - z) > 0
        self.outer = z * (3 - z) == 0
        self.pair = (dp, z + 1 - 2 * (z % 2))
        self.middle = (dp, 3 - z)
        self.sibling_dp = dp + 1 - 2 * (dp % 2)
        self.x_dp = dp + 2 - 4 * ((dp // 2) % 2)
        self.y_dp = dp + 4 - 8 * (dp // 4)
        self.xy_dp = self.x_dp + 4 - 8 * (dp // 4)
        self.sibling = (self.sibling_dp, z)
        self.far_dps = (self.x_dp, self.y_dp, self.xy_dp)
        self.far = tuple((d, z) for d in self.far_dps)
        self.x_side = (self.x_dp + self.sibling_dp - dp, z)
        self.y_side = (self.y_dp + self.sibling_dp - dp, z)
        self.line = tuple((dp, (z + k) % 4) for k in (1, 2, 3))

    def meet(self, devices):
        barrier = pltpu.get_barrier_semaphore()
        for device in devices:
            pl.semaphore_signal(barrier, inc=1, device_id=device, device_id_type=MESH)
        pl.semaphore_wait(barrier, len(devices))

    def meet_line(self):
        barrier = pltpu.get_barrier_semaphore()
        pl.semaphore_signal(barrier, inc=1, device_id=self.pair, device_id_type=MESH)

        @pl.when(self.inner)
        def _():
            pl.semaphore_signal(barrier, inc=1, device_id=self.middle, device_id_type=MESH)
            pl.semaphore_wait(barrier, 2)

        @pl.when(self.outer)
        def _():
            pl.semaphore_wait(barrier, 1)


def send(src, dst, send_sem, recv_sem, device):
    return pltpu.make_async_remote_copy(
        src_ref=src,
        dst_ref=dst,
        send_sem=send_sem,
        recv_sem=recv_sem,
        device_id=device,
        device_id_type=MESH,
    )


class LineSum:
    SEMS = 6

    def __init__(self, place, part, inbox, peer, total, sems, view):
        self.place, self.part, self.inbox, self.peer, self.total = place, part, inbox, peer, total
        self.sems, self.view = sems, view

    def up(self, k):
        s, v = self.sems, self.view
        return send(v(self.part, k), v(self.inbox, k), s.at[0, k], s.at[1, k], self.place.pair)

    def across(self, k):
        s, v = self.sems, self.view
        return send(v(self.part, k), v(self.peer, k), s.at[2, k], s.at[3, k], self.place.middle)

    def down(self, k):
        s, v = self.sems, self.view
        return send(v(self.total, k), v(self.total, k), s.at[4, k], s.at[5, k], self.place.pair)

    def push(self, k):
        @pl.when(self.place.outer)
        def _():
            self.up(k).start()

    def meet_up(self, k):
        @pl.when(self.place.inner)
        def _():
            self.up(k).wait_recv()
            mine, other = self.view(self.part, k), self.view(self.inbox, k)
            mine[...] = (mine[...].astype(jnp.float32) + other[...].astype(jnp.float32)).astype(
                jnp.bfloat16
            )
            self.across(k).start()

    def meet_across(self, k):
        @pl.when(self.place.inner)
        def _():
            self.across(k).wait_recv()
            mine, other = self.view(self.part, k), self.view(self.peer, k)
            self.view(self.total, k)[...] = (
                mine[...].astype(jnp.float32) + other[...].astype(jnp.float32)
            ).astype(jnp.bfloat16)
            self.down(k).start()

    def get(self, k):
        @pl.when(self.place.outer)
        def _():
            self.down(k).wait_recv()

    def finish(self, count):
        @pl.when(self.place.outer)
        def _():
            for k in range(count):
                self.up(k).wait_send()

        @pl.when(self.place.inner)
        def _():
            for k in range(count):
                self.across(k).wait_send()
                self.down(k).wait_send()


def chunk(ref, k):
    return ref.at[k]


def columns(ref, k, width):
    return ref.at[:, pl.ds(k * width, width)]


def row_live(lengths, rows):
    index = lax.broadcasted_iota(jnp.int32, (rows, 1), 0)
    return (index < lengths[0, 0] + lengths[0, 1]).astype(jnp.float32)


def encode_kernel(
    coords,
    lengths,
    counts,
    enc,
    grads,
    dec,
    attn,
    up,
    down,
    gain,
    bias,
    stream,
    grad_out,
    weights,
    vectors,
    counts_side,
    grads_side,
    counts_v,
    enc_v,
    grads_v,
    dec_v,
    work,
    places,
    part_a,
    inbox_a,
    peer_a,
    part_b,
    inbox_b,
    peer_b,
    load_sems,
    sems_a,
    sems_b,
    far_sems,
    side_sems,
    line_sems,
    pair_sems,
):
    place = Place()
    dp, z = place.dp, place.z
    chunks, rows, lanes = stream.shape
    width = chunks * lanes
    step = width // 4
    loads = [pltpu.make_async_copy(counts, counts_v, load_sems.at[0])]
    for j in range(4):
        loads.append(
            pltpu.make_async_copy(
                columns(enc, j, step), columns(enc_v, j, step), load_sems.at[1 + j]
            )
        )
    loads.append(pltpu.make_async_copy(grads, grads_v, load_sems.at[5]))
    for j in range(4):
        loads.append(
            pltpu.make_async_copy(
                columns(dec, j, step), columns(dec_v, j, step), load_sems.at[6 + j]
            )
        )
    for copy in loads:
        copy.start()
    for i, ref in enumerate((attn, up, down)):
        weights[i, dp] = ref[...]
    place.meet(place.far + (place.sibling,) + place.line)

    tile = vectors.at[dp * 4 + z]
    tile[...] = jnp.zeros_like(tile)
    tile[0:1, 0:64] = gain[...].astype(jnp.float32)
    tile[1:2, 0:64] = bias[...].astype(jnp.float32)
    line_out = [
        send(tile, tile, line_sems.at[0, i], line_sems.at[1, i], device)
        for i, device in enumerate(place.line)
    ]
    for copy in line_out:
        copy.start()

    def block_of(d):
        return weights.at[:, d]

    far_out = [
        send(block_of(dp), block_of(dp), far_sems.at[0, i], far_sems.at[1, i], device)
        for i, device in enumerate(place.far)
    ]
    far_in = [
        send(block_of(d), block_of(d), far_sems.at[0, i], far_sems.at[1, i], device)
        for i, (d, device) in enumerate(zip(place.far_dps, place.far))
    ]
    side_from = (dp,) + place.far_dps
    side = [
        send(block_of(d), block_of(d), side_sems.at[0, i], side_sems.at[1, i], place.sibling)
        for i, d in enumerate(side_from)
    ]
    for copy in far_out:
        copy.start()
    side[0].start()

    def lines(d):
        return vectors.at[pl.ds(d * 4, 4)]

    vec_far = [
        send(lines(dp), lines(dp), far_sems.at[2, i], far_sems.at[3, i], device)
        for i, device in enumerate(place.far)
    ]
    vec_side = [
        send(lines(d), lines(d), side_sems.at[2, i], side_sems.at[3, i], place.sibling)
        for i, d in enumerate(side_from)
    ]

    pair_out = [
        send(src, dst, pair_sems.at[0, i], pair_sems.at[1, i], place.sibling)
        for i, (src, dst) in enumerate(((counts_v, counts_side), (grads_v, grads_side)))
    ]

    own_rows = coords.shape[1]
    index = lax.broadcasted_iota(jnp.int32, (1, step), 1).astype(jnp.float32)
    freqs = jnp.exp(index * (-4.0 * math.log(10000.0) / width))
    for axis in range(2):
        along = jnp.broadcast_to(coords[axis : axis + 1, :], (own_rows, own_rows)).T
        angle = along[:, 0:1] * freqs
        places[2 * axis] = jnp.sin(angle)
        places[2 * axis + 1] = jnp.cos(angle)

    sum_a = LineSum(place, part_a, inbox_a, peer_a, stream, sems_a, chunk)
    sum_b = LineSum(place, part_b, inbox_b, peer_b, grad_out, sems_b, chunk)
    live = row_live(lengths, rows)
    own = pl.ds(pl.multiple_of(z * own_rows, own_rows), own_rows)
    per = step // lanes

    def encode(j):
        if j == 0:
            loads[0].wait()
            pair_out[0].start()
        loads[1 + j].wait()
        work[...] = contract_rows(counts_v[...], enc_v[:, j * step : (j + 1) * step])
        work[own, :] += places[j]
        for k in range(per):
            part_a[j * per + k] = work[:, k * lanes : (k + 1) * lanes].astype(jnp.bfloat16)
            sum_a.push(j * per + k)

    def decode(j):
        if j == 0:
            loads[5].wait()
            pair_out[1].start()
        loads[6 + j].wait()
        got = contract_rows(grads_v[...], dec_v[:, j * step : (j + 1) * step]) * live
        for k in range(per):
            part_b[j * per + k] = got[:, k * lanes : (k + 1) * lanes].astype(jnp.bfloat16)
            sum_b.push(j * per + k)

    produce = [functools.partial(encode, j) for j in range(4)]
    produce += [functools.partial(decode, j) for j in range(4)]
    ups = [functools.partial(sum_a.meet_up, k) for k in range(8)]
    ups += [functools.partial(sum_b.meet_up, k) for k in range(8)]
    acrosses = [functools.partial(sum_a.meet_across, k) for k in range(8)]
    acrosses += [functools.partial(sum_b.meet_across, k) for k in range(8)]

    def vectors_out():
        for copy in line_out:
            copy.wait_recv()
        for copy in vec_far + vec_side[:1]:
            copy.start()

    def weights_on():
        for i in range(3):
            far_in[i].wait_recv()
            side[1 + i].start()
            vec_far[i].wait_recv()
            vec_side[1 + i].start()

    made = 0
    for k in range(17):
        while made < 8 and made * per < k + per + 2:
            produce[made]()
            made += 1
        if k < 16:
            ups[k]()
        if k == 4:
            vectors_out()
        if k == 13:
            weights_on()
        if k >= 1:
            acrosses[k - 1]()
    for k in range(8):
        sum_a.get(k)
    for k in range(8):
        sum_b.get(k)
    sum_a.finish(8)
    sum_b.finish(8)
    for copy in line_out:
        copy.wait_send()
    for copy in far_out + vec_far:
        copy.wait_send()
    for copy in side + vec_side + pair_out:
        copy.wait()


def encode_call(coords, lengths, counts, enc, grads, dec, attn, up, down, gain, bias):
    genes, rows = counts.shape
    width = enc.shape[1]
    low, full = jnp.bfloat16, jnp.float32
    block = pltpu.VMEM((width // 128, rows, 128), low)
    return pl.pallas_call(
        encode_kernel,
        out_shape=(
            jax.ShapeDtypeStruct((width // 128, rows, 128), low),
            jax.ShapeDtypeStruct((width // 128, rows, 128), low),
            jax.ShapeDtypeStruct((3, 8) + attn.shape, low),
            jax.ShapeDtypeStruct((32, 8, 128), full),
            jax.ShapeDtypeStruct(counts.shape, low),
            jax.ShapeDtypeStruct(grads.shape, low),
        ),
        in_specs=[VMEM, SMEM, ANY, ANY, ANY, ANY, VMEM, VMEM, VMEM, VMEM, VMEM],
        out_specs=(VMEM, VMEM, VMEM, VMEM, ANY, ANY),
        scratch_shapes=[
            pltpu.VMEM((genes, rows), low),
            pltpu.VMEM((genes, width), low),
            pltpu.VMEM((genes, rows), low),
            pltpu.VMEM((genes, width), low),
            pltpu.VMEM((rows, width // 4), full),
            pltpu.VMEM((4, coords.shape[1], width // 4), full),
            block,
            block,
            block,
            block,
            block,
            block,
            DMA((10,)),
            DMA((6, 8)),
            DMA((6, 8)),
            DMA((4, 3)),
            DMA((4, 4)),
            DMA((2, 3)),
            DMA((2, 2)),
        ],
        compiler_params=pltpu.CompilerParams(
            collective_id=0, has_side_effects=True, vmem_limit_bytes=56 * MIB
        ),
        name="encode",
    )(coords, lengths, counts, enc, grads, dec, attn, up, down, gain, bias)


def exact(value):
    return value.astype(jnp.float32)


def low(value):
    return value.astype(jnp.bfloat16)


def rows_of(ref, k):
    return ref.at[pl.ds(k * 64, 64)]


def normalize(values):
    center = values - jnp.mean(values, axis=-1, keepdims=True)
    spread = jnp.mean(center * center, axis=-1, keepdims=True)
    scale = lax.rsqrt(spread + epsilon)
    return center * scale, scale


def norm_back(grad, gain, normed, scale):
    lifted = grad * gain
    return scale * (
        lifted
        - jnp.mean(lifted, axis=-1, keepdims=True)
        - normed * jnp.mean(lifted * normed, axis=-1, keepdims=True)
    )


def gelu_both(u):
    curve, factor = 0.044715, math.sqrt(2.0 / math.pi)
    square = u * u
    bent = jnp.tanh(factor * (u + curve * u * square))
    half = 0.5 * (1.0 + bent)
    slope = half + 0.5 * u * (1.0 - bent * bent) * (factor * (1.0 + 3.0 * curve * square))
    return u * half, slope


def layer_kernel(
    lengths,
    vectors,
    stream,
    branch,
    weights,
    counts,
    slopes,
    cells,
    grad_in,
    cells_four,
    grad_four,
    grads,
    sums,
    counts_far,
    slopes_far,
    qkv,
    key_masked,
    value_masked,
    soft,
    key_sum,
    value_sum,
    grad_mid,
    gains,
    offsets,
    part_m,
    part_o,
    part_s,
    part_f,
    inbox_m,
    inbox_o,
    peer_m,
    peer_o,
    peer_s,
    total_m,
    total_o,
    total_s,
    active,
    hidden,
    second,
    branch_rows,
    cat,
    first,
    outgoing,
    arriving,
    cells_out,
    grad_out,
    line_sems,
    side_sems,
    far_sems,
    pair_sems,
    four_sems,
):
    place = Place()
    group, width = cells.shape
    local = width // 4
    span = 128
    parts = group // span
    lane = lax.broadcasted_iota(jnp.int32, (1, span), 1)
    head_lanes = [low((lane // HEAD_DIM == h).astype(jnp.float32)) for h in range(2)]
    head_exact = [exact(h) for h in head_lanes]
    first_end, second_end = lengths[0, 0], lengths[0, 0] + lengths[0, 1]

    def slide_of(index):
        return (index >= first_end).astype(jnp.int32) + (index >= second_end).astype(jnp.int32)

    def rows(r):
        return slice(r * span, (r + 1) * span)

    def row_index(r):
        return lax.broadcasted_iota(jnp.int32, (span, 1), 0) + r * span

    def gathered(ref, r):
        return jnp.concatenate([ref[k, rows(r), :] for k in range(width // span)], axis=1)

    def matrix(i, start, stop):
        return weights[i, start:stop].reshape((stop - start) * span, width)

    def side_copy(ref, i):
        return send(ref.at[0], ref.at[1], side_sems.at[0, i], side_sems.at[1, i], place.sibling)

    side_active, side_hidden = side_copy(active, 0), side_copy(hidden, 1)
    side_second, side_branch = side_copy(second, 2), side_copy(branch_rows, 3)
    side_cat = side_copy(cat, 4)
    side_first, side_attn = side_copy(first.at[0], 5), side_copy(first.at[1], 6)

    pair_far = [
        send(src, dst.at[0], pair_sems.at[0, i], pair_sems.at[1, i], device)
        for i, (src, dst, device) in enumerate(
            ((counts, counts_far, place.far[1]), (slopes, slopes_far, place.far[0]))
        )
    ]
    pair_side = [
        send(dst.at[0], dst.at[1], pair_sems.at[0, 2 + i], pair_sems.at[1, 2 + i], place.sibling)
        for i, dst in enumerate((counts_far, slopes_far))
    ]
    cells_to = (place.sibling, place.far[0], place.x_side)
    grad_to = (place.sibling, place.far[1], place.y_side)

    def other_core(d):
        return d + 1 - 2 * (d % 2)

    x_dp, y_dp, xy_dp = place.far_dps
    own_pair, x_pair, y_pair = (place.dp, y_dp), (x_dp, xy_dp), (place.dp, x_dp)
    cells_blocks = (own_pair, tuple(map(other_core, own_pair)), x_pair, tuple(map(other_core, x_pair)))
    x_row = (y_dp, xy_dp)
    grad_blocks = (y_pair, tuple(map(other_core, y_pair)), x_row, tuple(map(other_core, x_row)))

    def four_copy(i, out, four, devices, t, r):
        block = pl.ds(r * span, span)
        return send(
            out.at[t, block],
            four.at[1 + t, block],
            four_sems.at[0, i, t, r],
            four_sems.at[1, i, t, r],
            devices[t],
        )

    def cells_copy(t, r):
        return four_copy(0, cells_out, cells_four, cells_to, t, r)

    def grad_copy(t, r):
        return four_copy(1, grad_out, grad_four, grad_to, t, r)

    def spread(ref, out, four, blocks, copy, r):
        for t, pair in enumerate(blocks):
            for n, d in enumerate(pair):
                block = ref[rows(r), pl.ds(pl.multiple_of(d * span, span), span)]
                at = slice(n * span, (n + 1) * span)
                if t == 0:
                    four[0, rows(r), at] = block
                else:
                    out[t - 1, rows(r), at] = block
            if t > 0:
                copy(t - 1, r).start()

    def line_sum(i, part, inbox, peer, total):
        return LineSum(place, part, inbox, peer, total, line_sems.at[i], rows_of)

    sum_m = line_sum(0, part_m, inbox_m, peer_m, total_m)
    sum_o = line_sum(1, part_o, inbox_o, peer_o, total_o)
    sum_s = line_sum(2, part_s, inbox_m, peer_s, total_s)
    sum_f = line_sum(3, part_f, inbox_m, peer_m, total_s)

    place.meet(place.far + (place.sibling, place.x_side, place.y_side) + place.line)
    for copy in pair_far:
        copy.start()

    for k in range(2 * width // span):
        for ref, row in ((gains, 0), (offsets, 1)):
            ref[0:1, k * span : (k + 1) * span] = jnp.concatenate(
                [vectors[2 * k + i, row : row + 1, 0:64] for i in range(2)], axis=1
            )
    gain_a, gain_b = gains[0:1, :width], gains[0:1, width:]
    offset_a, offset_b = offsets[0:1, :width], offsets[0:1, width:]
    sums[...] = jnp.zeros_like(sums)
    key_sum[...] = jnp.zeros_like(key_sum)
    value_sum[...] = jnp.zeros_like(value_sum)

    def project(r):
        normed, _ = normalize(exact(gathered(stream, r)))
        value = low(normed * gain_a + offset_a)
        first[0, 0, rows(r), :] = value
        qkv[rows(r), :] = low(contract_cols(value, matrix(0, 0, 6)))
        for p in range(2):
            for ref, at in ((key_masked, local), (value_masked, 2 * local)):
                block = qkv[rows(r), at + p * span : at + (p + 1) * span]
                for h in range(2):
                    ref[p, h * group + r * span : h * group + (r + 1) * span, :] = (
                        block * head_lanes[h]
                    )

    def attend(r):
        same = slide_of(row_index(r)) == slide_of(
            lax.broadcasted_iota(jnp.int32, (1, group), 1)
        )
        for p in range(2):
            query = qkv[rows(r), p * span : (p + 1) * span]
            scores = contract_cols(query, key_masked[p]) * (1.0 / math.sqrt(HEAD_DIM))
            for h in range(2):
                own = jnp.where(same, scores[:, h * group : (h + 1) * group], -1e30)
                raised = jnp.exp(own - jnp.max(own, axis=-1, keepdims=True))
                soft[p, rows(r), h * group : (h + 1) * group] = raised / jnp.sum(
                    raised, axis=-1, keepdims=True
                )
            cat[0, rows(r), 3 * local + p * span : 3 * local + (p + 1) * span] = low(
                product(low(soft[p, rows(r), :]), value_masked[p])
            )
        part_m[rows(r), :] = low(product(cat[0, rows(r), 3 * local :], matrix(0, 6, 8)))
        push(sum_m, r)

    def middle(r):
        return exact(gathered(stream, r)) + exact(total_m[rows(r), :])

    def feed(r):
        get(sum_m, r)
        normed, _ = normalize(middle(r))
        value = low(normed * gain_b + offset_b)
        second[0, rows(r), :] = value
        act, slope = gelu_both(contract_cols(value, matrix(1, 0, 8)))
        active[0, rows(r), :] = low(act)
        grad = gathered(branch, r)
        branch_rows[0, rows(r), :] = grad
        back = low(contract_cols(grad, matrix(2, 0, 8)) * slope)
        hidden[0, rows(r), :] = back
        part_s[rows(r), :] = low(product(back, matrix(1, 0, 8)))
        push(sum_s, r)
        part_o[rows(r), :] = low(product(active[0, rows(r), :], matrix(2, 0, 8)))

    def attend_back(r):
        get(sum_s, r)
        normed, scale = normalize(middle(r))
        grad = exact(total_s[rows(r), :])
        sums[1:2, :] += jnp.sum(grad * normed, axis=0, keepdims=True)
        sums[3:4, :] += jnp.sum(grad, axis=0, keepdims=True)
        mid = exact(branch_rows[0, rows(r), :]) + norm_back(grad, gain_b, normed, scale)
        grad_mid[rows(r), :] = mid
        first[1, 0, rows(r), :] = low(mid)
        back = low(contract_cols(low(mid), matrix(0, 6, 8)))
        for p in range(2):
            out = back[:, p * span : (p + 1) * span]
            slopes = contract_cols(out, value_masked[p])
            marks = []
            for h in range(2):
                block = soft[p, rows(r), h * group : (h + 1) * group]
                slope = slopes[:, h * group : (h + 1) * group]
                inner = jnp.sum(slope * block, axis=-1, keepdims=True)
                marks.append(low(block * (slope - inner)))
            scale_q = 1.0 / math.sqrt(HEAD_DIM)
            cat[0, rows(r), p * span : (p + 1) * span] = low(
                product(jnp.concatenate(marks, axis=1), key_masked[p]) * scale_q
            )
            query = qkv[rows(r), p * span : (p + 1) * span]
            at = slice(p * span, (p + 1) * span)
            key_sum[:, at] += contract_rows(
                jnp.concatenate(marks, axis=0),
                jnp.concatenate([query * lanes for lanes in head_lanes], axis=0),
            )
            value_sum[:, at] += contract_rows(
                jnp.concatenate(
                    [low(soft[p, rows(r), h * group : (h + 1) * group]) for h in range(2)], axis=0
                ),
                jnp.concatenate([out * lanes for lanes in head_lanes], axis=0),
            )

    def project_back(r):
        if r == 0:
            sum_s.finish(8)
            cat[0, :, local : 2 * local] = low(key_sum[...] * (1.0 / math.sqrt(HEAD_DIM)))
            cat[0, :, 2 * local : 3 * local] = low(value_sum[...])
        part_f[rows(r), :] = low(product(cat[0, rows(r), : 3 * local], matrix(0, 0, 6)))
        push(sum_f, r)

    def finish_in(r):
        get(sum_f, r)
        normed, scale = normalize(exact(gathered(stream, r)))
        grad = exact(total_s[rows(r), :])
        sums[0:1, :] += jnp.sum(grad * normed, axis=0, keepdims=True)
        sums[2:3, :] += jnp.sum(grad, axis=0, keepdims=True)
        grad_in[rows(r), :] = low(grad_mid[rows(r), :] + norm_back(grad, gain_a, normed, scale))
        spread(grad_in, grad_out, grad_four, grad_blocks, grad_copy, r)

    def finish_out(r):
        get(sum_o, r)
        live = (row_index(r) < second_end).astype(jnp.float32)
        cells[rows(r), :] = low((middle(r) + exact(total_o[rows(r), :])) * live)
        spread(cells, cells_out, cells_four, cells_blocks, cells_copy, r)

    def push(total, r):
        total.push(2 * r)
        total.push(2 * r + 1)

    def get(total, r):
        total.get(2 * r)
        total.get(2 * r + 1)

    chips = tuple(d // 2 for d in place.far_dps) + (place.chip,)

    def lanes_of(ref, slot, chip):
        start = pl.multiple_of((chip * 2 + place.core) * span, span)
        return ref[slot, :, pl.ds(start, span)]

    def far_copy(i, q):
        return send(
            outgoing.at[i, q],
            arriving.at[i, q],
            far_sems.at[0, i, q],
            far_sems.at[1, i, q],
            place.far[q],
        )

    def keep(i, q, value):
        if q == 3:
            grads[i] = value
        else:
            outgoing[i, q] = low(value)
            far_copy(i, q).start()

    def weight_grad(i, left, right, half):
        pair = chips[2 * half : 2 * half + 2]
        got = sum(
            contract_rows(
                jnp.concatenate([lanes_of(left, slot, chip) for chip in pair], axis=1),
                right[slot],
            )
            for slot in range(2)
        )
        for k in range(2):
            keep(i, 2 * half + k, got[k * span : (k + 1) * span])

    def attn_grad(q):
        kind = chips[q] // 3
        keep(
            0,
            q,
            sum(
                contract_rows(lanes_of(cat, slot, chips[q]), first[kind, slot]) for slot in range(2)
            ),
        )

    def run(word):
        name, k = word[:-1], int(word[-1])
        if name[0] in "ux":
            total = dict(m=sum_m, o=sum_o, s=sum_s, f=sum_f)[name[1]]
            (total.meet_up if name[0] == "u" else total.meet_across)(k)
        else:
            steps[name](k)

    def start_feed_sides(_):
        for copy in (side_hidden, side_second, side_active, side_branch):
            copy.start()

    def start_attn_sides(_):
        side_cat.start()
        side_attn.start()

    def pass_on(i):
        pair_far[i].wait_recv()
        pair_side[i].start()

    def up_grad(half):
        if half == 0:
            side_hidden.wait_recv()
            side_second.wait_recv()
        weight_grad(1, hidden, second, half)

    def down_grad(half):
        if half == 0:
            side_active.wait_recv()
            side_branch.wait_recv()
        weight_grad(2, active, branch_rows, half)

    def attn_grads(half):
        if half == 0:
            side_first.wait_recv()
            side_attn.wait_recv()
            side_cat.wait_recv()
        attn_grad(2 * half)
        attn_grad(2 * half + 1)

    steps = dict(
        A=project,
        B=attend,
        C=feed,
        D=attend_back,
        G=project_back,
        E=finish_in,
        F=finish_out,
        P=lambda r: push(sum_o, r),
        S=start_feed_sides,
        T=start_attn_sides,
        X=pass_on,
        H=up_grad,
        L=down_grad,
        K=attn_grads,
    )
    for r in range(parts):
        project(r)
    side_first.start()
    for word in SCHEDULE:
        run(word)
    for i in (2, 1, 0):
        for q in range(3):
            far_copy(i, q).wait_recv()
        grads[i] = grads[i] + sum(exact(arriving[i, q]) for q in range(3))
    for total in (sum_m, sum_o, sum_f):
        total.finish(8)
    for i in range(3):
        for q in range(3):
            far_copy(i, q).wait_send()
    for t in range(3):
        for r in range(parts):
            cells_copy(t, r).wait()
            grad_copy(t, r).wait()
    for copy in pair_far:
        copy.wait_send()
    for copy in pair_side:
        copy.wait()
    for copy in (
        side_active,
        side_hidden,
        side_second,
        side_branch,
        side_cat,
        side_first,
        side_attn,
    ):
        copy.wait_send()


SCHEDULE = (
    "B0", "um0", "um1", "B1", "xm0", "um2", "B2", "xm1", "um3", "um4", "xm2", "B3", "xm3", "um5",
    "um6", "xm4", "um7", "xm5", "xm6", "C0", "us0", "us1", "C1", "xm7", "us2", "C2", "xs0", "P0",
    "us3", "xs1", "C3", "P1", "xs2", "us4", "S0", "us5", "D0", "xs3", "uo0", "xs4", "xs5", "uo1",
    "us6", "P2", "xo0", "D1", "us7", "xs6", "uo2", "xo1", "H0", "L0", "uo3", "D2", "xs7", "P3",
    "uo4", "D3", "xo2", "G0", "T0", "G1", "uo5", "F0", "uo6", "xo3", "xo4", "H1", "G2", "xo5",
    "uf0", "xo6", "uf1", "xf0", "K0", "G3", "X0", "X1", "uf2", "uf3", "xf1", "uf4", "xf2", "xf3",
    "uf5", "xf4", "F1", "uf6", "L1", "xf5", "E0", "uo7", "E1", "E2", "uf7", "F2", "K1", "xf6",
    "xo7", "xf7", "F3", "E3",
)


def layer_call(lengths, vectors, stream, branch, weights, counts, slopes):
    chunks, group, lanes = stream.shape
    width = chunks * lanes
    half, full = jnp.bfloat16, jnp.float32
    plain = pltpu.VMEM((group, width), half)
    double = pltpu.VMEM((2, group, width), half)
    return pl.pallas_call(
        layer_kernel,
        out_shape=(
            jax.ShapeDtypeStruct((group, width), half),
            jax.ShapeDtypeStruct((group, width), half),
            jax.ShapeDtypeStruct((4, group, 256), half),
            jax.ShapeDtypeStruct((4, group, 256), half),
            jax.ShapeDtypeStruct((3, 128, width), full),
            jax.ShapeDtypeStruct((8, width), full),
            jax.ShapeDtypeStruct((2,) + counts.shape, half),
            jax.ShapeDtypeStruct((2,) + slopes.shape, half),
        ),
        in_specs=[SMEM, VMEM, VMEM, VMEM, VMEM, ANY, ANY],
        out_specs=(VMEM,) * 6 + (ANY, ANY),
        scratch_shapes=[
            pltpu.VMEM((group, 3 * width // 4), half),
            pltpu.VMEM((2, 2 * group, 128), half),
            pltpu.VMEM((2, 2 * group, 128), half),
            pltpu.VMEM((2, group, 2 * group), full),
            pltpu.VMEM((group, width // 4), full),
            pltpu.VMEM((group, width // 4), full),
            pltpu.VMEM((group, width), full),
            pltpu.VMEM((1, 2 * width), full),
            pltpu.VMEM((1, 2 * width), full),
        ]
        + [plain] * 12
        + [double] * 5
        + [
            pltpu.VMEM((2, 2, group, width), half),
            pltpu.VMEM((3, 3, 128, width), half),
            pltpu.VMEM((3, 3, 128, width), half),
            pltpu.VMEM((3, group, 256), half),
            pltpu.VMEM((3, group, 256), half),
            DMA((4, 6, 8)),
            DMA((2, 7)),
            DMA((2, 3, 3)),
            DMA((2, 4)),
            DMA((2, 2, 3, 4)),
        ],
        compiler_params=pltpu.CompilerParams(
            collective_id=1, has_side_effects=True, vmem_limit_bytes=60 * MIB
        ),
        name="layer",
    )(lengths, vectors, stream, branch, weights, counts, slopes)


def genes_kernel(
    counts,
    counts_side,
    counts_far,
    slopes,
    slopes_side,
    slopes_far,
    enc,
    dec,
    cells,
    grad_in,
    cells_four,
    grad_four,
    sums,
    logits,
    gene_grad,
    enc_grad,
    dec_grad,
    small,
    counts_v,
    slopes_v,
    outgoing,
    arriving,
    sums_side,
    sums_chip,
    sums_far,
    load_sems,
    far_sems,
    sum_sems,
):
    place = Place()
    genes, group = counts.shape
    span = 128
    bounds = [min(i * GENE_STEP, genes) for i in range(-(-genes // GENE_STEP) + 1)]
    pieces = list(zip(bounds[:-1], bounds[1:]))

    def load(src, dst, i):
        return pltpu.make_async_copy(src, dst, load_sems.at[i])

    loads = [
        [
            load(src, ref.at[t], 4 * i + t)
            for t, src in enumerate((own, side, far.at[0], far.at[1]))
        ]
        for i, (ref, own, side, far) in enumerate(
            (
                (counts_v, counts, counts_side, counts_far),
                (slopes_v, slopes, slopes_side, slopes_far),
            )
        )
    ]
    tables = [
        [load(src.at[:, pl.ds(t * group, group)], ref.at[t], 8 + 2 * i + t) for t in range(2)]
        for i, (src, ref) in enumerate(((enc, counts_v), (dec, slopes_v)))
    ]
    for copy in loads[0] + loads[1]:
        copy.start()
    tail = outgoing.shape[1] - GENE_TAIL
    for i in range(2):
        outgoing[i, tail:, :] = jnp.zeros((GENE_TAIL, span), jnp.bfloat16)
    place.meet(place.far + (place.sibling,))

    side = send(sums, sums_side, sum_sems.at[0, 0], sum_sems.at[1, 0], place.sibling)
    side.start()
    far_sums = [
        send(sums_chip, sums_far.at[q], sum_sems.at[0, 1 + q], sum_sems.at[1, 1 + q], device)
        for q, device in enumerate(place.far)
    ]

    def far_copy(i, k):
        block = pl.ds(k * GENE_STEP, min(GENE_STEP, outgoing.shape[1] - k * GENE_STEP))
        return send(
            outgoing.at[i, block],
            arriving.at[i, block],
            far_sems.at[0, i, k],
            far_sems.at[1, i, k],
            place.far[i],
        )

    def reduce_part(i, k):
        left, right, result = (
            (counts_v, grad_four, enc_grad),
            (slopes_v, cells_four, dec_grad),
        )[i]
        if k == 0:
            for copy in loads[i]:
                copy.wait()
        start, stop = pieces[k]
        got = sum(product(left[t, start:stop, :], right[t]) for t in range(4))
        result[start:stop, :] = got[:, :span]
        outgoing[i, start:stop, :] = low(got[:, span:])
        far_copy(i, k).start()
        if k == len(pieces) - 1:
            for copy in tables[i]:
                copy.start()

    def reduce_end(i, result):
        for k, (start, stop) in enumerate(pieces):
            far_copy(i, k).wait_recv()
            result[start:stop, :] = result[start:stop, :] + exact(arriving[i, start:stop, :])

    def expand(i, ref, right, result):
        for copy in tables[i]:
            copy.wait()
        for start, stop in pieces:
            result[start:stop, :] = low(
                sum(
                    contract_cols(ref[t, start:stop, :], right[:, t * group : (t + 1) * group])
                    for t in range(2)
                )
            )

    order = [(0, 0), (0, 1)]
    for k in range(2, len(pieces)):
        order += [(1, k - 2), (0, k)]
    order += [(1, k) for k in range(max(len(pieces) - 2, 0), len(pieces))]
    for i, k in order:
        reduce_part(i, k)
    side.wait()
    sums_chip[...] = sums[...] + sums_side[...]
    for copy in far_sums:
        copy.start()
    expand(0, counts_v, grad_in, gene_grad)
    expand(1, slopes_v, cells, logits)
    for copy in far_sums:
        copy.wait_recv()
    small[...] = sums_chip[...] + (sums_far[0] + sums_far[1] + sums_far[2])
    reduce_end(0, enc_grad)
    reduce_end(1, dec_grad)
    for i in range(2):
        for k in range(len(pieces)):
            far_copy(i, k).wait_send()
    for copy in far_sums:
        copy.wait_send()


GENE_STEP = 848
GENE_TAIL = 16


def genes_call(tables, rows):
    genes, group = tables[0].shape
    sums = rows[-1]
    padded = -(-genes // 16) * 16
    steps = -(-genes // GENE_STEP)
    half, full = jnp.bfloat16, jnp.float32
    return pl.pallas_call(
        genes_kernel,
        out_shape=(
            jax.ShapeDtypeStruct((genes, group), half),
            jax.ShapeDtypeStruct((genes, group), half),
            jax.ShapeDtypeStruct((genes, 128), full),
            jax.ShapeDtypeStruct((genes, 128), full),
            jax.ShapeDtypeStruct(sums.shape, full),
        ),
        in_specs=[ANY] * len(tables) + [VMEM] * len(rows),
        out_specs=(VMEM,) * 5,
        scratch_shapes=[
            pltpu.VMEM((4, genes, group), half),
            pltpu.VMEM((4, genes, group), half),
            pltpu.VMEM((2, padded, 128), half),
            pltpu.VMEM((2, padded, 128), half),
            pltpu.VMEM(sums.shape, full),
            pltpu.VMEM(sums.shape, full),
            pltpu.VMEM((3,) + sums.shape, full),
            DMA((12,)),
            DMA((2, 2, steps)),
            DMA((2, 4)),
        ],
        compiler_params=pltpu.CompilerParams(
            collective_id=2, has_side_effects=True, vmem_limit_bytes=60 * MIB
        ),
        name="genes",
    )(*tables, *rows)


def fast_body(
    gene_counts,
    coords,
    lengths,
    enc_weight,
    dec_weight,
    attn_weight,
    up_weight,
    down_weight,
    ln_gain,
    ln_bias,
    logit_grad,
):
    model_width = enc_weight.shape[1]
    counts, slopes, dec = gene_counts.T, logit_grad.T, dec_weight.T
    stream_in, grad_out, weights, vectors, counts_side, slopes_side = encode_call(
        coords,
        lengths,
        counts,
        enc_weight,
        slopes,
        dec,
        attn_weight,
        up_weight,
        down_weight,
        ln_gain[None],
        ln_bias[None],
    )
    cells, grad_in, cells_four, grad_four, layer_grad, sums, counts_far, slopes_far = layer_call(
        lengths, vectors, stream_in, grad_out, weights, counts, slopes
    )
    logits, gene_grad, enc_grad, dec_grad, small = genes_call(
        (counts, counts_side, counts_far, slopes, slopes_side, slopes_far, enc_weight, dec),
        (cells, grad_in, cells_four, grad_four, sums),
    )
    small = small[:4].reshape(-1)
    place = lax.axis_index("dp") * 4 + lax.axis_index("gene")
    gain_grad = lax.dynamic_slice_in_dim(small[: 2 * model_width], place * 64, 64)
    bias_grad = lax.dynamic_slice_in_dim(
        small[2 * model_width : 3 * model_width], place * 32, 32
    )
    mid_bias_grad = lax.dynamic_slice_in_dim(small[3 * model_width :], place * 32, 32)
    return (
        logits.T,
        gene_grad.T,
        enc_grad,
        dec_grad.T,
        layer_grad[0],
        layer_grad[1],
        layer_grad[2],
        gain_grad,
        bias_grad,
        mid_bias_grad,
    )


def solution(mesh):
    fast = dict(mesh.shape) == {"dp": 8, "gene": 4}
    in_specs = (
        P("dp", "gene"),
        P(None, ("dp", "gene")),
        P("dp", None),
        P("gene", None),
        P(None, "gene"),
        P(("dp", "gene"), None),
        P(("dp", "gene"), None),
        P(("dp", "gene"), None),
        P(("dp", "gene")),
        P(("dp", "gene")),
        P("dp", "gene"),
    )
    out_specs = (
        P("dp", "gene"),
        P("dp", "gene"),
        P("gene", "dp"),
        P("dp", "gene"),
        P(("dp", "gene"), None),
        P(("dp", "gene"), None),
        P(("dp", "gene"), None),
        P(("dp", "gene")),
        P(("dp", "gene")),
        P(("dp", "gene")),
    )
    return jax.shard_map(
        fast_body if fast else body, mesh=mesh, in_specs=in_specs, out_specs=out_specs, check_vma=False)
```

```python
import functools
import math

import jax
import jax.numpy as jnp
from jax import lax
from jax.experimental import pallas as pl
from jax.experimental.pallas import tpu as pltpu
from jax.sharding import PartitionSpec as P

HEADS = 16
HEAD_DIM = 64


epsilon = 1e-05


def norm_rows(values, gain, offset):
    center = values - jnp.mean(values, axis=-1, keepdims=True)
    spread = jnp.mean(center * center, axis=-1, keepdims=True)
    return center * lax.rsqrt(spread + epsilon) * gain + offset


def gelu_tanh(values):
    return jax.nn.gelu(values, approximate=True)


def positions(coords, model_width):
    indices = jnp.arange(model_width // 4).astype(coords.dtype)
    freqs = jnp.exp(indices * (-4.0 * math.log(10000.0) / model_width))
    along_x = coords[0][:, None] * freqs[None, :]
    along_y = coords[1][:, None] * freqs[None, :]
    return jnp.concatenate(
        [jnp.sin(along_x), jnp.cos(along_x), jnp.sin(along_y), jnp.cos(along_y)], axis=1
    )


def slide_ids(slide_lengths, length_all):
    places = jnp.arange(length_all, dtype=jnp.int32)
    return (places >= slide_lengths[0]).astype(jnp.int32) + (
        places >= slide_lengths[0] + slide_lengths[1]
    ).astype(jnp.int32)


def product(left, right):
    return jnp.dot(left, right, preferred_element_type=jnp.float32)


def contract_rows(left, right):
    return lax.dot_general(
        left, right, (((0,), (0,)), ((), ())), preferred_element_type=jnp.float32
    )


def contract_cols(left, right):
    return lax.dot_general(
        left, right, (((1,), (1,)), ((), ())), preferred_element_type=jnp.float32
    )


def body(
    gene_counts,
    coords,
    lengths,
    enc_weight,
    dec_weight,
    attn_weight,
    up_weight,
    down_weight,
    ln_gain,
    ln_bias,
    logit_grad,
):
    model_width = enc_weight.shape[1]
    group_rows = gene_counts.shape[0]
    own_rows = coords.shape[1]
    gene_index = lax.axis_index("gene")
    score_scale = 1.0 / math.sqrt(HEAD_DIM)
    slide_all = slide_ids(lengths[0], group_rows)
    slide_own = lax.dynamic_slice_in_dim(slide_all, gene_index * own_rows, own_rows)
    live_rows = (slide_all < 2).astype(jnp.bfloat16)[:, None]
    attn_full, up_full, down_full, gain_full, bias_full = (
        lax.all_gather(attn_weight, ("dp", "gene"), axis=0, tiled=True),
        lax.all_gather(up_weight, ("dp", "gene"), axis=0, tiled=True),
        lax.all_gather(down_weight, ("dp", "gene"), axis=0, tiled=True),
        lax.all_gather(ln_gain, ("dp", "gene"), axis=0, tiled=True),
        lax.all_gather(ln_bias, ("dp", "gene"), axis=0, tiled=True),
    )
    norm_gains = gain_full.astype(jnp.float32)
    offsets = bias_full.astype(jnp.float32)
    proj_weight = attn_full[: 3 * model_width]
    out_weight = attn_full[3 * model_width :]
    embedded = lax.psum_scatter(
        product(gene_counts, enc_weight).astype(jnp.bfloat16),
        "gene",
        scatter_dimension=0,
        tiled=True,
    ).astype(jnp.float32)
    stream_in = embedded + positions(coords, model_width)
    first_normed, first_pull = jax.vjp(
        norm_rows, stream_in, norm_gains[:model_width], offsets[:model_width]
    )
    first_low = first_normed.astype(jnp.bfloat16)
    projected = contract_cols(first_low, proj_weight).astype(jnp.bfloat16)
    queries = projected[:, :model_width].reshape(own_rows, HEADS, HEAD_DIM)
    keyval_all = lax.all_gather(projected[:, model_width:], "gene", axis=0, tiled=True)
    keys_all = keyval_all[:, :model_width].reshape(group_rows, HEADS, HEAD_DIM)
    values_all = keyval_all[:, model_width:].reshape(group_rows, HEADS, HEAD_DIM)
    same_slide = (slide_own[:, None] == slide_all[None, :])[None]
    scores = (
        jnp.einsum("qhd,khd->hqk", queries, keys_all, preferred_element_type=jnp.float32)
        * score_scale
    )
    scores = jnp.where(same_slide, scores, -1e30)
    row_max = jnp.max(scores, axis=-1, keepdims=True)
    raised = jnp.exp(scores - row_max)
    soft = raised / jnp.sum(raised, axis=-1, keepdims=True)
    soft_low = soft.astype(jnp.bfloat16)
    attended = jnp.einsum("hqk,khd->qhd", soft_low, values_all, preferred_element_type=jnp.float32)
    attended = attended.reshape(own_rows, model_width).astype(jnp.bfloat16)
    stream_mid = stream_in + product(attended, out_weight)
    second_normed, second_pull = jax.vjp(
        norm_rows, stream_mid, norm_gains[model_width:], offsets[model_width:]
    )
    second_low = second_normed.astype(jnp.bfloat16)
    hidden_pre = contract_cols(second_low, up_full)
    active, gelu_pull = jax.vjp(gelu_tanh, hidden_pre)
    active_low = active.astype(jnp.bfloat16)
    stream_out = stream_mid + product(active_low, down_full)
    cells_low = stream_out.astype(jnp.bfloat16)
    cells_all = lax.all_gather(cells_low, "gene", axis=0, tiled=True)
    logits_full = product(cells_all, dec_weight)
    logits = (logits_full * live_rows.astype(jnp.float32)).astype(jnp.bfloat16)
    masked_grad = logit_grad * live_rows
    grad_out = lax.psum_scatter(
        contract_cols(masked_grad, dec_weight).astype(jnp.bfloat16),
        "gene",
        scatter_dimension=0,
        tiled=True,
    ).astype(jnp.float32)
    dec_part = contract_rows(cells_all, masked_grad)
    grad_branch = grad_out.astype(jnp.bfloat16)
    down_part = contract_rows(active_low, grad_branch)
    grad_active = contract_cols(grad_branch, down_full)
    grad_hidden = gelu_pull(grad_active)[0].astype(jnp.bfloat16)
    up_part = contract_rows(grad_hidden, second_low)
    grad_second = product(grad_hidden, up_full)
    grad_mid_norm, gain_second, bias_second = second_pull(grad_second)
    grad_mid = grad_out + grad_mid_norm
    grad_attn = grad_mid.astype(jnp.bfloat16)
    out_part = contract_rows(attended, grad_attn)
    grad_attended = (
        contract_cols(grad_attn, out_weight).astype(jnp.bfloat16).reshape(own_rows, HEADS, HEAD_DIM)
    )
    grad_soft = jnp.einsum(
        "qhd,khd->hqk", grad_attended, values_all, preferred_element_type=jnp.float32
    )
    grad_scores = soft * (grad_soft - jnp.sum(grad_soft * soft, axis=-1, keepdims=True))
    grad_scores = grad_scores.astype(jnp.bfloat16)
    grad_query = (
        jnp.einsum("hqk,khd->qhd", grad_scores, keys_all, preferred_element_type=jnp.float32)
        * score_scale
    )
    grad_query = grad_query.reshape(own_rows, model_width).astype(jnp.bfloat16)
    grad_keys = (
        jnp.einsum("hqk,qhd->khd", grad_scores, queries, preferred_element_type=jnp.float32)
        * score_scale
    )
    grad_values = jnp.einsum(
        "hqk,qhd->khd", soft_low, grad_attended, preferred_element_type=jnp.float32
    )
    keyval_part = jnp.concatenate(
        [grad_keys.reshape(group_rows, model_width), grad_values.reshape(group_rows, model_width)],
        axis=1,
    )
    grad_keyval = lax.psum_scatter(
        keyval_part.astype(jnp.bfloat16), "gene", scatter_dimension=0, tiled=True
    )
    grad_proj = jnp.concatenate([grad_query, grad_keyval], axis=1)
    proj_part = contract_rows(grad_proj, first_low)
    grad_first = product(grad_proj, proj_weight)
    grad_in_norm, gain_first, bias_first = first_pull(grad_first)
    grad_in = (grad_mid + grad_in_norm).astype(jnp.bfloat16)
    grad_in_all = lax.all_gather(grad_in, "gene", axis=0, tiled=True)
    gene_grad = contract_cols(grad_in_all, enc_weight).astype(jnp.bfloat16)
    enc_part = contract_rows(gene_counts, grad_in_all)
    enc_grad, dec_grad = (
        lax.psum_scatter(enc_part, "dp", scatter_dimension=1, tiled=True),
        lax.psum_scatter(dec_part, "dp", scatter_dimension=0, tiled=True),
    )
    attn_part = jnp.concatenate([proj_part, out_part], axis=0)
    gain_part = jnp.concatenate([gain_first, gain_second], axis=0)
    attn_grad, up_grad, down_grad, gain_grad, bias_grad, mid_bias_grad = (
        lax.psum_scatter(attn_part, ("dp", "gene"), scatter_dimension=0, tiled=True),
        lax.psum_scatter(up_part, ("dp", "gene"), scatter_dimension=0, tiled=True),
        lax.psum_scatter(down_part, ("dp", "gene"), scatter_dimension=0, tiled=True),
        lax.psum_scatter(gain_part, ("dp", "gene"), scatter_dimension=0, tiled=True),
        lax.psum_scatter(bias_first, ("dp", "gene"), scatter_dimension=0, tiled=True),
        lax.psum_scatter(bias_second, ("dp", "gene"), scatter_dimension=0, tiled=True),
    )
    return (
        logits,
        gene_grad,
        enc_grad,
        dec_grad,
        attn_grad,
        up_grad,
        down_grad,
        gain_grad,
        bias_grad,
        mid_bias_grad,
    )


MESH = pl.DeviceIdType.MESH
MIB = 2**20
VMEM = pl.BlockSpec(memory_space=pltpu.VMEM)
SMEM = pl.BlockSpec(memory_space=pltpu.SMEM)
ANY = pl.BlockSpec(memory_space=pl.ANY)
DMA = pltpu.SemaphoreType.DMA


class Place:
    def __init__(self):
        self.dp = dp = lax.axis_index("dp")
        self.z = z = lax.axis_index("gene")
        self.core = dp % 2
        self.chip = dp // 2
        self.inner = z * (3 - z) > 0
        self.outer = z * (3 - z) == 0
        self.pair = (dp, z + 1 - 2 * (z % 2))
        self.middle = (dp, 3 - z)
        self.sibling_dp = dp + 1 - 2 * (dp % 2)
        self.x_dp = dp + 2 - 4 * ((dp // 2) % 2)
        self.y_dp = dp + 4 - 8 * (dp // 4)
        self.xy_dp = self.x_dp + 4 - 8 * (dp // 4)
        self.sibling = (self.sibling_dp, z)
        self.far_dps = (self.x_dp, self.y_dp, self.xy_dp)
        self.far = tuple((d, z) for d in self.far_dps)
        self.x_side = (self.x_dp + self.sibling_dp - dp, z)
        self.y_side = (self.y_dp + self.sibling_dp - dp, z)
        self.line = tuple((dp, (z + k) % 4) for k in (1, 2, 3))

    def meet(self, devices):
        barrier = pltpu.get_barrier_semaphore()
        for device in devices:
            pl.semaphore_signal(barrier, inc=1, device_id=device, device_id_type=MESH)
        pl.semaphore_wait(barrier, len(devices))

    def meet_line(self):
        barrier = pltpu.get_barrier_semaphore()
        pl.semaphore_signal(barrier, inc=1, device_id=self.pair, device_id_type=MESH)

        @pl.when(self.inner)
        def _():
            pl.semaphore_signal(barrier, inc=1, device_id=self.middle, device_id_type=MESH)
            pl.semaphore_wait(barrier, 2)

        @pl.when(self.outer)
        def _():
            pl.semaphore_wait(barrier, 1)


def send(src, dst, send_sem, recv_sem, device):
    return pltpu.make_async_remote_copy(
        src_ref=src,
        dst_ref=dst,
        send_sem=send_sem,
        recv_sem=recv_sem,
        device_id=device,
        device_id_type=MESH,
    )


class LineSum:
    SEMS = 6

    def __init__(self, place, part, inbox, peer, total, sems, view):
        self.place, self.part, self.inbox, self.peer, self.total = place, part, inbox, peer, total
        self.sems, self.view = sems, view

    def up(self, k):
        s, v = self.sems, self.view
        return send(v(self.part, k), v(self.inbox, k), s.at[0, k], s.at[1, k], self.place.pair)

    def across(self, k):
        s, v = self.sems, self.view
        return send(v(self.part, k), v(self.peer, k), s.at[2, k], s.at[3, k], self.place.middle)

    def down(self, k):
        s, v = self.sems, self.view
        return send(v(self.total, k), v(self.total, k), s.at[4, k], s.at[5, k], self.place.pair)

    def push(self, k):
        @pl.when(self.place.outer)
        def _():
            self.up(k).start()

    def meet_up(self, k):
        @pl.when(self.place.inner)
        def _():
            self.up(k).wait_recv()
            mine, other = self.view(self.part, k), self.view(self.inbox, k)
            mine[...] = (mine[...].astype(jnp.float32) + other[...].astype(jnp.float32)).astype(
                jnp.bfloat16
            )
            self.across(k).start()

    def meet_across(self, k):
        @pl.when(self.place.inner)
        def _():
            self.across(k).wait_recv()
            mine, other = self.view(self.part, k), self.view(self.peer, k)
            self.view(self.total, k)[...] = (
                mine[...].astype(jnp.float32) + other[...].astype(jnp.float32)
            ).astype(jnp.bfloat16)
            self.down(k).start()

    def get(self, k):
        @pl.when(self.place.outer)
        def _():
            self.down(k).wait_recv()

    def finish_part(self, count):
        @pl.when(self.place.outer)
        def _():
            for k in range(count):
                self.up(k).wait_send()

        @pl.when(self.place.inner)
        def _():
            for k in range(count):
                self.across(k).wait_send()

    def finish_total(self, count):
        @pl.when(self.place.inner)
        def _():
            for k in range(count):
                self.down(k).wait_send()


class Rows:
    def __init__(self, ref, base, group):
        self.ref, self.base, self.group = ref, base, group

    def slot(self, index):
        return self.ref.at[pl.ds(self.base + index * self.group, self.group)]


def lane_block(ref, k):
    return ref.at[:, pl.ds(k * 128, 128)]


def columns(ref, k, width):
    return ref.at[:, pl.ds(k * width, width)]


def row_live(lengths, rows):
    index = lax.broadcasted_iota(jnp.int32, (rows, 1), 0)
    return (index < lengths[0, 0] + lengths[0, 1]).astype(jnp.float32)


def exact(value):
    return value.astype(jnp.float32)


def low(value):
    return value.astype(jnp.bfloat16)


def rows_of(ref, k):
    return ref.at[pl.ds(k * 64, 64)]


def normalize(values):
    center = values - jnp.mean(values, axis=-1, keepdims=True)
    spread = jnp.mean(center * center, axis=-1, keepdims=True)
    scale = lax.rsqrt(spread + epsilon)
    return center * scale, scale


def norm_back(grad, gain, normed, scale):
    lifted = grad * gain
    return scale * (
        lifted
        - jnp.mean(lifted, axis=-1, keepdims=True)
        - normed * jnp.mean(lifted * normed, axis=-1, keepdims=True)
    )


def gelu_both(u):
    curve, factor = 0.044715, math.sqrt(2.0 / math.pi)
    square = u * u
    bent = jnp.tanh(factor * (u + curve * u * square))
    half = 0.5 * (1.0 + bent)
    slope = half + 0.5 * u * (1.0 - bent * bent) * (factor * (1.0 + 3.0 * curve * square))
    return u * half, slope


def layer_kernel(
    coords,
    lengths,
    counts,
    enc,
    slopes,
    dec,
    attn_own,
    up_own,
    down_own,
    gain_own,
    bias_own,
    cells,
    grad_in,
    cells_four,
    grad_four,
    grads,
    sums,
    counts_side,
    slopes_side,
    counts_far,
    slopes_far,
    weights,
    vectors,
    counts_v,
    enc_v,
    slopes_v,
    dec_v,
    work,
    places,
    qkv,
    soft,
    key_sum,
    value_sum,
    gains,
    offsets,
    part_m,
    part_o,
    part_s,
    inbox_m,
    inbox_o,
    peer_m,
    peer_o,
    peer_s,
    stream,
    total_m,
    total_o,
    total_s,
    branch_rows,
    outgoing,
    arriving,
    load_sems,
    line_sems,
    gather_sems,
    vector_sems,
    tile_sems,
    side_sems,
    far_sems,
    pair_sems,
    four_sems,
    ready_sem,
):
    place = Place()
    group, width = cells.shape
    dp, z = place.dp, place.z
    step = width // 4
    local = width // 4
    span = 128
    parts = group // span
    lane = lax.broadcasted_iota(jnp.int32, (1, span), 1)
    head_lanes = [low((lane // HEAD_DIM == h).astype(jnp.float32)) for h in range(2)]
    head_exact = [exact(h) for h in head_lanes]
    first_end, second_end = lengths[0, 0], lengths[0, 0] + lengths[0, 1]

    def slide_of(index):
        return (index >= first_end).astype(jnp.int32) + (index >= second_end).astype(jnp.int32)

    def rows(r):
        return slice(r * span, (r + 1) * span)

    def row_index(r):
        return lax.broadcasted_iota(jnp.int32, (span, 1), 0) + r * span

    def matrix(i, start, stop):
        return weights[i, start:stop].reshape((stop - start) * span, width)

    first, attn, cat = [Rows(enc_v, i * 2 * group, group) for i in range(3)]
    active, hidden, second = [Rows(dec_v, i * 2 * group, group) for i in range(3)]

    def key_masked(p):
        return counts_v.at[pl.ds(0, 2 * group), pl.ds(p * span, span)]

    def value_masked(p):
        return counts_v.at[pl.ds(0, 2 * group), pl.ds((2 + p) * span, span)]

    def staged(i, t):
        return counts_v.at[pl.ds((2 + t) * group, group), pl.ds(i * 2 * span, 2 * span)]

    def side_copy(ref, i):
        return send(
            ref.slot(0), ref.slot(1), side_sems.at[0, i], side_sems.at[1, i], place.sibling
        )

    side_active, side_hidden, side_second = [
        side_copy(ref, i) for i, ref in enumerate((active, hidden, second))
    ]
    side_cat, side_first, side_attn = [
        side_copy(ref, 4 + i) for i, ref in enumerate((cat, first, attn))
    ]
    side_branch = send(
        branch_rows.at[0], branch_rows.at[1], side_sems.at[0, 3], side_sems.at[1, 3], place.sibling
    )

    pair_far = [
        send(src, dst.at[0], pair_sems.at[0, i], pair_sems.at[1, i], device)
        for i, (src, dst, device) in enumerate(
            ((counts, counts_far, place.far[1]), (slopes, slopes_far, place.far[0]))
        )
    ]
    pair_side = [
        send(dst.at[0], dst.at[1], pair_sems.at[0, 2 + i], pair_sems.at[1, 2 + i], place.sibling)
        for i, dst in enumerate((counts_far, slopes_far))
    ]
    cells_to = (place.sibling, place.far[0], place.x_side)
    grad_to = (place.sibling, place.far[1], place.y_side)

    def other_core(d):
        return d + 1 - 2 * (d % 2)

    x_dp, y_dp, xy_dp = place.far_dps
    own_pair, x_pair, y_pair = (place.dp, y_dp), (x_dp, xy_dp), (place.dp, x_dp)
    cells_blocks = (own_pair, tuple(map(other_core, own_pair)), x_pair, tuple(map(other_core, x_pair)))
    x_row = (y_dp, xy_dp)
    grad_blocks = (y_pair, tuple(map(other_core, y_pair)), x_row, tuple(map(other_core, x_row)))

    def four_copy(i, four, devices, t, r):
        block = pl.ds(r * span, span)
        return send(
            staged(i, t).at[block],
            four.at[1 + t, block],
            four_sems.at[0, i, t, r],
            four_sems.at[1, i, t, r],
            devices[t],
        )

    def cells_copy(t, r):
        return four_copy(0, cells_four, cells_to, t, r)

    def grad_copy(t, r):
        return four_copy(1, grad_four, grad_to, t, r)

    def spread(ref, i, four, blocks, copy, r):
        for t, pair in enumerate(blocks):
            for n, d in enumerate(pair):
                block = ref[rows(r), pl.ds(pl.multiple_of(d * span, span), span)]
                at = slice(n * span, (n + 1) * span)
                if t == 0:
                    four[0, rows(r), at] = block
                else:
                    staged(i, t - 1)[rows(r), at] = block
            if t > 0:
                copy(t - 1, r).start()

    def line_sum(i, part, inbox, peer, total, view):
        return LineSum(place, part, inbox, peer, total, line_sems.at[i], view)

    sum_a = line_sum(0, part_m, inbox_m, peer_s, stream, lane_block)
    sum_b = line_sum(1, part_o, inbox_o, peer_o, branch_rows.at[0], lane_block)
    sum_m = line_sum(2, part_m, inbox_m, peer_m, total_m, rows_of)
    sum_o = line_sum(3, part_o, inbox_o, peer_o, total_o, rows_of)
    sum_s = line_sum(4, part_s, inbox_m, peer_s, total_s, rows_of)
    sum_f = line_sum(5, part_s, inbox_m, peer_m, total_s, rows_of)
    all_sums = dict(a=sum_a, b=sum_b, m=sum_m, o=sum_o, s=sum_s, f=sum_f)

    def loads_of(table, table_v, wide, wide_v, i):
        found = [pltpu.make_async_copy(table, table_v, load_sems.at[i, 0])]
        for j in range(4):
            found.append(
                pltpu.make_async_copy(
                    columns(wide, j, step), columns(wide_v, j, step), load_sems.at[i, 1 + j]
                )
            )
        return found

    loads = [
        loads_of(counts, counts_v, enc, enc_v, 0),
        loads_of(slopes, slopes_v, dec, dec_v, 1),
    ]
    for copy in loads[0] + loads[1]:
        copy.start()
    for i, ref in enumerate((attn_own, up_own, down_own)):
        weights[i, dp] = ref[...]
    tile = vectors.at[dp * 4 + z]
    tile[...] = jnp.zeros_like(tile)
    tile[0:1, 0:64] = exact(gain_own[...])
    tile[1:2, 0:64] = exact(bias_own[...])
    place.meet(place.far + (place.sibling, place.x_side, place.y_side) + place.line)

    line_out = [
        send(tile, tile, tile_sems.at[0, i], tile_sems.at[1, i], device)
        for i, device in enumerate(place.line)
    ]
    for copy in line_out:
        copy.start()

    def weight_far(i, q, d):
        block = weights.at[i, d]
        return send(
            block, block, gather_sems.at[0, i, q], gather_sems.at[1, i, q], place.far[q]
        )

    def weight_side(i, q):
        block = weights.at[i, ((dp,) + place.far_dps)[q]]
        return send(
            block, block, gather_sems.at[2, i, q], gather_sems.at[3, i, q], place.sibling
        )

    def tiles(d):
        return vectors.at[pl.ds(d * 4, 4)]

    vec_far = [
        send(tiles(dp), tiles(dp), vector_sems.at[0, q], vector_sems.at[1, q], device)
        for q, device in enumerate(place.far)
    ]
    vec_side = [
        send(tiles(d), tiles(d), vector_sems.at[2, q], vector_sems.at[3, q], place.sibling)
        for q, d in enumerate((dp,) + place.far_dps)
    ]
    def weights_out(some):
        for i in some:
            for q in range(3):
                weight_far(i, q, dp).start()
            weight_side(i, 0).start()

    weights_out((0,))
    own_side = [
        send(src, dst, pair_sems.at[0, 4 + i], pair_sems.at[1, 4 + i], place.sibling)
        for i, (src, dst) in enumerate(((counts_v, counts_side), (slopes_v, slopes_side)))
    ]

    own_rows = coords.shape[1]
    index = lax.broadcasted_iota(jnp.int32, (1, step), 1).astype(jnp.float32)
    freqs = jnp.exp(index * (-4.0 * math.log(10000.0) / width))
    for axis in range(2):
        along = jnp.broadcast_to(coords[axis : axis + 1, :], (own_rows, own_rows)).T
        angle = along[:, 0:1] * freqs
        places[2 * axis] = jnp.sin(angle)
        places[2 * axis + 1] = jnp.cos(angle)
    own = pl.ds(pl.multiple_of(z * own_rows, own_rows), own_rows)
    sums[...] = jnp.zeros_like(sums)
    key_sum[...] = jnp.zeros_like(key_sum)
    value_sum[...] = jnp.zeros_like(value_sum)

    def vectors_on(k):
        if k == 0:
            for copy in line_out:
                copy.wait_recv()
            for copy in vec_far + vec_side[:1]:
                copy.start()
            weights_out((1, 2))
            for copy in pair_far:
                copy.start()
        if k == 1:
            for q in range(3):
                vec_far[q].wait_recv()
                vec_side[1 + q].start()
        if k == 2:
            for copy in vec_side:
                copy.wait_recv()
            for n in range(2 * width // span):
                for ref, row in ((gains, 0), (offsets, 1)):
                    ref[0:1, n * span : (n + 1) * span] = jnp.concatenate(
                        [vectors[2 * n + i, row : row + 1, 0:64] for i in range(2)], axis=1
                    )

    def weights_on(some):
        for i in some:
            for q, d in enumerate(place.far_dps):
                weight_far(i, q, d).wait_recv()
                weight_side(i, 1 + q).start()
        for i in some:
            for q in range(4):
                weight_side(i, q).wait_recv()

    def encode(j):
        if j == 0:
            loads[0][0].wait()
            own_side[0].start()
        loads[0][1 + j].wait()
        work[...] = contract_rows(counts_v[...], enc_v[:, j * step : (j + 1) * step])
        work[own, :] += places[j]
        part_m[:, j * step : (j + 1) * step] = low(work[...])
        for k in range(2 * j, 2 * j + 2):
            sum_a.push(k)

    def decode(j):
        if j == 0:
            loads[1][0].wait()
            own_side[1].start()
        loads[1][1 + j].wait()
        live = (lax.broadcasted_iota(jnp.int32, (group, 1), 0) < second_end).astype(jnp.float32)
        part_o[:, j * step : (j + 1) * step] = low(
            contract_rows(slopes_v[...], dec_v[:, j * step : (j + 1) * step]) * live
        )

    def project(r):
        gain_a, offset_a = gains[0:1, :width], offsets[0:1, :width]
        if r == 0:
            for k in range(8):
                sum_a.get(k)
            own_side[0].wait_send()
            pl.semaphore_signal(
                ready_sem, inc=1, device_id=place.sibling, device_id_type=MESH
            )
        normed, _ = normalize(exact(stream[rows(r), :]))
        value = low(normed * gain_a + offset_a)
        first.slot(0)[rows(r), :] = value
        qkv[rows(r), :] = low(contract_cols(value, matrix(0, 0, 6)))
        for p in range(2):
            for ref, at in ((key_masked(p), local), (value_masked(p), 2 * local)):
                block = qkv[rows(r), at + p * span : at + (p + 1) * span]
                for h in range(2):
                    ref[h * group + r * span : h * group + (r + 1) * span, :] = (
                        block * head_lanes[h]
                    )

    def attend(r):
        if r == 0:
            pl.semaphore_wait(ready_sem, 1)
            side_first.start()
            sum_a.finish_part(8)
        same = slide_of(row_index(r)) == slide_of(
            lax.broadcasted_iota(jnp.int32, (1, group), 1)
        )
        for p in range(2):
            query = qkv[rows(r), p * span : (p + 1) * span]
            scores = contract_cols(query, key_masked(p)[...]) * (1.0 / math.sqrt(HEAD_DIM))
            for h in range(2):
                own = jnp.where(same, scores[:, h * group : (h + 1) * group], -1e30)
                raised = jnp.exp(own - jnp.max(own, axis=-1, keepdims=True))
                soft[p, rows(r), h * group : (h + 1) * group] = low(
                    raised / jnp.sum(raised, axis=-1, keepdims=True)
                )
            cat.slot(0)[rows(r), 3 * local + p * span : 3 * local + (p + 1) * span] = low(
                product(soft[p, rows(r), :], value_masked(p)[...])
            )
        part_m[rows(r), :] = low(product(cat.slot(0)[rows(r), 3 * local :], matrix(0, 6, 8)))
        push(sum_m, r)

    def middle(r):
        return exact(stream[rows(r), :]) + exact(total_m[rows(r), :])

    def feed(r):
        gain_b, offset_b = gains[0:1, width:], offsets[0:1, width:]
        if r == 0:
            for k in range(8):
                sum_b.get(k)
            sum_b.finish_part(8)
        get(sum_m, r)
        normed, _ = normalize(middle(r))
        value = low(normed * gain_b + offset_b)
        second.slot(0)[rows(r), :] = value
        act, slope = gelu_both(contract_cols(value, matrix(1, 0, 8)))
        active.slot(0)[rows(r), :] = low(act)
        grad = branch_rows[0, rows(r), :]
        back = low(contract_cols(grad, matrix(2, 0, 8)) * slope)
        hidden.slot(0)[rows(r), :] = back
        part_s[rows(r), :] = low(product(back, matrix(1, 0, 8)))
        push(sum_s, r)
        part_o[rows(r), :] = low(product(active.slot(0)[rows(r), :], matrix(2, 0, 8)))

    def attend_back(r):
        gain_b = gains[0:1, width:]
        get(sum_s, r)
        normed, scale = normalize(middle(r))
        grad = exact(total_s[rows(r), :])
        sums[1:2, :] += jnp.sum(grad * normed, axis=0, keepdims=True)
        sums[3:4, :] += jnp.sum(grad, axis=0, keepdims=True)
        mid = exact(branch_rows[0, rows(r), :]) + norm_back(grad, gain_b, normed, scale)
        attn.slot(0)[rows(r), :] = low(mid)
        back = low(contract_cols(low(mid), matrix(0, 6, 8)))
        for p in range(2):
            out = back[:, p * span : (p + 1) * span]
            slopes = contract_cols(out, value_masked(p)[...])
            marks = []
            for h in range(2):
                block = exact(soft[p, rows(r), h * group : (h + 1) * group])
                slope = slopes[:, h * group : (h + 1) * group]
                inner = jnp.sum(slope * block, axis=-1, keepdims=True)
                marks.append(low(block * (slope - inner)))
            scale_q = 1.0 / math.sqrt(HEAD_DIM)
            cat.slot(0)[rows(r), p * span : (p + 1) * span] = low(
                product(jnp.concatenate(marks, axis=1), key_masked(p)[...]) * scale_q
            )
            query = qkv[rows(r), p * span : (p + 1) * span]
            at = slice(p * span, (p + 1) * span)
            key_sum[:, at] += contract_rows(
                jnp.concatenate(marks, axis=0),
                jnp.concatenate([query * lanes for lanes in head_lanes], axis=0),
            )
            value_sum[:, at] += contract_rows(
                jnp.concatenate(
                    [soft[p, rows(r), h * group : (h + 1) * group] for h in range(2)], axis=0
                ),
                jnp.concatenate([out * lanes for lanes in head_lanes], axis=0),
            )

    def project_back(r):
        if r == 0:
            sum_s.finish_part(8)
            sum_s.finish_total(8)
            cat.slot(0)[:, local : 2 * local] = low(key_sum[...] * (1.0 / math.sqrt(HEAD_DIM)))
            cat.slot(0)[:, 2 * local : 3 * local] = low(value_sum[...])
        part_s[rows(r), :] = low(product(cat.slot(0)[rows(r), : 3 * local], matrix(0, 0, 6)))
        push(sum_f, r)

    def finish_in(r):
        gain_a = gains[0:1, :width]
        get(sum_f, r)
        normed, scale = normalize(exact(stream[rows(r), :]))
        grad = exact(total_s[rows(r), :])
        sums[0:1, :] += jnp.sum(grad * normed, axis=0, keepdims=True)
        sums[2:3, :] += jnp.sum(grad, axis=0, keepdims=True)
        grad_in[rows(r), :] = low(
            exact(attn.slot(0)[rows(r), :]) + norm_back(grad, gain_a, normed, scale)
        )
        spread(grad_in, 1, grad_four, grad_blocks, grad_copy, r)

    def finish_out(r):
        get(sum_o, r)
        live = (row_index(r) < second_end).astype(jnp.float32)
        cells[rows(r), :] = low((middle(r) + exact(total_o[rows(r), :])) * live)
        spread(cells, 0, cells_four, cells_blocks, cells_copy, r)

    def push(total, r):
        total.push(2 * r)
        total.push(2 * r + 1)

    def get(total, r):
        total.get(2 * r)
        total.get(2 * r + 1)

    chips = tuple(d // 2 for d in place.far_dps) + (place.chip,)

    def lanes_of(ref, slot, chip):
        start = pl.multiple_of((chip * 2 + place.core) * span, span)
        return ref.slot(slot)[:, pl.ds(start, span)]

    def far_copy(i, q):
        return send(
            outgoing.at[i, q],
            arriving.at[i, q],
            far_sems.at[0, i, q],
            far_sems.at[1, i, q],
            place.far[q],
        )

    def keep(i, q, value):
        if q == 3:
            grads[i] = value
        else:
            outgoing[i, q] = low(value)
            far_copy(i, q).start()

    def weight_grad(i, left, right, half):
        pair = chips[2 * half : 2 * half + 2]
        got = sum(
            contract_rows(
                jnp.concatenate([lanes_of(left, slot, chip) for chip in pair], axis=1),
                right(slot),
            )
            for slot in range(2)
        )
        for k in range(2):
            keep(i, 2 * half + k, got[k * span : (k + 1) * span])

    def attn_right(kind, slot):
        start = pl.multiple_of(kind * 2 * group + slot * group, group)
        return enc_v[pl.ds(start, group), :]

    def attn_grad(q):
        kind = chips[q] // 3
        keep(
            0,
            q,
            sum(
                contract_rows(lanes_of(cat, slot, chips[q]), attn_right(kind, slot))
                for slot in range(2)
            ),
        )

    def run(word):
        name, k = word[:-1], int(word[-1])
        if name[0] in "ux":
            total = all_sums[name[1]]
            (total.meet_up if name[0] == "u" else total.meet_across)(k)
        else:
            steps[name](k)

    def start_feed_sides(_):
        for copy in (side_hidden, side_second, side_active, side_branch):
            copy.start()

    def start_attn_sides(_):
        side_cat.start()
        side_attn.start()

    def pass_on(i):
        pair_far[i].wait_recv()
        pair_side[i].start()

    def up_grad(half):
        if half == 0:
            side_hidden.wait_recv()
            side_second.wait_recv()
        weight_grad(1, hidden, lambda slot: second.slot(slot)[...], half)

    def down_grad(half):
        if half == 0:
            side_active.wait_recv()
            side_branch.wait_recv()
        weight_grad(2, active, lambda slot: branch_rows[slot], half)

    def attn_grads(half):
        if half == 0:
            side_first.wait_recv()
            side_attn.wait_recv()
            side_cat.wait_recv()
        attn_grad(2 * half)
        attn_grad(2 * half + 1)

    def push_branch(j):
        sum_b.push(2 * j)
        sum_b.push(2 * j + 1)

    steps = dict(
        N=encode,
        M=decode,
        Q=push_branch,
        V=vectors_on,
        W=lambda _: weights_on((0,)),
        Y=lambda _: weights_on((1, 2)),
        A=project,
        B=attend,
        C=feed,
        D=attend_back,
        G=project_back,
        E=finish_in,
        F=finish_out,
        P=lambda r: push(sum_o, r),
        S=start_feed_sides,
        T=start_attn_sides,
        X=pass_on,
        H=up_grad,
        L=down_grad,
        K=attn_grads,
    )
    for word in SCHEDULE:
        run(word)
    for i in (2, 1, 0):
        for q in range(3):
            far_copy(i, q).wait_recv()
        grads[i] = grads[i] + sum(exact(arriving[i, q]) for q in range(3))
    for total in (sum_m, sum_o, sum_f):
        total.finish_part(8)
    for total in (sum_a, sum_b, sum_m, sum_o, sum_f):
        total.finish_total(8)
    for i in range(3):
        for q in range(3):
            weight_far(i, q, dp).wait_send()
        for q in range(4):
            weight_side(i, q).wait_send()
    for copy in line_out + vec_far + vec_side:
        copy.wait_send()
    own_side[0].wait_recv()
    own_side[1].wait()
    for i in range(3):
        for q in range(3):
            far_copy(i, q).wait_send()
    for t in range(3):
        for r in range(parts):
            cells_copy(t, r).wait()
            grad_copy(t, r).wait()
    for copy in pair_far:
        copy.wait_send()
    for copy in pair_side:
        copy.wait()
    for copy in (
        side_active,
        side_hidden,
        side_second,
        side_branch,
        side_cat,
        side_first,
        side_attn,
    ):
        copy.wait_send()


SCHEDULE = (
    "N0", "M0", "N1", "ua0", "ua1", "Q0", "M1", "xa0", "ua2", "ua3", "V0", "xa1", "N2", "ub0",
    "N3", "V1", "xa2", "ub1", "W0", "M2", "xa3", "V2", "ua4", "Q1", "xb0", "ua5", "M3", "xa4",
    "ua6", "Q2", "ua7", "xa5", "ub2", "xa6", "ub3", "xa7", "xb1", "Q3", "ub4", "xb2", "ub5",
    "xb3", "A0", "ub6", "A1", "xb4", "xb5", "A2", "ub7", "A3", "B0", "um0", "xb6", "B1", "um1",
    "xb7", "B2", "um2", "xm0", "xm1", "Y0", "um3", "B3", "xm2", "um4", "xm3", "um5", "C0", "xm4",
    "um6", "um7", "xm5", "C1", "us0", "xm6", "us1", "xm7", "C2", "us2", "xs0", "us3", "xs1", "C3",
    "xs2", "us4", "us5", "S0", "P0", "xs3", "P1", "D0", "us6", "xs4", "D1", "xs5", "us7", "D2",
    "uo0", "xs6", "xs7", "uo1", "P2", "H0", "xo0", "uo2", "D3", "xo1", "uo3", "G0", "uo4", "xo2",
    "G1", "T0", "F0", "uo5", "xo3", "L0", "uf0", "H1", "xo4", "uf1", "xo5", "uf2", "P3", "xf0",
    "L1", "G2", "uf3", "xf1", "uo6", "G3", "xf2", "F1", "K0", "uo7", "xf3", "F2", "xo6", "uf4",
    "uf5", "xo7", "E0", "xf4", "uf6", "K1", "E1", "xf5", "uf7", "xf6", "xf7", "X0", "X1", "E2",
    "F3", "E3",
)


def layer_call(coords, lengths, counts, enc, slopes, dec, attn, up, down, gain, bias):
    genes, group = counts.shape
    width = enc.shape[1]
    half, full = jnp.bfloat16, jnp.float32
    plain = pltpu.VMEM((group, width), half)
    table, wide = pltpu.VMEM((genes, group), half), pltpu.VMEM((genes, width), half)
    return pl.pallas_call(
        layer_kernel,
        out_shape=(
            jax.ShapeDtypeStruct((group, width), half),
            jax.ShapeDtypeStruct((group, width), half),
            jax.ShapeDtypeStruct((4, group, 256), half),
            jax.ShapeDtypeStruct((4, group, 256), half),
            jax.ShapeDtypeStruct((3, 128, width), full),
            jax.ShapeDtypeStruct((8, width), full),
            jax.ShapeDtypeStruct(counts.shape, half),
            jax.ShapeDtypeStruct(slopes.shape, half),
            jax.ShapeDtypeStruct((2,) + counts.shape, half),
            jax.ShapeDtypeStruct((2,) + slopes.shape, half),
        ),
        in_specs=[VMEM, SMEM, ANY, ANY, ANY, ANY] + [VMEM] * 5,
        out_specs=(VMEM,) * 6 + (ANY,) * 4,
        scratch_shapes=[
            pltpu.VMEM((3, 8) + attn.shape, half),
            pltpu.VMEM((32, 8, 128), full),
            table,
            wide,
            table,
            wide,
            pltpu.VMEM((group, width // 4), full),
            pltpu.VMEM((4, coords.shape[1], width // 4), full),
            pltpu.VMEM((group, 3 * width // 4), half),
            pltpu.VMEM((2, group, 2 * group), half),
            pltpu.VMEM((group, width // 4), full),
            pltpu.VMEM((group, width // 4), full),
            pltpu.VMEM((1, 2 * width), full),
            pltpu.VMEM((1, 2 * width), full),
        ]
        + [plain] * 12
        + [
            pltpu.VMEM((2, group, width), half),
            pltpu.VMEM((3, 3, 128, width), half),
            pltpu.VMEM((3, 3, 128, width), half),
            DMA((2, 5)),
            DMA((6, 6, 8)),
            DMA((4, 3, 4)),
            DMA((4, 4)),
            DMA((2, 3)),
            DMA((2, 7)),
            DMA((2, 3, 3)),
            DMA((2, 6)),
            DMA((2, 2, 3, 4)),
            pltpu.SemaphoreType.REGULAR,
        ],
        compiler_params=pltpu.CompilerParams(
            collective_id=1, has_side_effects=True, vmem_limit_bytes=60 * MIB
        ),
        name="layer",
    )(coords, lengths, counts, enc, slopes, dec, attn, up, down, gain, bias)


def genes_kernel(
    counts,
    counts_side,
    counts_far,
    slopes,
    slopes_side,
    slopes_far,
    enc,
    dec,
    cells,
    grad_in,
    cells_four,
    grad_four,
    sums,
    logits,
    gene_grad,
    enc_grad,
    dec_grad,
    small,
    counts_v,
    slopes_v,
    outgoing,
    arriving,
    sums_side,
    sums_chip,
    sums_far,
    load_sems,
    far_sems,
    sum_sems,
):
    place = Place()
    genes, group = counts.shape
    span = 128
    bounds = [min(i * GENE_STEP, genes) for i in range(-(-genes // GENE_STEP) + 1)]
    pieces = list(zip(bounds[:-1], bounds[1:]))

    def load(src, dst, i):
        return pltpu.make_async_copy(src, dst, load_sems.at[i])

    loads = [
        [
            load(src, ref.at[t], 4 * i + t)
            for t, src in enumerate((own, side, far.at[0], far.at[1]))
        ]
        for i, (ref, own, side, far) in enumerate(
            (
                (counts_v, counts, counts_side, counts_far),
                (slopes_v, slopes, slopes_side, slopes_far),
            )
        )
    ]
    tables = [
        [load(src.at[:, pl.ds(t * group, group)], ref.at[t], 8 + 2 * i + t) for t in range(2)]
        for i, (src, ref) in enumerate(((enc, counts_v), (dec, slopes_v)))
    ]
    for copy in loads[0] + loads[1]:
        copy.start()
    tail = outgoing.shape[1] - GENE_TAIL
    for i in range(2):
        outgoing[i, tail:, :] = jnp.zeros((GENE_TAIL, span), jnp.bfloat16)
    place.meet(place.far + (place.sibling,))

    side = send(sums, sums_side, sum_sems.at[0, 0], sum_sems.at[1, 0], place.sibling)
    side.start()
    far_sums = [
        send(sums_chip, sums_far.at[q], sum_sems.at[0, 1 + q], sum_sems.at[1, 1 + q], device)
        for q, device in enumerate(place.far)
    ]

    def far_copy(i, k):
        block = pl.ds(k * GENE_STEP, min(GENE_STEP, outgoing.shape[1] - k * GENE_STEP))
        return send(
            outgoing.at[i, block],
            arriving.at[i, block],
            far_sems.at[0, i, k],
            far_sems.at[1, i, k],
            place.far[i],
        )

    def reduce_part(i, k):
        left, right, result = (
            (counts_v, grad_four, enc_grad),
            (slopes_v, cells_four, dec_grad),
        )[i]
        if k == 0:
            for copy in loads[i]:
                copy.wait()
        start, stop = pieces[k]
        got = sum(product(left[t, start:stop, :], right[t]) for t in range(4))
        result[start:stop, :] = got[:, :span]
        outgoing[i, start:stop, :] = low(got[:, span:])
        far_copy(i, k).start()
        if k == len(pieces) - 1:
            for copy in tables[i]:
                copy.start()

    def reduce_end(i, result):
        for k, (start, stop) in enumerate(pieces):
            far_copy(i, k).wait_recv()
            result[start:stop, :] = result[start:stop, :] + exact(arriving[i, start:stop, :])

    def expand(i, ref, right, result):
        for copy in tables[i]:
            copy.wait()
        for start, stop in pieces:
            result[start:stop, :] = low(
                sum(
                    contract_cols(ref[t, start:stop, :], right[:, t * group : (t + 1) * group])
                    for t in range(2)
                )
            )

    order = [(0, 0), (0, 1)]
    for k in range(2, len(pieces)):
        order += [(1, k - 2), (0, k)]
    order += [(1, k) for k in range(max(len(pieces) - 2, 0), len(pieces))]
    for i, k in order:
        reduce_part(i, k)
    side.wait()
    sums_chip[...] = sums[...] + sums_side[...]
    for copy in far_sums:
        copy.start()
    expand(0, counts_v, grad_in, gene_grad)
    expand(1, slopes_v, cells, logits)
    for copy in far_sums:
        copy.wait_recv()
    small[...] = sums_chip[...] + (sums_far[0] + sums_far[1] + sums_far[2])
    reduce_end(0, enc_grad)
    reduce_end(1, dec_grad)
    for i in range(2):
        for k in range(len(pieces)):
            far_copy(i, k).wait_send()
    for copy in far_sums:
        copy.wait_send()


GENE_STEP = 848
GENE_TAIL = 16


def genes_call(tables, rows):
    genes, group = tables[0].shape
    sums = rows[-1]
    padded = -(-genes // 16) * 16
    steps = -(-genes // GENE_STEP)
    half, full = jnp.bfloat16, jnp.float32
    return pl.pallas_call(
        genes_kernel,
        out_shape=(
            jax.ShapeDtypeStruct((genes, group), half),
            jax.ShapeDtypeStruct((genes, group), half),
            jax.ShapeDtypeStruct((genes, 128), full),
            jax.ShapeDtypeStruct((genes, 128), full),
            jax.ShapeDtypeStruct(sums.shape, full),
        ),
        in_specs=[ANY] * len(tables) + [VMEM] * len(rows),
        out_specs=(VMEM,) * 5,
        scratch_shapes=[
            pltpu.VMEM((4, genes, group), half),
            pltpu.VMEM((4, genes, group), half),
            pltpu.VMEM((2, padded, 128), half),
            pltpu.VMEM((2, padded, 128), half),
            pltpu.VMEM(sums.shape, full),
            pltpu.VMEM(sums.shape, full),
            pltpu.VMEM((3,) + sums.shape, full),
            DMA((12,)),
            DMA((2, 2, steps)),
            DMA((2, 4)),
        ],
        compiler_params=pltpu.CompilerParams(
            collective_id=2, has_side_effects=True, vmem_limit_bytes=60 * MIB
        ),
        name="genes",
    )(*tables, *rows)


def fast_body(
    gene_counts,
    coords,
    lengths,
    enc_weight,
    dec_weight,
    attn_weight,
    up_weight,
    down_weight,
    ln_gain,
    ln_bias,
    logit_grad,
):
    model_width = enc_weight.shape[1]
    counts, slopes, dec = gene_counts.T, logit_grad.T, dec_weight.T
    (
        cells,
        grad_in,
        cells_four,
        grad_four,
        layer_grad,
        sums,
        counts_side,
        slopes_side,
        counts_far,
        slopes_far,
    ) = layer_call(
        coords,
        lengths,
        counts,
        enc_weight,
        slopes,
        dec,
        attn_weight,
        up_weight,
        down_weight,
        ln_gain[None],
        ln_bias[None],
    )
    logits, gene_grad, enc_grad, dec_grad, small = genes_call(
        (counts, counts_side, counts_far, slopes, slopes_side, slopes_far, enc_weight, dec),
        (cells, grad_in, cells_four, grad_four, sums),
    )
    small = small[:4].reshape(-1)
    place = lax.axis_index("dp") * 4 + lax.axis_index("gene")
    gain_grad = lax.dynamic_slice_in_dim(small[: 2 * model_width], place * 64, 64)
    bias_grad = lax.dynamic_slice_in_dim(
        small[2 * model_width : 3 * model_width], place * 32, 32
    )
    mid_bias_grad = lax.dynamic_slice_in_dim(small[3 * model_width :], place * 32, 32)
    return (
        logits.T,
        gene_grad.T,
        enc_grad,
        dec_grad.T,
        layer_grad[0],
        layer_grad[1],
        layer_grad[2],
        gain_grad,
        bias_grad,
        mid_bias_grad,
    )


def solution(mesh):
    fast = dict(mesh.shape) == {"dp": 8, "gene": 4}
    in_specs = (
        P("dp", "gene"),
        P(None, ("dp", "gene")),
        P("dp", None),
        P("gene", None),
        P(None, "gene"),
        P(("dp", "gene"), None),
        P(("dp", "gene"), None),
        P(("dp", "gene"), None),
        P(("dp", "gene")),
        P(("dp", "gene")),
        P("dp", "gene"),
    )
    out_specs = (
        P("dp", "gene"),
        P("dp", "gene"),
        P("gene", "dp"),
        P("dp", "gene"),
        P(("dp", "gene"), None),
        P(("dp", "gene"), None),
        P(("dp", "gene"), None),
        P(("dp", "gene")),
        P(("dp", "gene")),
        P(("dp", "gene")),
    )
    return jax.shard_map(
        fast_body if fast else body, mesh=mesh, in_specs=in_specs, out_specs=out_specs, check_vma=False)
```

```python
import functools
import math

import jax
import jax.numpy as jnp
from jax import lax
from jax.experimental import pallas as pl
from jax.experimental.pallas import tpu as pltpu
from jax.sharding import PartitionSpec as P

HEADS = 16
HEAD_DIM = 64


epsilon = 1e-05


def norm_rows(values, gain, offset):
    center = values - jnp.mean(values, axis=-1, keepdims=True)
    spread = jnp.mean(center * center, axis=-1, keepdims=True)
    return center * lax.rsqrt(spread + epsilon) * gain + offset


def gelu_tanh(values):
    return jax.nn.gelu(values, approximate=True)


def positions(coords, model_width):
    indices = jnp.arange(model_width // 4).astype(coords.dtype)
    freqs = jnp.exp(indices * (-4.0 * math.log(10000.0) / model_width))
    along_x = coords[0][:, None] * freqs[None, :]
    along_y = coords[1][:, None] * freqs[None, :]
    return jnp.concatenate(
        [jnp.sin(along_x), jnp.cos(along_x), jnp.sin(along_y), jnp.cos(along_y)], axis=1
    )


def slide_ids(slide_lengths, length_all):
    places = jnp.arange(length_all, dtype=jnp.int32)
    return (places >= slide_lengths[0]).astype(jnp.int32) + (
        places >= slide_lengths[0] + slide_lengths[1]
    ).astype(jnp.int32)


def product(left, right):
    return jnp.dot(left, right, preferred_element_type=jnp.float32)


def contract_rows(left, right):
    return lax.dot_general(
        left, right, (((0,), (0,)), ((), ())), preferred_element_type=jnp.float32
    )


def contract_cols(left, right):
    return lax.dot_general(
        left, right, (((1,), (1,)), ((), ())), preferred_element_type=jnp.float32
    )


def body(
    gene_counts,
    coords,
    lengths,
    enc_weight,
    dec_weight,
    attn_weight,
    up_weight,
    down_weight,
    ln_gain,
    ln_bias,
    logit_grad,
):
    model_width = enc_weight.shape[1]
    group_rows = gene_counts.shape[0]
    own_rows = coords.shape[1]
    gene_index = lax.axis_index("gene")
    score_scale = 1.0 / math.sqrt(HEAD_DIM)
    slide_all = slide_ids(lengths[0], group_rows)
    slide_own = lax.dynamic_slice_in_dim(slide_all, gene_index * own_rows, own_rows)
    live_rows = (slide_all < 2).astype(jnp.bfloat16)[:, None]
    attn_full, up_full, down_full, gain_full, bias_full = (
        lax.all_gather(attn_weight, ("dp", "gene"), axis=0, tiled=True),
        lax.all_gather(up_weight, ("dp", "gene"), axis=0, tiled=True),
        lax.all_gather(down_weight, ("dp", "gene"), axis=0, tiled=True),
        lax.all_gather(ln_gain, ("dp", "gene"), axis=0, tiled=True),
        lax.all_gather(ln_bias, ("dp", "gene"), axis=0, tiled=True),
    )
    norm_gains = gain_full.astype(jnp.float32)
    offsets = bias_full.astype(jnp.float32)
    proj_weight = attn_full[: 3 * model_width]
    out_weight = attn_full[3 * model_width :]
    embedded = lax.psum_scatter(
        product(gene_counts, enc_weight).astype(jnp.bfloat16),
        "gene",
        scatter_dimension=0,
        tiled=True,
    ).astype(jnp.float32)
    stream_in = embedded + positions(coords, model_width)
    first_normed, first_pull = jax.vjp(
        norm_rows, stream_in, norm_gains[:model_width], offsets[:model_width]
    )
    first_low = first_normed.astype(jnp.bfloat16)
    projected = contract_cols(first_low, proj_weight).astype(jnp.bfloat16)
    queries = projected[:, :model_width].reshape(own_rows, HEADS, HEAD_DIM)
    keyval_all = lax.all_gather(projected[:, model_width:], "gene", axis=0, tiled=True)
    keys_all = keyval_all[:, :model_width].reshape(group_rows, HEADS, HEAD_DIM)
    values_all = keyval_all[:, model_width:].reshape(group_rows, HEADS, HEAD_DIM)
    same_slide = (slide_own[:, None] == slide_all[None, :])[None]
    scores = (
        jnp.einsum("qhd,khd->hqk", queries, keys_all, preferred_element_type=jnp.float32)
        * score_scale
    )
    scores = jnp.where(same_slide, scores, -1e30)
    row_max = jnp.max(scores, axis=-1, keepdims=True)
    raised = jnp.exp(scores - row_max)
    soft = raised / jnp.sum(raised, axis=-1, keepdims=True)
    soft_low = soft.astype(jnp.bfloat16)
    attended = jnp.einsum("hqk,khd->qhd", soft_low, values_all, preferred_element_type=jnp.float32)
    attended = attended.reshape(own_rows, model_width).astype(jnp.bfloat16)
    stream_mid = stream_in + product(attended, out_weight)
    second_normed, second_pull = jax.vjp(
        norm_rows, stream_mid, norm_gains[model_width:], offsets[model_width:]
    )
    second_low = second_normed.astype(jnp.bfloat16)
    hidden_pre = contract_cols(second_low, up_full)
    active, gelu_pull = jax.vjp(gelu_tanh, hidden_pre)
    active_low = active.astype(jnp.bfloat16)
    stream_out = stream_mid + product(active_low, down_full)
    cells_low = stream_out.astype(jnp.bfloat16)
    cells_all = lax.all_gather(cells_low, "gene", axis=0, tiled=True)
    logits_full = product(cells_all, dec_weight)
    logits = (logits_full * live_rows.astype(jnp.float32)).astype(jnp.bfloat16)
    masked_grad = logit_grad * live_rows
    grad_out = lax.psum_scatter(
        contract_cols(masked_grad, dec_weight).astype(jnp.bfloat16),
        "gene",
        scatter_dimension=0,
        tiled=True,
    ).astype(jnp.float32)
    dec_part = contract_rows(cells_all, masked_grad)
    grad_branch = grad_out.astype(jnp.bfloat16)
    down_part = contract_rows(active_low, grad_branch)
    grad_active = contract_cols(grad_branch, down_full)
    grad_hidden = gelu_pull(grad_active)[0].astype(jnp.bfloat16)
    up_part = contract_rows(grad_hidden, second_low)
    grad_second = product(grad_hidden, up_full)
    grad_mid_norm, gain_second, bias_second = second_pull(grad_second)
    grad_mid = grad_out + grad_mid_norm
    grad_attn = grad_mid.astype(jnp.bfloat16)
    out_part = contract_rows(attended, grad_attn)
    grad_attended = (
        contract_cols(grad_attn, out_weight).astype(jnp.bfloat16).reshape(own_rows, HEADS, HEAD_DIM)
    )
    grad_soft = jnp.einsum(
        "qhd,khd->hqk", grad_attended, values_all, preferred_element_type=jnp.float32
    )
    grad_scores = soft * (grad_soft - jnp.sum(grad_soft * soft, axis=-1, keepdims=True))
    grad_scores = grad_scores.astype(jnp.bfloat16)
    grad_query = (
        jnp.einsum("hqk,khd->qhd", grad_scores, keys_all, preferred_element_type=jnp.float32)
        * score_scale
    )
    grad_query = grad_query.reshape(own_rows, model_width).astype(jnp.bfloat16)
    grad_keys = (
        jnp.einsum("hqk,qhd->khd", grad_scores, queries, preferred_element_type=jnp.float32)
        * score_scale
    )
    grad_values = jnp.einsum(
        "hqk,qhd->khd", soft_low, grad_attended, preferred_element_type=jnp.float32
    )
    keyval_part = jnp.concatenate(
        [grad_keys.reshape(group_rows, model_width), grad_values.reshape(group_rows, model_width)],
        axis=1,
    )
    grad_keyval = lax.psum_scatter(
        keyval_part.astype(jnp.bfloat16), "gene", scatter_dimension=0, tiled=True
    )
    grad_proj = jnp.concatenate([grad_query, grad_keyval], axis=1)
    proj_part = contract_rows(grad_proj, first_low)
    grad_first = product(grad_proj, proj_weight)
    grad_in_norm, gain_first, bias_first = first_pull(grad_first)
    grad_in = (grad_mid + grad_in_norm).astype(jnp.bfloat16)
    grad_in_all = lax.all_gather(grad_in, "gene", axis=0, tiled=True)
    gene_grad = contract_cols(grad_in_all, enc_weight).astype(jnp.bfloat16)
    enc_part = contract_rows(gene_counts, grad_in_all)
    enc_grad, dec_grad = (
        lax.psum_scatter(enc_part, "dp", scatter_dimension=1, tiled=True),
        lax.psum_scatter(dec_part, "dp", scatter_dimension=0, tiled=True),
    )
    attn_part = jnp.concatenate([proj_part, out_part], axis=0)
    gain_part = jnp.concatenate([gain_first, gain_second], axis=0)
    attn_grad, up_grad, down_grad, gain_grad, bias_grad, mid_bias_grad = (
        lax.psum_scatter(attn_part, ("dp", "gene"), scatter_dimension=0, tiled=True),
        lax.psum_scatter(up_part, ("dp", "gene"), scatter_dimension=0, tiled=True),
        lax.psum_scatter(down_part, ("dp", "gene"), scatter_dimension=0, tiled=True),
        lax.psum_scatter(gain_part, ("dp", "gene"), scatter_dimension=0, tiled=True),
        lax.psum_scatter(bias_first, ("dp", "gene"), scatter_dimension=0, tiled=True),
        lax.psum_scatter(bias_second, ("dp", "gene"), scatter_dimension=0, tiled=True),
    )
    return (
        logits,
        gene_grad,
        enc_grad,
        dec_grad,
        attn_grad,
        up_grad,
        down_grad,
        gain_grad,
        bias_grad,
        mid_bias_grad,
    )


MESH = pl.DeviceIdType.MESH
MIB = 2**20
VMEM = pl.BlockSpec(memory_space=pltpu.VMEM)
SMEM = pl.BlockSpec(memory_space=pltpu.SMEM)
ANY = pl.BlockSpec(memory_space=pl.ANY)
DMA = pltpu.SemaphoreType.DMA


class Place:
    def __init__(self):
        self.dp = dp = lax.axis_index("dp")
        self.z = z = lax.axis_index("gene")
        self.core = dp % 2
        self.chip = dp // 2
        self.inner = z * (3 - z) > 0
        self.outer = z * (3 - z) == 0
        self.pair = (dp, z + 1 - 2 * (z % 2))
        self.middle = (dp, 3 - z)
        self.sibling_dp = dp + 1 - 2 * (dp % 2)
        self.x_dp = dp + 2 - 4 * ((dp // 2) % 2)
        self.y_dp = dp + 4 - 8 * (dp // 4)
        self.xy_dp = self.x_dp + 4 - 8 * (dp // 4)
        self.sibling = (self.sibling_dp, z)
        self.far_dps = (self.x_dp, self.y_dp, self.xy_dp)
        self.far = tuple((d, z) for d in self.far_dps)
        self.x_side = (self.x_dp + self.sibling_dp - dp, z)
        self.y_side = (self.y_dp + self.sibling_dp - dp, z)
        self.xy_side = (self.xy_dp + self.sibling_dp - dp, z)
        self.plane = self.far + (self.sibling, self.x_side, self.y_side, self.xy_side)
        self.line = tuple((dp, (z + k) % 4) for k in (1, 2, 3))

    def meet(self, devices):
        barrier = pltpu.get_barrier_semaphore()
        for device in devices:
            pl.semaphore_signal(barrier, inc=1, device_id=device, device_id_type=MESH)
        pl.semaphore_wait(barrier, len(devices))

    def meet_line(self):
        barrier = pltpu.get_barrier_semaphore()
        pl.semaphore_signal(barrier, inc=1, device_id=self.pair, device_id_type=MESH)

        @pl.when(self.inner)
        def _():
            pl.semaphore_signal(barrier, inc=1, device_id=self.middle, device_id_type=MESH)
            pl.semaphore_wait(barrier, 2)

        @pl.when(self.outer)
        def _():
            pl.semaphore_wait(barrier, 1)


def send(src, dst, send_sem, recv_sem, device):
    return pltpu.make_async_remote_copy(
        src_ref=src,
        dst_ref=dst,
        send_sem=send_sem,
        recv_sem=recv_sem,
        device_id=device,
        device_id_type=MESH,
    )


class LineSum:
    SEMS = 6

    def __init__(self, place, part, inbox, peer, total, sems, view):
        self.place, self.part, self.inbox, self.peer, self.total = place, part, inbox, peer, total
        self.sems, self.view = sems, view

    def up(self, k):
        s, v = self.sems, self.view
        return send(v(self.part, k), v(self.inbox, k), s.at[0, k], s.at[1, k], self.place.pair)

    def across(self, k):
        s, v = self.sems, self.view
        return send(v(self.part, k), v(self.peer, k), s.at[2, k], s.at[3, k], self.place.middle)

    def down(self, k):
        s, v = self.sems, self.view
        return send(v(self.total, k), v(self.total, k), s.at[4, k], s.at[5, k], self.place.pair)

    def push(self, k):
        @pl.when(self.place.outer)
        def _():
            self.up(k).start()

    def meet_up(self, k):
        @pl.when(self.place.inner)
        def _():
            self.up(k).wait_recv()
            mine, other = self.view(self.part, k), self.view(self.inbox, k)
            mine[...] = (mine[...].astype(jnp.float32) + other[...].astype(jnp.float32)).astype(
                jnp.bfloat16
            )
            self.across(k).start()

    def meet_across(self, k):
        @pl.when(self.place.inner)
        def _():
            self.across(k).wait_recv()
            mine, other = self.view(self.part, k), self.view(self.peer, k)
            self.view(self.total, k)[...] = (
                mine[...].astype(jnp.float32) + other[...].astype(jnp.float32)
            ).astype(jnp.bfloat16)
            self.down(k).start()

    def get(self, k):
        @pl.when(self.place.outer)
        def _():
            self.down(k).wait_recv()

    def finish_part(self, count):
        @pl.when(self.place.outer)
        def _():
            for k in range(count):
                self.up(k).wait_send()

        @pl.when(self.place.inner)
        def _():
            for k in range(count):
                self.across(k).wait_send()

    def finish_total(self, count):
        @pl.when(self.place.inner)
        def _():
            for k in range(count):
                self.down(k).wait_send()


class Rows:
    def __init__(self, ref, base, group):
        self.ref, self.base, self.group = ref, base, group

    def slot(self, index):
        return self.ref.at[pl.ds(self.base + index * self.group, self.group)]


def lane_block(ref, k):
    return ref.at[:, pl.ds(k * 128, 128)]


def columns(ref, k, width):
    return ref.at[:, pl.ds(k * width, width)]


def row_live(lengths, rows):
    index = lax.broadcasted_iota(jnp.int32, (rows, 1), 0)
    return (index < lengths[0, 0] + lengths[0, 1]).astype(jnp.float32)


def exact(value):
    return value.astype(jnp.float32)


def low(value):
    return value.astype(jnp.bfloat16)


def rows_of(ref, k):
    return ref.at[pl.ds(k * 64, 64)]


def normalize(values):
    center = values - jnp.mean(values, axis=-1, keepdims=True)
    spread = jnp.mean(center * center, axis=-1, keepdims=True)
    scale = lax.rsqrt(spread + epsilon)
    return center * scale, scale


def norm_back(grad, gain, normed, scale):
    lifted = grad * gain
    return scale * (
        lifted
        - jnp.mean(lifted, axis=-1, keepdims=True)
        - normed * jnp.mean(lifted * normed, axis=-1, keepdims=True)
    )


def gelu_both(u):
    curve, factor = 0.044715, math.sqrt(2.0 / math.pi)
    square = u * u
    bent = jnp.tanh(factor * (u + curve * u * square))
    half = 0.5 * (1.0 + bent)
    slope = half + 0.5 * u * (1.0 - bent * bent) * (factor * (1.0 + 3.0 * curve * square))
    return u * half, slope


def layer_kernel(
    coords,
    lengths,
    counts,
    enc,
    slopes,
    dec,
    attn_own,
    up_own,
    down_own,
    gain_own,
    bias_own,
    cells,
    grad_in,
    cells_four,
    grad_four,
    grads,
    sums_all,
    counts_side,
    slopes_side,
    counts_far,
    slopes_far,
    weights,
    vectors,
    counts_v,
    enc_v,
    slopes_v,
    dec_v,
    work,
    places,
    qkv,
    soft,
    key_sum,
    value_sum,
    gains,
    offsets,
    part_m,
    part_o,
    part_s,
    inbox_m,
    inbox_o,
    peer_m,
    peer_o,
    peer_s,
    stream,
    total_m,
    total_o,
    total_s,
    branch_rows,
    outgoing,
    arriving,
    sums,
    sums_box,
    load_sems,
    line_sems,
    gather_sems,
    vector_sems,
    tile_sems,
    side_sems,
    far_sems,
    pair_sems,
    four_sems,
    sums_sems,
    ready_sem,
):
    place = Place()
    group, width = cells.shape
    dp, z = place.dp, place.z
    step = width // 4
    local = width // 4
    span = 128
    parts = group // span
    lane = lax.broadcasted_iota(jnp.int32, (1, span), 1)
    head_lanes = [low((lane // HEAD_DIM == h).astype(jnp.float32)) for h in range(2)]
    head_exact = [exact(h) for h in head_lanes]
    first_end, second_end = lengths[0, 0], lengths[0, 0] + lengths[0, 1]

    def slide_of(index):
        return (index >= first_end).astype(jnp.int32) + (index >= second_end).astype(jnp.int32)

    def rows(r):
        return slice(r * span, (r + 1) * span)

    def row_index(r):
        return lax.broadcasted_iota(jnp.int32, (span, 1), 0) + r * span

    def matrix(i, start, stop):
        return weights[i, start:stop].reshape((stop - start) * span, width)

    first, attn, cat = [Rows(enc_v, i * 2 * group, group) for i in range(3)]
    active, hidden, second = [Rows(dec_v, i * 2 * group, group) for i in range(3)]

    def key_masked(p):
        return counts_v.at[pl.ds(0, 2 * group), pl.ds(p * span, span)]

    def value_masked(p):
        return counts_v.at[pl.ds(0, 2 * group), pl.ds((2 + p) * span, span)]

    def staged(i, t):
        return counts_v.at[pl.ds((2 + t) * group, group), pl.ds(i * 2 * span, 2 * span)]

    def side_copy(ref, i):
        return send(
            ref.slot(0), ref.slot(1), side_sems.at[0, i], side_sems.at[1, i], place.sibling
        )

    side_active, side_hidden, side_second = [
        side_copy(ref, i) for i, ref in enumerate((active, hidden, second))
    ]
    side_cat, side_first, side_attn = [
        side_copy(ref, 4 + i) for i, ref in enumerate((cat, first, attn))
    ]
    side_branch = send(
        branch_rows.at[0], branch_rows.at[1], side_sems.at[0, 3], side_sems.at[1, 3], place.sibling
    )

    pair_far = [
        send(src, dst.at[0], pair_sems.at[0, i], pair_sems.at[1, i], device)
        for i, (src, dst, device) in enumerate(
            ((counts, counts_far, place.far[1]), (slopes, slopes_far, place.far[0]))
        )
    ]
    pair_side = [
        send(dst.at[0], dst.at[1], pair_sems.at[0, 2 + i], pair_sems.at[1, 2 + i], place.sibling)
        for i, dst in enumerate((counts_far, slopes_far))
    ]
    cells_to = (place.sibling, place.far[0], place.x_side)
    grad_to = (place.sibling, place.far[1], place.y_side)

    def other_core(d):
        return d + 1 - 2 * (d % 2)

    x_dp, y_dp, xy_dp = place.far_dps
    own_pair, x_pair, y_pair = (place.dp, y_dp), (x_dp, xy_dp), (place.dp, x_dp)
    cells_blocks = (own_pair, tuple(map(other_core, own_pair)), x_pair, tuple(map(other_core, x_pair)))
    x_row = (y_dp, xy_dp)
    grad_blocks = (y_pair, tuple(map(other_core, y_pair)), x_row, tuple(map(other_core, x_row)))

    def four_copy(i, four, devices, t, r):
        block = pl.ds(r * span, span)
        return send(
            staged(i, t).at[block],
            four.at[1 + t, block],
            four_sems.at[0, i, t, r],
            four_sems.at[1, i, t, r],
            devices[t],
        )

    def cells_copy(t, r):
        return four_copy(0, cells_four, cells_to, t, r)

    def grad_copy(t, r):
        return four_copy(1, grad_four, grad_to, t, r)

    def spread(ref, i, four, blocks, copy, r):
        for t, pair in enumerate(blocks):
            for n, d in enumerate(pair):
                block = ref[rows(r), pl.ds(pl.multiple_of(d * span, span), span)]
                at = slice(n * span, (n + 1) * span)
                if t == 0:
                    four[0, rows(r), at] = block
                else:
                    staged(i, t - 1)[rows(r), at] = block
            if t > 0:
                copy(t - 1, r).start()

    def line_sum(i, part, inbox, peer, total, view):
        return LineSum(place, part, inbox, peer, total, line_sems.at[i], view)

    sum_a = line_sum(0, part_m, inbox_m, peer_s, stream, lane_block)
    sum_b = line_sum(1, part_o, inbox_o, peer_o, branch_rows.at[0], lane_block)
    sum_m = line_sum(2, part_m, inbox_m, peer_m, total_m, rows_of)
    sum_o = line_sum(3, part_o, inbox_o, peer_o, total_o, rows_of)
    sum_s = line_sum(4, part_s, inbox_m, peer_s, total_s, rows_of)
    sum_f = line_sum(5, part_s, inbox_m, peer_m, total_s, rows_of)
    all_sums = dict(a=sum_a, b=sum_b, m=sum_m, o=sum_o, s=sum_s, f=sum_f)

    def loads_of(table, table_v, wide, wide_v, i):
        found = [pltpu.make_async_copy(table, table_v, load_sems.at[i, 0])]
        for j in range(4):
            found.append(
                pltpu.make_async_copy(
                    columns(wide, j, step), columns(wide_v, j, step), load_sems.at[i, 1 + j]
                )
            )
        return found

    loads = [
        loads_of(counts, counts_v, enc, enc_v, 0),
        loads_of(slopes, slopes_v, dec, dec_v, 1),
    ]
    for copy in loads[0] + loads[1]:
        copy.start()
    for i, ref in enumerate((attn_own, up_own, down_own)):
        weights[i, dp] = ref[...]
    tile = vectors.at[dp * 4 + z]
    tile[...] = jnp.zeros_like(tile)
    tile[0:1, 0:64] = exact(gain_own[...])
    tile[1:2, 0:64] = exact(bias_own[...])
    place.meet(place.plane + place.line)

    line_out = [
        send(tile, tile, tile_sems.at[0, i], tile_sems.at[1, i], device)
        for i, device in enumerate(place.line)
    ]
    for copy in line_out:
        copy.start()

    def weight_far(i, q, d):
        block = weights.at[i, d]
        return send(
            block, block, gather_sems.at[0, i, q], gather_sems.at[1, i, q], place.far[q]
        )

    def weight_side(i, q):
        block = weights.at[i, ((dp,) + place.far_dps)[q]]
        return send(
            block, block, gather_sems.at[2, i, q], gather_sems.at[3, i, q], place.sibling
        )

    def tiles(d):
        return vectors.at[pl.ds(d * 4, 4)]

    vec_far = [
        send(tiles(dp), tiles(dp), vector_sems.at[0, q], vector_sems.at[1, q], device)
        for q, device in enumerate(place.far)
    ]
    vec_side = [
        send(tiles(d), tiles(d), vector_sems.at[2, q], vector_sems.at[3, q], place.sibling)
        for q, d in enumerate((dp,) + place.far_dps)
    ]
    def weights_out(some):
        for i in some:
            for q in range(3):
                weight_far(i, q, dp).start()
            weight_side(i, 0).start()

    weights_out((0,))
    own_side = [
        send(src, dst, pair_sems.at[0, 4 + i], pair_sems.at[1, 4 + i], place.sibling)
        for i, (src, dst) in enumerate(((counts_v, counts_side), (slopes_v, slopes_side)))
    ]

    own_rows = coords.shape[1]
    index = lax.broadcasted_iota(jnp.int32, (1, step), 1).astype(jnp.float32)
    freqs = jnp.exp(index * (-4.0 * math.log(10000.0) / width))
    for axis in range(2):
        along = jnp.broadcast_to(coords[axis : axis + 1, :], (own_rows, own_rows)).T
        angle = along[:, 0:1] * freqs
        places[2 * axis] = jnp.sin(angle)
        places[2 * axis + 1] = jnp.cos(angle)
    own = pl.ds(pl.multiple_of(z * own_rows, own_rows), own_rows)
    sums[...] = jnp.zeros_like(sums)
    key_sum[...] = jnp.zeros_like(key_sum)
    value_sum[...] = jnp.zeros_like(value_sum)

    def vectors_on(k):
        if k == 0:
            for copy in line_out:
                copy.wait_recv()
            for copy in vec_far + vec_side[:1]:
                copy.start()
            weights_out((1, 2))
            for copy in pair_far:
                copy.start()
        if k == 1:
            for q in range(3):
                vec_far[q].wait_recv()
                vec_side[1 + q].start()
        if k == 2:
            for copy in vec_side:
                copy.wait_recv()
            for n in range(2 * width // span):
                for ref, row in ((gains, 0), (offsets, 1)):
                    ref[0:1, n * span : (n + 1) * span] = jnp.concatenate(
                        [vectors[2 * n + i, row : row + 1, 0:64] for i in range(2)], axis=1
                    )

    def weights_on(some):
        for i in some:
            for q, d in enumerate(place.far_dps):
                weight_far(i, q, d).wait_recv()
                weight_side(i, 1 + q).start()
        for i in some:
            for q in range(4):
                weight_side(i, q).wait_recv()

    def encode(j):
        if j == 0:
            loads[0][0].wait()
            own_side[0].start()
        loads[0][1 + j].wait()
        work[...] = contract_rows(counts_v[...], enc_v[:, j * step : (j + 1) * step])
        work[own, :] += places[j]
        part_m[:, j * step : (j + 1) * step] = low(work[...])
        for k in range(2 * j, 2 * j + 2):
            sum_a.push(k)

    def decode(j):
        if j == 0:
            loads[1][0].wait()
            own_side[1].start()
        loads[1][1 + j].wait()
        live = (lax.broadcasted_iota(jnp.int32, (group, 1), 0) < second_end).astype(jnp.float32)
        part_o[:, j * step : (j + 1) * step] = low(
            contract_rows(slopes_v[...], dec_v[:, j * step : (j + 1) * step]) * live
        )

    def project(r):
        gain_a, offset_a = gains[0:1, :width], offsets[0:1, :width]
        if r == 0:
            for k in range(8):
                sum_a.get(k)
            own_side[0].wait_send()
            pl.semaphore_signal(
                ready_sem, inc=1, device_id=place.sibling, device_id_type=MESH
            )
        normed, _ = normalize(exact(stream[rows(r), :]))
        value = low(normed * gain_a + offset_a)
        first.slot(0)[rows(r), :] = value
        qkv[rows(r), :] = low(contract_cols(value, matrix(0, 0, 6)))
        for p in range(2):
            for ref, at in ((key_masked(p), local), (value_masked(p), 2 * local)):
                block = qkv[rows(r), at + p * span : at + (p + 1) * span]
                for h in range(2):
                    ref[h * group + r * span : h * group + (r + 1) * span, :] = (
                        block * head_lanes[h]
                    )

    def attend(r):
        if r == 0:
            pl.semaphore_wait(ready_sem, 1)
            side_first.start()
            sum_a.finish_part(8)
        same = slide_of(row_index(r)) == slide_of(
            lax.broadcasted_iota(jnp.int32, (1, group), 1)
        )
        for p in range(2):
            query = qkv[rows(r), p * span : (p + 1) * span]
            scores = contract_cols(query, key_masked(p)[...]) * (1.0 / math.sqrt(HEAD_DIM))
            for h in range(2):
                own = jnp.where(same, scores[:, h * group : (h + 1) * group], -1e30)
                raised = jnp.exp(own - jnp.max(own, axis=-1, keepdims=True))
                soft[p, rows(r), h * group : (h + 1) * group] = low(
                    raised / jnp.sum(raised, axis=-1, keepdims=True)
                )
            cat.slot(0)[rows(r), 3 * local + p * span : 3 * local + (p + 1) * span] = low(
                product(soft[p, rows(r), :], value_masked(p)[...])
            )
        part_m[rows(r), :] = low(product(cat.slot(0)[rows(r), 3 * local :], matrix(0, 6, 8)))
        push(sum_m, r)

    def middle(r):
        return exact(stream[rows(r), :]) + exact(total_m[rows(r), :])

    def feed(r):
        gain_b, offset_b = gains[0:1, width:], offsets[0:1, width:]
        if r == 0:
            for k in range(8):
                sum_b.get(k)
            sum_b.finish_part(8)
        get(sum_m, r)
        normed, _ = normalize(middle(r))
        value = low(normed * gain_b + offset_b)
        second.slot(0)[rows(r), :] = value
        act, slope = gelu_both(contract_cols(value, matrix(1, 0, 8)))
        active.slot(0)[rows(r), :] = low(act)
        grad = branch_rows[0, rows(r), :]
        back = low(contract_cols(grad, matrix(2, 0, 8)) * slope)
        hidden.slot(0)[rows(r), :] = back
        part_s[rows(r), :] = low(product(back, matrix(1, 0, 8)))
        push(sum_s, r)
        part_o[rows(r), :] = low(product(active.slot(0)[rows(r), :], matrix(2, 0, 8)))

    def attend_back(r):
        gain_b = gains[0:1, width:]
        get(sum_s, r)
        normed, scale = normalize(middle(r))
        grad = exact(total_s[rows(r), :])
        sums[1:2, :] += jnp.sum(grad * normed, axis=0, keepdims=True)
        sums[3:4, :] += jnp.sum(grad, axis=0, keepdims=True)
        mid = exact(branch_rows[0, rows(r), :]) + norm_back(grad, gain_b, normed, scale)
        attn.slot(0)[rows(r), :] = low(mid)
        back = low(contract_cols(low(mid), matrix(0, 6, 8)))
        for p in range(2):
            out = back[:, p * span : (p + 1) * span]
            slopes = contract_cols(out, value_masked(p)[...])
            marks = []
            for h in range(2):
                block = exact(soft[p, rows(r), h * group : (h + 1) * group])
                slope = slopes[:, h * group : (h + 1) * group]
                inner = jnp.sum(slope * block, axis=-1, keepdims=True)
                marks.append(low(block * (slope - inner)))
            scale_q = 1.0 / math.sqrt(HEAD_DIM)
            cat.slot(0)[rows(r), p * span : (p + 1) * span] = low(
                product(jnp.concatenate(marks, axis=1), key_masked(p)[...]) * scale_q
            )
            query = qkv[rows(r), p * span : (p + 1) * span]
            at = slice(p * span, (p + 1) * span)
            key_sum[:, at] += contract_rows(
                jnp.concatenate(marks, axis=0),
                jnp.concatenate([query * lanes for lanes in head_lanes], axis=0),
            )
            value_sum[:, at] += contract_rows(
                jnp.concatenate(
                    [soft[p, rows(r), h * group : (h + 1) * group] for h in range(2)], axis=0
                ),
                jnp.concatenate([out * lanes for lanes in head_lanes], axis=0),
            )

    def project_back(r):
        if r == 0:
            sum_s.finish_part(8)
            sum_s.finish_total(8)
            cat.slot(0)[:, local : 2 * local] = low(key_sum[...] * (1.0 / math.sqrt(HEAD_DIM)))
            cat.slot(0)[:, 2 * local : 3 * local] = low(value_sum[...])
        part_s[rows(r), :] = low(product(cat.slot(0)[rows(r), : 3 * local], matrix(0, 0, 6)))
        push(sum_f, r)

    def finish_in(r):
        gain_a = gains[0:1, :width]
        get(sum_f, r)
        normed, scale = normalize(exact(stream[rows(r), :]))
        grad = exact(total_s[rows(r), :])
        sums[0:1, :] += jnp.sum(grad * normed, axis=0, keepdims=True)
        sums[2:3, :] += jnp.sum(grad, axis=0, keepdims=True)
        grad_in[rows(r), :] = low(
            exact(attn.slot(0)[rows(r), :]) + norm_back(grad, gain_a, normed, scale)
        )
        spread(grad_in, 1, grad_four, grad_blocks, grad_copy, r)

    def finish_out(r):
        get(sum_o, r)
        live = (row_index(r) < second_end).astype(jnp.float32)
        cells[rows(r), :] = low((middle(r) + exact(total_o[rows(r), :])) * live)
        spread(cells, 0, cells_four, cells_blocks, cells_copy, r)

    def push(total, r):
        total.push(2 * r)
        total.push(2 * r + 1)

    def get(total, r):
        total.get(2 * r)
        total.get(2 * r + 1)

    chips = tuple(d // 2 for d in place.far_dps) + (place.chip,)

    def lanes_of(ref, slot, chip):
        start = pl.multiple_of((chip * 2 + place.core) * span, span)
        return ref.slot(slot)[:, pl.ds(start, span)]

    def far_copy(i, q):
        return send(
            outgoing.at[i, q],
            arriving.at[i, q],
            far_sems.at[0, i, q],
            far_sems.at[1, i, q],
            place.far[q],
        )

    def keep(i, q, value):
        if q == 3:
            grads[i] = value
        else:
            outgoing[i, q] = low(value)
            far_copy(i, q).start()

    def weight_grad(i, left, right, half):
        pair = chips[2 * half : 2 * half + 2]
        got = sum(
            contract_rows(
                jnp.concatenate([lanes_of(left, slot, chip) for chip in pair], axis=1),
                right(slot),
            )
            for slot in range(2)
        )
        for k in range(2):
            keep(i, 2 * half + k, got[k * span : (k + 1) * span])

    def attn_right(kind, slot):
        start = pl.multiple_of(kind * 2 * group + slot * group, group)
        return enc_v[pl.ds(start, group), :]

    def attn_grad(q):
        kind = chips[q] // 3
        keep(
            0,
            q,
            sum(
                contract_rows(lanes_of(cat, slot, chips[q]), attn_right(kind, slot))
                for slot in range(2)
            ),
        )

    def run(word):
        name, k = word[:-1], int(word[-1])
        if name[0] in "ux":
            total = all_sums[name[1]]
            (total.meet_up if name[0] == "u" else total.meet_across)(k)
        else:
            steps[name](k)

    def start_feed_sides(_):
        for copy in (side_hidden, side_second, side_active, side_branch):
            copy.start()

    def start_attn_sides(_):
        side_cat.start()
        side_attn.start()

    def pass_on(i):
        pair_far[i].wait_recv()
        pair_side[i].start()

    def up_grad(half):
        if half == 0:
            side_hidden.wait_recv()
            side_second.wait_recv()
        weight_grad(1, hidden, lambda slot: second.slot(slot)[...], half)

    def down_grad(half):
        if half == 0:
            side_active.wait_recv()
            side_branch.wait_recv()
        weight_grad(2, active, lambda slot: branch_rows[slot], half)

    def attn_grads(half):
        if half == 0:
            side_first.wait_recv()
            side_attn.wait_recv()
            side_cat.wait_recv()
        attn_grad(2 * half)
        attn_grad(2 * half + 1)

    def push_branch(j):
        sum_b.push(2 * j)
        sum_b.push(2 * j + 1)

    steps = dict(
        N=encode,
        M=decode,
        Q=push_branch,
        V=vectors_on,
        W=lambda _: weights_on((0,)),
        Y=lambda _: weights_on((1, 2)),
        A=project,
        B=attend,
        C=feed,
        D=attend_back,
        G=project_back,
        E=finish_in,
        F=finish_out,
        P=lambda r: push(sum_o, r),
        S=start_feed_sides,
        T=start_attn_sides,
        X=pass_on,
        H=up_grad,
        L=down_grad,
        K=attn_grads,
    )
    for word in SCHEDULE:
        run(word)
    sums_out = [
        send(sums, sums_box.at[i], sums_sems.at[0, i], sums_sems.at[1, i], device)
        for i, device in enumerate(place.plane)
    ]
    for copy in sums_out:
        copy.start()
    for i in (2, 1, 0):
        for q in range(3):
            far_copy(i, q).wait_recv()
        grads[i] = grads[i] + sum(exact(arriving[i, q]) for q in range(3))
    for copy in sums_out:
        copy.wait()
    sums_all[...] = sums[...] + sum(sums_box[i] for i in range(len(sums_out)))
    for total in (sum_m, sum_o, sum_f):
        total.finish_part(8)
    for total in (sum_a, sum_b, sum_m, sum_o, sum_f):
        total.finish_total(8)
    for i in range(3):
        for q in range(3):
            weight_far(i, q, dp).wait_send()
        for q in range(4):
            weight_side(i, q).wait_send()
    for copy in line_out + vec_far + vec_side:
        copy.wait_send()
    own_side[0].wait_recv()
    own_side[1].wait()
    for i in range(3):
        for q in range(3):
            far_copy(i, q).wait_send()
    for t in range(3):
        for r in range(parts):
            cells_copy(t, r).wait()
            grad_copy(t, r).wait()
    for copy in pair_far:
        copy.wait_send()
    for copy in pair_side:
        copy.wait()
    for copy in (
        side_active,
        side_hidden,
        side_second,
        side_branch,
        side_cat,
        side_first,
        side_attn,
    ):
        copy.wait_send()


SCHEDULE = (
    "N0", "M0", "N1", "ua0", "ua1", "Q0", "M1", "xa0", "ua2", "ua3", "V0", "xa1", "N2", "ub0",
    "N3", "V1", "xa2", "ub1", "W0", "M2", "xa3", "V2", "ua4", "Q1", "xb0", "ua5", "M3", "xa4",
    "ua6", "Q2", "ua7", "xa5", "ub2", "xa6", "ub3", "xa7", "xb1", "Q3", "ub4", "xb2", "ub5",
    "xb3", "A0", "ub6", "A1", "xb4", "xb5", "A2", "ub7", "A3", "B0", "um0", "xb6", "B1", "um1",
    "xb7", "B2", "um2", "xm0", "xm1", "Y0", "um3", "B3", "xm2", "um4", "xm3", "um5", "C0", "xm4",
    "um6", "um7", "xm5", "C1", "us0", "xm6", "us1", "xm7", "C2", "us2", "xs0", "us3", "xs1", "C3",
    "xs2", "us4", "us5", "S0", "P0", "xs3", "P1", "D0", "us6", "xs4", "D1", "xs5", "us7", "D2",
    "uo0", "xs6", "xs7", "uo1", "P2", "H0", "xo0", "uo2", "D3", "xo1", "uo3", "G0", "uo4", "xo2",
    "G1", "T0", "F0", "uo5", "xo3", "L0", "uf0", "H1", "xo4", "uf1", "xo5", "uf2", "P3", "xf0",
    "L1", "G2", "uf3", "xf1", "uo6", "G3", "xf2", "F1", "K0", "uo7", "xf3", "F2", "xo6", "uf4",
    "uf5", "xo7", "E0", "xf4", "uf6", "K1", "E1", "xf5", "uf7", "xf6", "xf7", "X0", "X1", "E2",
    "F3", "E3",
)


def layer_call(coords, lengths, counts, enc, slopes, dec, attn, up, down, gain, bias):
    genes, group = counts.shape
    width = enc.shape[1]
    half, full = jnp.bfloat16, jnp.float32
    plain = pltpu.VMEM((group, width), half)
    table, wide = pltpu.VMEM((genes, group), half), pltpu.VMEM((genes, width), half)
    return pl.pallas_call(
        layer_kernel,
        out_shape=(
            jax.ShapeDtypeStruct((group, width), half),
            jax.ShapeDtypeStruct((group, width), half),
            jax.ShapeDtypeStruct((4, group, 256), half),
            jax.ShapeDtypeStruct((4, group, 256), half),
            jax.ShapeDtypeStruct((3, 128, width), full),
            jax.ShapeDtypeStruct((8, width), full),
            jax.ShapeDtypeStruct(counts.shape, half),
            jax.ShapeDtypeStruct(slopes.shape, half),
            jax.ShapeDtypeStruct((2,) + counts.shape, half),
            jax.ShapeDtypeStruct((2,) + slopes.shape, half),
        ),
        in_specs=[VMEM, SMEM, ANY, ANY, ANY, ANY] + [VMEM] * 5,
        out_specs=(VMEM,) * 6 + (ANY,) * 4,
        scratch_shapes=[
            pltpu.VMEM((3, 8) + attn.shape, half),
            pltpu.VMEM((32, 8, 128), full),
            table,
            wide,
            table,
            wide,
            pltpu.VMEM((group, width // 4), full),
            pltpu.VMEM((4, coords.shape[1], width // 4), full),
            pltpu.VMEM((group, 3 * width // 4), half),
            pltpu.VMEM((2, group, 2 * group), half),
            pltpu.VMEM((group, width // 4), full),
            pltpu.VMEM((group, width // 4), full),
            pltpu.VMEM((1, 2 * width), full),
            pltpu.VMEM((1, 2 * width), full),
        ]
        + [plain] * 12
        + [
            pltpu.VMEM((2, group, width), half),
            pltpu.VMEM((3, 3, 128, width), half),
            pltpu.VMEM((3, 3, 128, width), half),
            pltpu.VMEM((8, width), full),
            pltpu.VMEM((7, 8, width), full),
            DMA((2, 5)),
            DMA((6, 6, 8)),
            DMA((4, 3, 4)),
            DMA((4, 4)),
            DMA((2, 3)),
            DMA((2, 7)),
            DMA((2, 3, 3)),
            DMA((2, 6)),
            DMA((2, 2, 3, 4)),
            DMA((2, 7)),
            pltpu.SemaphoreType.REGULAR,
        ],
        compiler_params=pltpu.CompilerParams(
            collective_id=1, has_side_effects=True, vmem_limit_bytes=60 * MIB
        ),
        name="layer",
    )(coords, lengths, counts, enc, slopes, dec, attn, up, down, gain, bias)


GENE_STEP = 848


def parts_kernel(
    counts,
    counts_side,
    counts_far,
    slopes,
    slopes_side,
    slopes_far,
    grad_four,
    cells_four,
    enc_own,
    enc_out,
    dec_own,
    dec_out,
):
    for own, side, far, right, kept, sent in (
        (counts, counts_side, counts_far, grad_four, enc_own, enc_out),
        (slopes, slopes_side, slopes_far, cells_four, dec_own, dec_out),
    ):
        lefts = (own[...], side[...], far[0], far[1])
        got = sum(product(left, right[t]) for t, left in enumerate(lefts))
        kept[...] = got[:, :128]
        sent[...] = low(got[:, 128:])


def parts_call(tables, fours, first, last):
    genes, group = tables[0].shape
    rows = min(last * GENE_STEP, genes) - first * GENE_STEP
    full = jax.ShapeDtypeStruct((rows, 128), jnp.float32)
    half = jax.ShapeDtypeStruct((rows, 128), jnp.bfloat16)
    flat = pl.BlockSpec((GENE_STEP, group), lambda i: (i + first, 0))
    pair = pl.BlockSpec((2, GENE_STEP, group), lambda i: (0, i + first, 0))
    four = pl.BlockSpec(fours[0].shape, lambda i: (0, 0, 0))
    return pl.pallas_call(
        parts_kernel,
        out_shape=(full, half, full, half),
        grid=(last - first,),
        in_specs=[flat, flat, pair, flat, flat, pair, four, four],
        out_specs=(pl.BlockSpec((GENE_STEP, 128), lambda i: (i, 0)),) * 4,
        cost_estimate=pl.CostEstimate(
            flops=16 * rows * group * 256,
            bytes_accessed=16 * rows * group + 12 * rows * 128,
            transcendentals=0,
        ),
        compiler_params=pltpu.CompilerParams(vmem_limit_bytes=60 * MIB),
        name="parts",
    )(*tables, *fours)


def join_kernel(*refs):
    block = pl.program_id(0)
    for n in range(2):
        kept_a, came_a, kept_b, came_b = refs[4 * n : 4 * n + 4]
        result = refs[8 + n]

        @pl.when(block < 2)
        def _():
            result[...] = kept_a[...] + exact(came_a[...])

        @pl.when(block >= 2)
        def _():
            result[...] = kept_b[...] + exact(came_b[...])


def join_call(genes, parts):
    early = pl.BlockSpec((GENE_STEP, 128), lambda i: (jnp.minimum(i, 1), 0))
    late = pl.BlockSpec((GENE_STEP, 128), lambda i: (jnp.maximum(i - 2, 0), 0))
    return pl.pallas_call(
        join_kernel,
        out_shape=(jax.ShapeDtypeStruct((genes, 128), jnp.float32),) * 2,
        grid=(-(-genes // GENE_STEP),),
        in_specs=[early, early, late, late] * 2,
        out_specs=(pl.BlockSpec((GENE_STEP, 128), lambda i: (i, 0)),) * 2,
        compiler_params=pltpu.CompilerParams(vmem_limit_bytes=60 * MIB),
        name="join",
    )(*parts)


def expand_kernel(enc, dec, cells, grad_in, logits, gene_grad):
    logits[...] = low(contract_cols(dec[...], cells[...]))
    gene_grad[...] = low(contract_cols(enc[...], grad_in[...]))


def expand_call(enc, dec, cells, grad_in):
    genes, width = enc.shape
    group = cells.shape[0]
    steps = -(-genes // GENE_STEP)
    half = jax.ShapeDtypeStruct((genes, group), jnp.bfloat16)
    table = pl.BlockSpec((GENE_STEP, width), lambda i: (i, 0))
    whole = pl.BlockSpec((group, width), lambda i: (0, 0))
    return pl.pallas_call(
        expand_kernel,
        out_shape=(half, half),
        grid=(steps,),
        in_specs=[table, table, whole, whole],
        out_specs=(pl.BlockSpec((GENE_STEP, group), lambda i: (i, 0)),) * 2,
        cost_estimate=pl.CostEstimate(
            flops=4 * genes * group * width,
            bytes_accessed=4 * genes * (width + group),
            transcendentals=0,
        ),
        compiler_params=pltpu.CompilerParams(vmem_limit_bytes=60 * MIB),
        name="expand",
    )(enc, dec, cells, grad_in)


def swap(values, bit):
    return lax.ppermute(values, "dp", [(d, d ^ bit) for d in range(8)])


def fast_body(
    gene_counts,
    coords,
    lengths,
    enc_weight,
    dec_weight,
    attn_weight,
    up_weight,
    down_weight,
    ln_gain,
    ln_bias,
    logit_grad,
):
    model_width = enc_weight.shape[1]
    counts, slopes, dec = gene_counts.T, logit_grad.T, dec_weight.T
    (
        cells,
        grad_in,
        cells_four,
        grad_four,
        layer_grad,
        sums,
        counts_side,
        slopes_side,
        counts_far,
        slopes_far,
    ) = layer_call(
        coords,
        lengths,
        counts,
        enc_weight,
        slopes,
        dec,
        attn_weight,
        up_weight,
        down_weight,
        ln_gain[None],
        ln_bias[None],
    )
    tables = (counts, counts_side, counts_far, slopes, slopes_side, slopes_far)
    enc_parts, dec_parts = [], []
    for first, last in ((0, 2), (2, 4)):
        enc_own, enc_out, dec_own, dec_out = parts_call(
            tables, (grad_four, cells_four), first, last
        )
        enc_parts += [enc_own, swap(enc_out, 2)]
        dec_parts += [dec_own, swap(dec_out, 4)]
    cells, grad_in, _ = lax.optimization_barrier((cells, grad_in, enc_out))
    logits, gene_grad = expand_call(enc_weight, dec, cells, grad_in)
    enc_grad, dec_grad = join_call(counts.shape[0], enc_parts + dec_parts)
    small = sums[:4].reshape(-1)
    place = lax.axis_index("dp") * 4 + lax.axis_index("gene")
    gain_grad = lax.dynamic_slice_in_dim(small[: 2 * model_width], place * 64, 64)
    bias_grad = lax.dynamic_slice_in_dim(
        small[2 * model_width : 3 * model_width], place * 32, 32
    )
    mid_bias_grad = lax.dynamic_slice_in_dim(small[3 * model_width :], place * 32, 32)
    return (
        logits.T,
        gene_grad.T,
        enc_grad,
        dec_grad.T,
        layer_grad[0],
        layer_grad[1],
        layer_grad[2],
        gain_grad,
        bias_grad,
        mid_bias_grad,
    )


def solution(mesh):
    fast = dict(mesh.shape) == {"dp": 8, "gene": 4}
    in_specs = (
        P("dp", "gene"),
        P(None, ("dp", "gene")),
        P("dp", None),
        P("gene", None),
        P(None, "gene"),
        P(("dp", "gene"), None),
        P(("dp", "gene"), None),
        P(("dp", "gene"), None),
        P(("dp", "gene")),
        P(("dp", "gene")),
        P("dp", "gene"),
    )
    out_specs = (
        P("dp", "gene"),
        P("dp", "gene"),
        P("gene", "dp"),
        P("dp", "gene"),
        P(("dp", "gene"), None),
        P(("dp", "gene"), None),
        P(("dp", "gene"), None),
        P(("dp", "gene")),
        P(("dp", "gene")),
        P(("dp", "gene")),
    )
    return jax.shard_map(
        fast_body if fast else body, mesh=mesh, in_specs=in_specs, out_specs=out_specs, check_vma=False)
```

```python
import functools
import math

import jax
import jax.numpy as jnp
from jax import lax
from jax.experimental import pallas as pl
from jax.experimental.pallas import tpu as pltpu
from jax.sharding import PartitionSpec as P

HEADS = 16
HEAD_DIM = 64


epsilon = 1e-05


def norm_rows(values, gain, offset):
    center = values - jnp.mean(values, axis=-1, keepdims=True)
    spread = jnp.mean(center * center, axis=-1, keepdims=True)
    return center * lax.rsqrt(spread + epsilon) * gain + offset


def gelu_tanh(values):
    return jax.nn.gelu(values, approximate=True)


def positions(coords, model_width):
    indices = jnp.arange(model_width // 4).astype(coords.dtype)
    freqs = jnp.exp(indices * (-4.0 * math.log(10000.0) / model_width))
    along_x = coords[0][:, None] * freqs[None, :]
    along_y = coords[1][:, None] * freqs[None, :]
    return jnp.concatenate(
        [jnp.sin(along_x), jnp.cos(along_x), jnp.sin(along_y), jnp.cos(along_y)], axis=1
    )


def slide_ids(slide_lengths, length_all):
    places = jnp.arange(length_all, dtype=jnp.int32)
    return (places >= slide_lengths[0]).astype(jnp.int32) + (
        places >= slide_lengths[0] + slide_lengths[1]
    ).astype(jnp.int32)


def product(left, right):
    return jnp.dot(left, right, preferred_element_type=jnp.float32)


def contract_rows(left, right):
    return lax.dot_general(
        left, right, (((0,), (0,)), ((), ())), preferred_element_type=jnp.float32
    )


def contract_cols(left, right):
    return lax.dot_general(
        left, right, (((1,), (1,)), ((), ())), preferred_element_type=jnp.float32
    )


def body(
    gene_counts,
    coords,
    lengths,
    enc_weight,
    dec_weight,
    attn_weight,
    up_weight,
    down_weight,
    ln_gain,
    ln_bias,
    logit_grad,
):
    model_width = enc_weight.shape[1]
    group_rows = gene_counts.shape[0]
    own_rows = coords.shape[1]
    gene_index = lax.axis_index("gene")
    score_scale = 1.0 / math.sqrt(HEAD_DIM)
    slide_all = slide_ids(lengths[0], group_rows)
    slide_own = lax.dynamic_slice_in_dim(slide_all, gene_index * own_rows, own_rows)
    live_rows = (slide_all < 2).astype(jnp.bfloat16)[:, None]
    attn_full, up_full, down_full, gain_full, bias_full = (
        lax.all_gather(attn_weight, ("dp", "gene"), axis=0, tiled=True),
        lax.all_gather(up_weight, ("dp", "gene"), axis=0, tiled=True),
        lax.all_gather(down_weight, ("dp", "gene"), axis=0, tiled=True),
        lax.all_gather(ln_gain, ("dp", "gene"), axis=0, tiled=True),
        lax.all_gather(ln_bias, ("dp", "gene"), axis=0, tiled=True),
    )
    norm_gains = gain_full.astype(jnp.float32)
    offsets = bias_full.astype(jnp.float32)
    proj_weight = attn_full[: 3 * model_width]
    out_weight = attn_full[3 * model_width :]
    embedded = lax.psum_scatter(
        product(gene_counts, enc_weight).astype(jnp.bfloat16),
        "gene",
        scatter_dimension=0,
        tiled=True,
    ).astype(jnp.float32)
    stream_in = embedded + positions(coords, model_width)
    first_normed, first_pull = jax.vjp(
        norm_rows, stream_in, norm_gains[:model_width], offsets[:model_width]
    )
    first_low = first_normed.astype(jnp.bfloat16)
    projected = contract_cols(first_low, proj_weight).astype(jnp.bfloat16)
    queries = projected[:, :model_width].reshape(own_rows, HEADS, HEAD_DIM)
    keyval_all = lax.all_gather(projected[:, model_width:], "gene", axis=0, tiled=True)
    keys_all = keyval_all[:, :model_width].reshape(group_rows, HEADS, HEAD_DIM)
    values_all = keyval_all[:, model_width:].reshape(group_rows, HEADS, HEAD_DIM)
    same_slide = (slide_own[:, None] == slide_all[None, :])[None]
    scores = (
        jnp.einsum("qhd,khd->hqk", queries, keys_all, preferred_element_type=jnp.float32)
        * score_scale
    )
    scores = jnp.where(same_slide, scores, -1e30)
    row_max = jnp.max(scores, axis=-1, keepdims=True)
    raised = jnp.exp(scores - row_max)
    soft = raised / jnp.sum(raised, axis=-1, keepdims=True)
    soft_low = soft.astype(jnp.bfloat16)
    attended = jnp.einsum("hqk,khd->qhd", soft_low, values_all, preferred_element_type=jnp.float32)
    attended = attended.reshape(own_rows, model_width).astype(jnp.bfloat16)
    stream_mid = stream_in + product(attended, out_weight)
    second_normed, second_pull = jax.vjp(
        norm_rows, stream_mid, norm_gains[model_width:], offsets[model_width:]
    )
    second_low = second_normed.astype(jnp.bfloat16)
    hidden_pre = contract_cols(second_low, up_full)
    active, gelu_pull = jax.vjp(gelu_tanh, hidden_pre)
    active_low = active.astype(jnp.bfloat16)
    stream_out = stream_mid + product(active_low, down_full)
    cells_low = stream_out.astype(jnp.bfloat16)
    cells_all = lax.all_gather(cells_low, "gene", axis=0, tiled=True)
    logits_full = product(cells_all, dec_weight)
    logits = (logits_full * live_rows.astype(jnp.float32)).astype(jnp.bfloat16)
    masked_grad = logit_grad * live_rows
    grad_out = lax.psum_scatter(
        contract_cols(masked_grad, dec_weight).astype(jnp.bfloat16),
        "gene",
        scatter_dimension=0,
        tiled=True,
    ).astype(jnp.float32)
    dec_part = contract_rows(cells_all, masked_grad)
    grad_branch = grad_out.astype(jnp.bfloat16)
    down_part = contract_rows(active_low, grad_branch)
    grad_active = contract_cols(grad_branch, down_full)
    grad_hidden = gelu_pull(grad_active)[0].astype(jnp.bfloat16)
    up_part = contract_rows(grad_hidden, second_low)
    grad_second = product(grad_hidden, up_full)
    grad_mid_norm, gain_second, bias_second = second_pull(grad_second)
    grad_mid = grad_out + grad_mid_norm
    grad_attn = grad_mid.astype(jnp.bfloat16)
    out_part = contract_rows(attended, grad_attn)
    grad_attended = (
        contract_cols(grad_attn, out_weight).astype(jnp.bfloat16).reshape(own_rows, HEADS, HEAD_DIM)
    )
    grad_soft = jnp.einsum(
        "qhd,khd->hqk", grad_attended, values_all, preferred_element_type=jnp.float32
    )
    grad_scores = soft * (grad_soft - jnp.sum(grad_soft * soft, axis=-1, keepdims=True))
    grad_scores = grad_scores.astype(jnp.bfloat16)
    grad_query = (
        jnp.einsum("hqk,khd->qhd", grad_scores, keys_all, preferred_element_type=jnp.float32)
        * score_scale
    )
    grad_query = grad_query.reshape(own_rows, model_width).astype(jnp.bfloat16)
    grad_keys = (
        jnp.einsum("hqk,qhd->khd", grad_scores, queries, preferred_element_type=jnp.float32)
        * score_scale
    )
    grad_values = jnp.einsum(
        "hqk,qhd->khd", soft_low, grad_attended, preferred_element_type=jnp.float32
    )
    keyval_part = jnp.concatenate(
        [grad_keys.reshape(group_rows, model_width), grad_values.reshape(group_rows, model_width)],
        axis=1,
    )
    grad_keyval = lax.psum_scatter(
        keyval_part.astype(jnp.bfloat16), "gene", scatter_dimension=0, tiled=True
    )
    grad_proj = jnp.concatenate([grad_query, grad_keyval], axis=1)
    proj_part = contract_rows(grad_proj, first_low)
    grad_first = product(grad_proj, proj_weight)
    grad_in_norm, gain_first, bias_first = first_pull(grad_first)
    grad_in = (grad_mid + grad_in_norm).astype(jnp.bfloat16)
    grad_in_all = lax.all_gather(grad_in, "gene", axis=0, tiled=True)
    gene_grad = contract_cols(grad_in_all, enc_weight).astype(jnp.bfloat16)
    enc_part = contract_rows(gene_counts, grad_in_all)
    enc_grad, dec_grad = (
        lax.psum_scatter(enc_part, "dp", scatter_dimension=1, tiled=True),
        lax.psum_scatter(dec_part, "dp", scatter_dimension=0, tiled=True),
    )
    attn_part = jnp.concatenate([proj_part, out_part], axis=0)
    gain_part = jnp.concatenate([gain_first, gain_second], axis=0)
    attn_grad, up_grad, down_grad, gain_grad, bias_grad, mid_bias_grad = (
        lax.psum_scatter(attn_part, ("dp", "gene"), scatter_dimension=0, tiled=True),
        lax.psum_scatter(up_part, ("dp", "gene"), scatter_dimension=0, tiled=True),
        lax.psum_scatter(down_part, ("dp", "gene"), scatter_dimension=0, tiled=True),
        lax.psum_scatter(gain_part, ("dp", "gene"), scatter_dimension=0, tiled=True),
        lax.psum_scatter(bias_first, ("dp", "gene"), scatter_dimension=0, tiled=True),
        lax.psum_scatter(bias_second, ("dp", "gene"), scatter_dimension=0, tiled=True),
    )
    return (
        logits,
        gene_grad,
        enc_grad,
        dec_grad,
        attn_grad,
        up_grad,
        down_grad,
        gain_grad,
        bias_grad,
        mid_bias_grad,
    )


MESH = pl.DeviceIdType.MESH
MIB = 2**20
VMEM = pl.BlockSpec(memory_space=pltpu.VMEM)
SMEM = pl.BlockSpec(memory_space=pltpu.SMEM)
ANY = pl.BlockSpec(memory_space=pl.ANY)
DMA = pltpu.SemaphoreType.DMA


class Place:
    def __init__(self):
        self.dp = dp = lax.axis_index("dp")
        self.z = z = lax.axis_index("gene")
        self.core = dp % 2
        self.chip = dp // 2
        self.inner = z * (3 - z) > 0
        self.outer = z * (3 - z) == 0
        self.pair = (dp, z + 1 - 2 * (z % 2))
        self.middle = (dp, 3 - z)
        self.sibling_dp = dp + 1 - 2 * (dp % 2)
        self.x_dp = dp + 2 - 4 * ((dp // 2) % 2)
        self.y_dp = dp + 4 - 8 * (dp // 4)
        self.xy_dp = self.x_dp + 4 - 8 * (dp // 4)
        self.sibling = (self.sibling_dp, z)
        self.far_dps = (self.x_dp, self.y_dp, self.xy_dp)
        self.far = tuple((d, z) for d in self.far_dps)
        self.x_side = (self.x_dp + self.sibling_dp - dp, z)
        self.y_side = (self.y_dp + self.sibling_dp - dp, z)
        self.xy_side = (self.xy_dp + self.sibling_dp - dp, z)
        self.plane = self.far + (self.sibling, self.x_side, self.y_side, self.xy_side)
        self.line = tuple((dp, (z + k) % 4) for k in (1, 2, 3))

    def meet(self, devices):
        barrier = pltpu.get_barrier_semaphore()
        for device in devices:
            pl.semaphore_signal(barrier, inc=1, device_id=device, device_id_type=MESH)
        pl.semaphore_wait(barrier, len(devices))

    def meet_line(self):
        barrier = pltpu.get_barrier_semaphore()
        pl.semaphore_signal(barrier, inc=1, device_id=self.pair, device_id_type=MESH)

        @pl.when(self.inner)
        def _():
            pl.semaphore_signal(barrier, inc=1, device_id=self.middle, device_id_type=MESH)
            pl.semaphore_wait(barrier, 2)

        @pl.when(self.outer)
        def _():
            pl.semaphore_wait(barrier, 1)


def send(src, dst, send_sem, recv_sem, device):
    return pltpu.make_async_remote_copy(
        src_ref=src,
        dst_ref=dst,
        send_sem=send_sem,
        recv_sem=recv_sem,
        device_id=device,
        device_id_type=MESH,
    )


class LineSum:
    SEMS = 6

    def __init__(self, place, part, inbox, peer, total, sems, view):
        self.place, self.part, self.inbox, self.peer, self.total = place, part, inbox, peer, total
        self.sems, self.view = sems, view

    def up(self, k):
        s, v = self.sems, self.view
        return send(v(self.part, k), v(self.inbox, k), s.at[0, k], s.at[1, k], self.place.pair)

    def across(self, k):
        s, v = self.sems, self.view
        return send(v(self.part, k), v(self.peer, k), s.at[2, k], s.at[3, k], self.place.middle)

    def down(self, k):
        s, v = self.sems, self.view
        return send(v(self.total, k), v(self.total, k), s.at[4, k], s.at[5, k], self.place.pair)

    def push(self, k):
        @pl.when(self.place.outer)
        def _():
            self.up(k).start()

    def meet_up(self, k):
        @pl.when(self.place.inner)
        def _():
            self.up(k).wait_recv()
            mine, other = self.view(self.part, k), self.view(self.inbox, k)
            mine[...] = (mine[...].astype(jnp.float32) + other[...].astype(jnp.float32)).astype(
                jnp.bfloat16
            )
            self.across(k).start()

    def meet_across(self, k):
        @pl.when(self.place.inner)
        def _():
            self.across(k).wait_recv()
            mine, other = self.view(self.part, k), self.view(self.peer, k)
            self.view(self.total, k)[...] = (
                mine[...].astype(jnp.float32) + other[...].astype(jnp.float32)
            ).astype(jnp.bfloat16)
            self.down(k).start()

    def get(self, k):
        @pl.when(self.place.outer)
        def _():
            self.down(k).wait_recv()

    def finish_part(self, count):
        @pl.when(self.place.outer)
        def _():
            for k in range(count):
                self.up(k).wait_send()

        @pl.when(self.place.inner)
        def _():
            for k in range(count):
                self.across(k).wait_send()

    def finish_total(self, count):
        @pl.when(self.place.inner)
        def _():
            for k in range(count):
                self.down(k).wait_send()


class Rows:
    def __init__(self, ref, base, group):
        self.ref, self.base, self.group = ref, base, group

    def slot(self, index):
        return self.ref.at[pl.ds(self.base + index * self.group, self.group)]


def lane_block(ref, k):
    return ref.at[:, pl.ds(k * 128, 128)]


def columns(ref, k, width):
    return ref.at[:, pl.ds(k * width, width)]


def row_live(lengths, rows):
    index = lax.broadcasted_iota(jnp.int32, (rows, 1), 0)
    return (index < lengths[0, 0] + lengths[0, 1]).astype(jnp.float32)


def exact(value):
    return value.astype(jnp.float32)


def low(value):
    return value.astype(jnp.bfloat16)


def rows_of(ref, k):
    return ref.at[pl.ds(k * 64, 64)]


def normalize(values):
    center = values - jnp.mean(values, axis=-1, keepdims=True)
    spread = jnp.mean(center * center, axis=-1, keepdims=True)
    scale = lax.rsqrt(spread + epsilon)
    return center * scale, scale


def norm_back(grad, gain, normed, scale):
    lifted = grad * gain
    return scale * (
        lifted
        - jnp.mean(lifted, axis=-1, keepdims=True)
        - normed * jnp.mean(lifted * normed, axis=-1, keepdims=True)
    )


def gelu_both(u):
    curve, factor = 0.044715, math.sqrt(2.0 / math.pi)
    square = u * u
    bent = jnp.tanh(factor * (u + curve * u * square))
    half = 0.5 * (1.0 + bent)
    slope = half + 0.5 * u * (1.0 - bent * bent) * (factor * (1.0 + 3.0 * curve * square))
    return u * half, slope


def layer_kernel(
    coords,
    lengths,
    counts,
    enc,
    slopes,
    dec,
    attn_own,
    up_own,
    down_own,
    gain_own,
    bias_own,
    cells,
    grad_in,
    cells_four,
    grad_four,
    grads,
    sums_all,
    counts_side,
    slopes_side,
    counts_far,
    slopes_far,
    weights,
    vectors,
    counts_v,
    enc_v,
    slopes_v,
    dec_v,
    work,
    places,
    qkv,
    soft,
    key_sum,
    value_sum,
    gains,
    offsets,
    part_m,
    part_o,
    part_s,
    inbox_m,
    inbox_o,
    peer_m,
    peer_o,
    peer_s,
    stream,
    total_m,
    total_o,
    total_s,
    branch_rows,
    outgoing,
    arriving,
    sums,
    sums_box,
    load_sems,
    line_sems,
    gather_sems,
    vector_sems,
    tile_sems,
    side_sems,
    far_sems,
    pair_sems,
    four_sems,
    sums_sems,
    ready_sem,
):
    place = Place()
    group, width = cells.shape
    dp, z = place.dp, place.z
    step = width // 4
    local = width // 4
    span = 128
    parts = group // span
    lane = lax.broadcasted_iota(jnp.int32, (1, span), 1)
    head_lanes = [low((lane // HEAD_DIM == h).astype(jnp.float32)) for h in range(2)]
    head_exact = [exact(h) for h in head_lanes]
    first_end, second_end = lengths[0, 0], lengths[0, 0] + lengths[0, 1]

    def slide_of(index):
        return (index >= first_end).astype(jnp.int32) + (index >= second_end).astype(jnp.int32)

    def rows(r):
        return slice(r * span, (r + 1) * span)

    def row_index(r):
        return lax.broadcasted_iota(jnp.int32, (span, 1), 0) + r * span

    def matrix(i, start, stop):
        return weights[i, start:stop].reshape((stop - start) * span, width)

    first, attn, cat = [Rows(enc_v, i * 2 * group, group) for i in range(3)]
    active, hidden, second = [Rows(dec_v, i * 2 * group, group) for i in range(3)]

    def key_masked(p):
        return counts_v.at[pl.ds(0, 2 * group), pl.ds(p * span, span)]

    def value_masked(p):
        return counts_v.at[pl.ds(0, 2 * group), pl.ds((2 + p) * span, span)]

    def staged(i, t):
        return counts_v.at[pl.ds((2 + t) * group, group), pl.ds(i * 2 * span, 2 * span)]

    def side_copy(ref, i):
        return send(
            ref.slot(0), ref.slot(1), side_sems.at[0, i], side_sems.at[1, i], place.sibling
        )

    side_active, side_hidden, side_second = [
        side_copy(ref, i) for i, ref in enumerate((active, hidden, second))
    ]
    side_cat, side_first, side_attn = [
        side_copy(ref, 4 + i) for i, ref in enumerate((cat, first, attn))
    ]
    side_branch = send(
        branch_rows.at[0], branch_rows.at[1], side_sems.at[0, 3], side_sems.at[1, 3], place.sibling
    )

    pair_far = [
        send(src, dst.at[0], pair_sems.at[0, i], pair_sems.at[1, i], device)
        for i, (src, dst, device) in enumerate(
            ((counts, counts_far, place.far[1]), (slopes, slopes_far, place.far[0]))
        )
    ]
    pair_side = [
        send(dst.at[0], dst.at[1], pair_sems.at[0, 2 + i], pair_sems.at[1, 2 + i], place.sibling)
        for i, dst in enumerate((counts_far, slopes_far))
    ]
    cells_to = (place.sibling, place.far[0], place.x_side)
    grad_to = (place.sibling, place.far[1], place.y_side)

    def other_core(d):
        return d + 1 - 2 * (d % 2)

    x_dp, y_dp, xy_dp = place.far_dps
    own_pair, x_pair, y_pair = (place.dp, y_dp), (x_dp, xy_dp), (place.dp, x_dp)
    cells_blocks = (own_pair, tuple(map(other_core, own_pair)), x_pair, tuple(map(other_core, x_pair)))
    x_row = (y_dp, xy_dp)
    grad_blocks = (y_pair, tuple(map(other_core, y_pair)), x_row, tuple(map(other_core, x_row)))

    def four_copy(i, four, devices, t, r):
        block = pl.ds(r * span, span)
        return send(
            staged(i, t).at[block],
            four.at[1 + t, block],
            four_sems.at[0, i, t, r],
            four_sems.at[1, i, t, r],
            devices[t],
        )

    def cells_copy(t, r):
        return four_copy(0, cells_four, cells_to, t, r)

    def grad_copy(t, r):
        return four_copy(1, grad_four, grad_to, t, r)

    def spread(ref, i, four, blocks, copy, r):
        for t, pair in enumerate(blocks):
            for n, d in enumerate(pair):
                block = ref[rows(r), pl.ds(pl.multiple_of(d * span, span), span)]
                at = slice(n * span, (n + 1) * span)
                if t == 0:
                    four[0, rows(r), at] = block
                else:
                    staged(i, t - 1)[rows(r), at] = block
            if t > 0:
                copy(t - 1, r).start()

    def line_sum(i, part, inbox, peer, total, view):
        return LineSum(place, part, inbox, peer, total, line_sems.at[i], view)

    sum_a = line_sum(0, part_m, inbox_m, peer_s, stream, lane_block)
    sum_b = line_sum(1, part_o, inbox_o, peer_o, branch_rows.at[0], lane_block)
    sum_m = line_sum(2, part_m, inbox_m, peer_m, total_m, rows_of)
    sum_o = line_sum(3, part_o, inbox_o, peer_o, total_o, rows_of)
    sum_s = line_sum(4, part_s, inbox_m, peer_s, total_s, rows_of)
    sum_f = line_sum(5, part_s, inbox_m, peer_m, total_s, rows_of)
    all_sums = dict(a=sum_a, b=sum_b, m=sum_m, o=sum_o, s=sum_s, f=sum_f)

    def loads_of(table, table_v, wide, wide_v, i):
        found = [pltpu.make_async_copy(table, table_v, load_sems.at[i, 0])]
        for j in range(4):
            found.append(
                pltpu.make_async_copy(
                    columns(wide, j, step), columns(wide_v, j, step), load_sems.at[i, 1 + j]
                )
            )
        return found

    loads = [
        loads_of(counts, counts_v, enc, enc_v, 0),
        loads_of(slopes, slopes_v, dec, dec_v, 1),
    ]
    for copy in loads[0] + loads[1]:
        copy.start()
    for i, ref in enumerate((attn_own, up_own, down_own)):
        weights[i, dp] = ref[...]
    tile = vectors.at[dp * 4 + z]
    tile[...] = jnp.zeros_like(tile)
    tile[0:1, 0:64] = exact(gain_own[...])
    tile[1:2, 0:64] = exact(bias_own[...])
    place.meet(place.plane + place.line)

    line_out = [
        send(tile, tile, tile_sems.at[0, i], tile_sems.at[1, i], device)
        for i, device in enumerate(place.line)
    ]
    for copy in line_out:
        copy.start()

    def weight_far(i, q, d):
        block = weights.at[i, d]
        return send(
            block, block, gather_sems.at[0, i, q], gather_sems.at[1, i, q], place.far[q]
        )

    def weight_side(i, q):
        block = weights.at[i, ((dp,) + place.far_dps)[q]]
        return send(
            block, block, gather_sems.at[2, i, q], gather_sems.at[3, i, q], place.sibling
        )

    def tiles(d):
        return vectors.at[pl.ds(d * 4, 4)]

    vec_far = [
        send(tiles(dp), tiles(dp), vector_sems.at[0, q], vector_sems.at[1, q], device)
        for q, device in enumerate(place.far)
    ]
    vec_side = [
        send(tiles(d), tiles(d), vector_sems.at[2, q], vector_sems.at[3, q], place.sibling)
        for q, d in enumerate((dp,) + place.far_dps)
    ]
    def weights_out(some):
        for i in some:
            for q in range(3):
                weight_far(i, q, dp).start()
            weight_side(i, 0).start()

    weights_out((0,))
    own_side = [
        send(src, dst, pair_sems.at[0, 4 + i], pair_sems.at[1, 4 + i], place.sibling)
        for i, (src, dst) in enumerate(((counts_v, counts_side), (slopes_v, slopes_side)))
    ]

    own_rows = coords.shape[1]
    index = lax.broadcasted_iota(jnp.int32, (1, step), 1).astype(jnp.float32)
    freqs = jnp.exp(index * (-4.0 * math.log(10000.0) / width))
    for axis in range(2):
        along = jnp.broadcast_to(coords[axis : axis + 1, :], (own_rows, own_rows)).T
        angle = along[:, 0:1] * freqs
        places[2 * axis] = jnp.sin(angle)
        places[2 * axis + 1] = jnp.cos(angle)
    own = pl.ds(pl.multiple_of(z * own_rows, own_rows), own_rows)
    sums[...] = jnp.zeros_like(sums)
    key_sum[...] = jnp.zeros_like(key_sum)
    value_sum[...] = jnp.zeros_like(value_sum)

    def vectors_on(k):
        if k == 0:
            for copy in line_out:
                copy.wait_recv()
            for copy in vec_far + vec_side[:1]:
                copy.start()
            weights_out((1, 2))
            for copy in pair_far:
                copy.start()
        if k == 1:
            for q in range(3):
                vec_far[q].wait_recv()
                vec_side[1 + q].start()
        if k == 2:
            for copy in vec_side:
                copy.wait_recv()
            for n in range(2 * width // span):
                for ref, row in ((gains, 0), (offsets, 1)):
                    ref[0:1, n * span : (n + 1) * span] = jnp.concatenate(
                        [vectors[2 * n + i, row : row + 1, 0:64] for i in range(2)], axis=1
                    )

    def weights_on(some, k):
        for i in some:
            if k == 0:
                for q, d in enumerate(place.far_dps):
                    weight_far(i, q, d).wait_recv()
                    weight_side(i, 1 + q).start()
            else:
                for q in range(4):
                    weight_side(i, q).wait_recv()

    def encode(j):
        if j == 0:
            loads[0][0].wait()
            own_side[0].start()
        loads[0][1 + j].wait()
        work[...] = contract_rows(counts_v[...], enc_v[:, j * step : (j + 1) * step])
        work[own, :] += places[j]
        part_m[:, j * step : (j + 1) * step] = low(work[...])
        for k in range(2 * j, 2 * j + 2):
            sum_a.push(k)

    def decode(j):
        if j == 0:
            loads[1][0].wait()
            own_side[1].start()
        loads[1][1 + j].wait()
        live = (lax.broadcasted_iota(jnp.int32, (group, 1), 0) < second_end).astype(jnp.float32)
        part_o[:, j * step : (j + 1) * step] = low(
            contract_rows(slopes_v[...], dec_v[:, j * step : (j + 1) * step]) * live
        )

    def project(r):
        gain_a, offset_a = gains[0:1, :width], offsets[0:1, :width]
        if r == 0:
            for k in range(8):
                sum_a.get(k)
            own_side[0].wait_send()
            pl.semaphore_signal(
                ready_sem, inc=1, device_id=place.sibling, device_id_type=MESH
            )
        normed, _ = normalize(exact(stream[rows(r), :]))
        value = low(normed * gain_a + offset_a)
        first.slot(0)[rows(r), :] = value
        qkv[rows(r), :] = low(contract_cols(value, matrix(0, 0, 6)))
        for p in range(2):
            for ref, at in ((key_masked(p), local), (value_masked(p), 2 * local)):
                block = qkv[rows(r), at + p * span : at + (p + 1) * span]
                for h in range(2):
                    ref[h * group + r * span : h * group + (r + 1) * span, :] = (
                        block * head_lanes[h]
                    )

    def attend(r):
        if r == 0:
            pl.semaphore_wait(ready_sem, 1)
            side_first.start()
            sum_a.finish_part(8)
        same = slide_of(row_index(r)) == slide_of(
            lax.broadcasted_iota(jnp.int32, (1, group), 1)
        )
        for p in range(2):
            query = qkv[rows(r), p * span : (p + 1) * span]
            scores = contract_cols(query, key_masked(p)[...]) * (1.0 / math.sqrt(HEAD_DIM))
            for h in range(2):
                own = jnp.where(same, scores[:, h * group : (h + 1) * group], -1e30)
                raised = jnp.exp(own - jnp.max(own, axis=-1, keepdims=True))
                soft[p, rows(r), h * group : (h + 1) * group] = low(
                    raised / jnp.sum(raised, axis=-1, keepdims=True)
                )
            cat.slot(0)[rows(r), 3 * local + p * span : 3 * local + (p + 1) * span] = low(
                product(soft[p, rows(r), :], value_masked(p)[...])
            )
        part_m[rows(r), :] = low(product(cat.slot(0)[rows(r), 3 * local :], matrix(0, 6, 8)))
        push(sum_m, r)

    def middle(r):
        return exact(stream[rows(r), :]) + exact(total_m[rows(r), :])

    def feed(r):
        gain_b, offset_b = gains[0:1, width:], offsets[0:1, width:]
        if r == 0:
            for k in range(8):
                sum_b.get(k)
            sum_b.finish_part(8)
        get(sum_m, r)
        normed, _ = normalize(middle(r))
        value = low(normed * gain_b + offset_b)
        second.slot(0)[rows(r), :] = value
        act, slope = gelu_both(contract_cols(value, matrix(1, 0, 8)))
        active.slot(0)[rows(r), :] = low(act)
        grad = branch_rows[0, rows(r), :]
        back = low(contract_cols(grad, matrix(2, 0, 8)) * slope)
        hidden.slot(0)[rows(r), :] = back
        part_s[rows(r), :] = low(product(back, matrix(1, 0, 8)))
        push(sum_s, r)
        part_o[rows(r), :] = low(product(active.slot(0)[rows(r), :], matrix(2, 0, 8)))

    def attend_back(r):
        gain_b = gains[0:1, width:]
        get(sum_s, r)
        normed, scale = normalize(middle(r))
        grad = exact(total_s[rows(r), :])
        sums[1:2, :] += jnp.sum(grad * normed, axis=0, keepdims=True)
        sums[3:4, :] += jnp.sum(grad, axis=0, keepdims=True)
        mid = exact(branch_rows[0, rows(r), :]) + norm_back(grad, gain_b, normed, scale)
        attn.slot(0)[rows(r), :] = low(mid)
        back = low(contract_cols(low(mid), matrix(0, 6, 8)))
        for p in range(2):
            out = back[:, p * span : (p + 1) * span]
            slopes = contract_cols(out, value_masked(p)[...])
            marks = []
            for h in range(2):
                block = exact(soft[p, rows(r), h * group : (h + 1) * group])
                slope = slopes[:, h * group : (h + 1) * group]
                inner = jnp.sum(slope * block, axis=-1, keepdims=True)
                marks.append(low(block * (slope - inner)))
            scale_q = 1.0 / math.sqrt(HEAD_DIM)
            cat.slot(0)[rows(r), p * span : (p + 1) * span] = low(
                product(jnp.concatenate(marks, axis=1), key_masked(p)[...]) * scale_q
            )
            query = qkv[rows(r), p * span : (p + 1) * span]
            at = slice(p * span, (p + 1) * span)
            key_sum[:, at] += contract_rows(
                jnp.concatenate(marks, axis=0),
                jnp.concatenate([query * lanes for lanes in head_lanes], axis=0),
            )
            value_sum[:, at] += contract_rows(
                jnp.concatenate(
                    [soft[p, rows(r), h * group : (h + 1) * group] for h in range(2)], axis=0
                ),
                jnp.concatenate([out * lanes for lanes in head_lanes], axis=0),
            )

    def project_back(r):
        if r == 0:
            sum_s.finish_part(8)
            sum_s.finish_total(8)
            cat.slot(0)[:, local : 2 * local] = low(key_sum[...] * (1.0 / math.sqrt(HEAD_DIM)))
            cat.slot(0)[:, 2 * local : 3 * local] = low(value_sum[...])
        part_s[rows(r), :] = low(product(cat.slot(0)[rows(r), : 3 * local], matrix(0, 0, 6)))
        push(sum_f, r)

    def finish_in(r):
        gain_a = gains[0:1, :width]
        get(sum_f, r)
        normed, scale = normalize(exact(stream[rows(r), :]))
        grad = exact(total_s[rows(r), :])
        sums[0:1, :] += jnp.sum(grad * normed, axis=0, keepdims=True)
        sums[2:3, :] += jnp.sum(grad, axis=0, keepdims=True)
        grad_in[rows(r), :] = low(
            exact(attn.slot(0)[rows(r), :]) + norm_back(grad, gain_a, normed, scale)
        )
        spread(grad_in, 1, grad_four, grad_blocks, grad_copy, r)

    def finish_out(r):
        get(sum_o, r)
        live = (row_index(r) < second_end).astype(jnp.float32)
        cells[rows(r), :] = low((middle(r) + exact(total_o[rows(r), :])) * live)
        spread(cells, 0, cells_four, cells_blocks, cells_copy, r)

    def push(total, r):
        total.push(2 * r)
        total.push(2 * r + 1)

    def get(total, r):
        total.get(2 * r)
        total.get(2 * r + 1)

    chips = tuple(d // 2 for d in place.far_dps) + (place.chip,)

    def lanes_of(ref, slot, chip):
        start = pl.multiple_of((chip * 2 + place.core) * span, span)
        return ref.slot(slot)[:, pl.ds(start, span)]

    def far_copy(i, q):
        return send(
            outgoing.at[i, q],
            arriving.at[i, q],
            far_sems.at[0, i, q],
            far_sems.at[1, i, q],
            place.far[q],
        )

    def keep(i, q, value):
        if q == 3:
            grads[i] = value
        else:
            outgoing[i, q] = low(value)
            far_copy(i, q).start()

    def weight_grad(i, left, right, half):
        pair = chips[2 * half : 2 * half + 2]
        got = sum(
            contract_rows(
                jnp.concatenate([lanes_of(left, slot, chip) for chip in pair], axis=1),
                right(slot),
            )
            for slot in range(2)
        )
        for k in range(2):
            keep(i, 2 * half + k, got[k * span : (k + 1) * span])

    def attn_right(kind, slot):
        start = pl.multiple_of(kind * 2 * group + slot * group, group)
        return enc_v[pl.ds(start, group), :]

    def attn_grad(q):
        kind = chips[q] // 3
        keep(
            0,
            q,
            sum(
                contract_rows(lanes_of(cat, slot, chips[q]), attn_right(kind, slot))
                for slot in range(2)
            ),
        )

    def run(word):
        name, k = word[:-1], int(word[-1])
        if name[0] in "ux":
            total = all_sums[name[1]]
            (total.meet_up if name[0] == "u" else total.meet_across)(k)
        else:
            steps[name](k)

    def start_feed_sides(_):
        for copy in (side_hidden, side_second, side_active, side_branch):
            copy.start()

    def start_attn_sides(_):
        side_cat.start()
        side_attn.start()

    def pass_on(i):
        pair_far[i].wait_recv()
        pair_side[i].start()

    def up_grad(half):
        if half == 0:
            side_hidden.wait_recv()
            side_second.wait_recv()
        weight_grad(1, hidden, lambda slot: second.slot(slot)[...], half)

    def down_grad(half):
        if half == 0:
            side_active.wait_recv()
            side_branch.wait_recv()
        weight_grad(2, active, lambda slot: branch_rows[slot], half)

    def attn_grads(half):
        if half == 0:
            side_first.wait_recv()
            side_attn.wait_recv()
            side_cat.wait_recv()
        attn_grad(2 * half)
        attn_grad(2 * half + 1)

    def push_branch(j):
        sum_b.push(2 * j)
        sum_b.push(2 * j + 1)

    steps = dict(
        N=encode,
        M=decode,
        Q=push_branch,
        V=vectors_on,
        W=functools.partial(weights_on, (0,)),
        Y=functools.partial(weights_on, (1, 2)),
        A=project,
        B=attend,
        C=feed,
        D=attend_back,
        G=project_back,
        E=finish_in,
        F=finish_out,
        P=lambda r: push(sum_o, r),
        S=start_feed_sides,
        T=start_attn_sides,
        X=pass_on,
        H=up_grad,
        L=down_grad,
        K=attn_grads,
    )
    for word in SCHEDULE:
        run(word)
    sums_out = [
        send(sums, sums_box.at[i], sums_sems.at[0, i], sums_sems.at[1, i], device)
        for i, device in enumerate(place.plane)
    ]
    for copy in sums_out:
        copy.start()
    for i in (2, 1, 0):
        for q in range(3):
            far_copy(i, q).wait_recv()
        grads[i] = grads[i] + sum(exact(arriving[i, q]) for q in range(3))
    for copy in sums_out:
        copy.wait()
    sums_all[...] = sums[...] + sum(sums_box[i] for i in range(len(sums_out)))
    for total in (sum_m, sum_o, sum_f):
        total.finish_part(8)
    for total in (sum_a, sum_b, sum_m, sum_o, sum_f):
        total.finish_total(8)
    for i in range(3):
        for q in range(3):
            weight_far(i, q, dp).wait_send()
        for q in range(4):
            weight_side(i, q).wait_send()
    for copy in line_out + vec_far + vec_side:
        copy.wait_send()
    own_side[0].wait_recv()
    own_side[1].wait()
    for i in range(3):
        for q in range(3):
            far_copy(i, q).wait_send()
    for t in range(3):
        for r in range(parts):
            cells_copy(t, r).wait()
            grad_copy(t, r).wait()
    for copy in pair_far:
        copy.wait_send()
    for copy in pair_side:
        copy.wait()
    for copy in (
        side_active,
        side_hidden,
        side_second,
        side_branch,
        side_cat,
        side_first,
        side_attn,
    ):
        copy.wait_send()


SCHEDULE = (
    "N0", "M0", "N1", "ua0", "ua1", "Q0", "M1", "xa0", "ua2", "ua3", "V0", "xa1", "N2", "ub0",
    "N3", "V1", "xa2", "ub1", "W0", "M2", "xa3", "V2", "ua4", "Q1", "xb0", "ua5", "M3", "xa4",
    "ua6", "Q2", "ua7", "xa5", "ub2", "xa6", "ub3", "xa7", "xb1", "Q3", "ub4", "xb2", "ub5",
    "xb3", "W1", "A0", "ub6", "A1", "xb4", "xb5", "A2", "ub7", "A3", "B0", "um0", "xb6", "B1",
    "um1", "xb7", "B2", "um2", "xm0", "xm1", "Y0", "um3", "B3", "xm2", "um4", "xm3", "um5", "Y1",
    "C0", "xm4", "um6", "um7", "xm5", "C1", "us0", "xm6", "us1", "xm7", "C2", "us2", "xs0", "us3",
    "xs1", "C3", "xs2", "us4", "us5", "S0", "P0", "xs3", "P1", "D0", "us6", "xs4", "D1", "xs5",
    "us7", "D2", "uo0", "xs6", "xs7", "uo1", "P2", "H0", "xo0", "uo2", "D3", "xo1", "uo3", "G0",
    "uo4", "xo2", "G1", "T0", "F0", "uo5", "xo3", "L0", "uf0", "H1", "xo4", "uf1", "xo5", "uf2",
    "P3", "xf0", "L1", "G2", "uf3", "xf1", "uo6", "G3", "xf2", "F1", "K0", "uo7", "xf3", "F2",
    "xo6", "uf4", "uf5", "xo7", "E0", "xf4", "uf6", "K1", "E1", "xf5", "uf7", "xf6", "xf7", "X0",
    "X1", "E2", "F3", "E3",
)


def layer_call(coords, lengths, counts, enc, slopes, dec, attn, up, down, gain, bias):
    genes, group = counts.shape
    width = enc.shape[1]
    half, full = jnp.bfloat16, jnp.float32
    plain = pltpu.VMEM((group, width), half)
    table, wide = pltpu.VMEM((genes, group), half), pltpu.VMEM((genes, width), half)
    return pl.pallas_call(
        layer_kernel,
        out_shape=(
            jax.ShapeDtypeStruct((group, width), half),
            jax.ShapeDtypeStruct((group, width), half),
            jax.ShapeDtypeStruct((4, group, 256), half),
            jax.ShapeDtypeStruct((4, group, 256), half),
            jax.ShapeDtypeStruct((3, 128, width), full),
            jax.ShapeDtypeStruct((8, width), full),
            jax.ShapeDtypeStruct(counts.shape, half),
            jax.ShapeDtypeStruct(slopes.shape, half),
            jax.ShapeDtypeStruct((2,) + counts.shape, half),
            jax.ShapeDtypeStruct((2,) + slopes.shape, half),
        ),
        in_specs=[VMEM, SMEM, ANY, ANY, ANY, ANY] + [VMEM] * 5,
        out_specs=(VMEM,) * 6 + (ANY,) * 4,
        scratch_shapes=[
            pltpu.VMEM((3, 8) + attn.shape, half),
            pltpu.VMEM((32, 8, 128), full),
            table,
            wide,
            table,
            wide,
            pltpu.VMEM((group, width // 4), full),
            pltpu.VMEM((4, coords.shape[1], width // 4), full),
            pltpu.VMEM((group, 3 * width // 4), half),
            pltpu.VMEM((2, group, 2 * group), half),
            pltpu.VMEM((group, width // 4), full),
            pltpu.VMEM((group, width // 4), full),
            pltpu.VMEM((1, 2 * width), full),
            pltpu.VMEM((1, 2 * width), full),
        ]
        + [plain] * 12
        + [
            pltpu.VMEM((2, group, width), half),
            pltpu.VMEM((3, 3, 128, width), half),
            pltpu.VMEM((3, 3, 128, width), half),
            pltpu.VMEM((8, width), full),
            pltpu.VMEM((7, 8, width), full),
            DMA((2, 5)),
            DMA((6, 6, 8)),
            DMA((4, 3, 4)),
            DMA((4, 4)),
            DMA((2, 3)),
            DMA((2, 7)),
            DMA((2, 3, 3)),
            DMA((2, 6)),
            DMA((2, 2, 3, 4)),
            DMA((2, 7)),
            pltpu.SemaphoreType.REGULAR,
        ],
        compiler_params=pltpu.CompilerParams(
            collective_id=1, has_side_effects=True, vmem_limit_bytes=60 * MIB
        ),
        name="layer",
    )(coords, lengths, counts, enc, slopes, dec, attn, up, down, gain, bias)


GENE_STEP = 848


def parts_kernel(
    counts,
    counts_side,
    counts_far,
    slopes,
    slopes_side,
    slopes_far,
    grad_four,
    cells_four,
    enc_own,
    enc_out,
    dec_own,
    dec_out,
):
    for own, side, far, right, kept, sent in (
        (counts, counts_side, counts_far, grad_four, enc_own, enc_out),
        (slopes, slopes_side, slopes_far, cells_four, dec_own, dec_out),
    ):
        lefts = (own[...], side[...], far[0], far[1])
        got = sum(product(left, right[t]) for t, left in enumerate(lefts))
        kept[...] = got[:, :128]
        sent[...] = low(got[:, 128:])


def parts_call(tables, fours, first, last):
    genes, group = tables[0].shape
    rows = min(last * GENE_STEP, genes) - first * GENE_STEP
    full = jax.ShapeDtypeStruct((rows, 128), jnp.float32)
    half = jax.ShapeDtypeStruct((rows, 128), jnp.bfloat16)
    flat = pl.BlockSpec((GENE_STEP, group), lambda i: (i + first, 0))
    pair = pl.BlockSpec((2, GENE_STEP, group), lambda i: (0, i + first, 0))
    four = pl.BlockSpec(fours[0].shape, lambda i: (0, 0, 0))
    return pl.pallas_call(
        parts_kernel,
        out_shape=(full, half, full, half),
        grid=(last - first,),
        in_specs=[flat, flat, pair, flat, flat, pair, four, four],
        out_specs=(pl.BlockSpec((GENE_STEP, 128), lambda i: (i, 0)),) * 4,
        cost_estimate=pl.CostEstimate(
            flops=16 * rows * group * 256,
            bytes_accessed=16 * rows * group + 12 * rows * 128,
            transcendentals=0,
        ),
        compiler_params=pltpu.CompilerParams(vmem_limit_bytes=60 * MIB),
        name="parts",
    )(*tables, *fours)


def join_kernel(*refs):
    block = pl.program_id(0)
    for n in range(2):
        kept_a, came_a, kept_b, came_b = refs[4 * n : 4 * n + 4]
        result = refs[8 + n]

        @pl.when(block < 2)
        def _():
            result[...] = kept_a[...] + exact(came_a[...])

        @pl.when(block >= 2)
        def _():
            result[...] = kept_b[...] + exact(came_b[...])


def join_call(genes, parts):
    early = pl.BlockSpec((GENE_STEP, 128), lambda i: (jnp.minimum(i, 1), 0))
    late = pl.BlockSpec((GENE_STEP, 128), lambda i: (jnp.maximum(i - 2, 0), 0))
    return pl.pallas_call(
        join_kernel,
        out_shape=(jax.ShapeDtypeStruct((genes, 128), jnp.float32),) * 2,
        grid=(-(-genes // GENE_STEP),),
        in_specs=[early, early, late, late] * 2,
        out_specs=(pl.BlockSpec((GENE_STEP, 128), lambda i: (i, 0)),) * 2,
        compiler_params=pltpu.CompilerParams(vmem_limit_bytes=60 * MIB),
        name="join",
    )(*parts)


def expand_kernel(enc, dec, cells, grad_in, logits, gene_grad):
    logits[...] = low(contract_cols(dec[...], cells[...]))
    gene_grad[...] = low(contract_cols(enc[...], grad_in[...]))


def expand_call(enc, dec, cells, grad_in):
    genes, width = enc.shape
    group = cells.shape[0]
    steps = -(-genes // GENE_STEP)
    half = jax.ShapeDtypeStruct((genes, group), jnp.bfloat16)
    table = pl.BlockSpec((GENE_STEP, width), lambda i: (i, 0))
    whole = pl.BlockSpec((group, width), lambda i: (0, 0))
    return pl.pallas_call(
        expand_kernel,
        out_shape=(half, half),
        grid=(steps,),
        in_specs=[table, table, whole, whole],
        out_specs=(pl.BlockSpec((GENE_STEP, group), lambda i: (i, 0)),) * 2,
        cost_estimate=pl.CostEstimate(
            flops=4 * genes * group * width,
            bytes_accessed=4 * genes * (width + group),
            transcendentals=0,
        ),
        compiler_params=pltpu.CompilerParams(vmem_limit_bytes=60 * MIB),
        name="expand",
    )(enc, dec, cells, grad_in)


def swap(values, bit):
    return lax.ppermute(values, "dp", [(d, d ^ bit) for d in range(8)])


def fast_body(
    gene_counts,
    coords,
    lengths,
    enc_weight,
    dec_weight,
    attn_weight,
    up_weight,
    down_weight,
    ln_gain,
    ln_bias,
    logit_grad,
):
    model_width = enc_weight.shape[1]
    counts, slopes, dec = gene_counts.T, logit_grad.T, dec_weight.T
    (
        cells,
        grad_in,
        cells_four,
        grad_four,
        layer_grad,
        sums,
        counts_side,
        slopes_side,
        counts_far,
        slopes_far,
    ) = layer_call(
        coords,
        lengths,
        counts,
        enc_weight,
        slopes,
        dec,
        attn_weight,
        up_weight,
        down_weight,
        ln_gain[None],
        ln_bias[None],
    )
    tables = (counts, counts_side, counts_far, slopes, slopes_side, slopes_far)
    enc_parts, dec_parts = [], []
    for first, last in ((0, 2), (2, 4)):
        enc_own, enc_out, dec_own, dec_out = parts_call(
            tables, (grad_four, cells_four), first, last
        )
        enc_parts += [enc_own, swap(enc_out, 2)]
        dec_parts += [dec_own, swap(dec_out, 4)]
    cells, grad_in, _ = lax.optimization_barrier((cells, grad_in, enc_out))
    logits, gene_grad = expand_call(enc_weight, dec, cells, grad_in)
    enc_grad, dec_grad = join_call(counts.shape[0], enc_parts + dec_parts)
    small = sums[:4].reshape(-1)
    place = lax.axis_index("dp") * 4 + lax.axis_index("gene")
    gain_grad = lax.dynamic_slice_in_dim(small[: 2 * model_width], place * 64, 64)
    bias_grad = lax.dynamic_slice_in_dim(
        small[2 * model_width : 3 * model_width], place * 32, 32
    )
    mid_bias_grad = lax.dynamic_slice_in_dim(small[3 * model_width :], place * 32, 32)
    return (
        logits.T,
        gene_grad.T,
        enc_grad,
        dec_grad.T,
        layer_grad[0],
        layer_grad[1],
        layer_grad[2],
        gain_grad,
        bias_grad,
        mid_bias_grad,
    )


def solution(mesh):
    fast = dict(mesh.shape) == {"dp": 8, "gene": 4}
    in_specs = (
        P("dp", "gene"),
        P(None, ("dp", "gene")),
        P("dp", None),
        P("gene", None),
        P(None, "gene"),
        P(("dp", "gene"), None),
        P(("dp", "gene"), None),
        P(("dp", "gene"), None),
        P(("dp", "gene")),
        P(("dp", "gene")),
        P("dp", "gene"),
    )
    out_specs = (
        P("dp", "gene"),
        P("dp", "gene"),
        P("gene", "dp"),
        P("dp", "gene"),
        P(("dp", "gene"), None),
        P(("dp", "gene"), None),
        P(("dp", "gene"), None),
        P(("dp", "gene")),
        P(("dp", "gene")),
        P(("dp", "gene")),
    )
    return jax.shard_map(
        fast_body if fast else body, mesh=mesh, in_specs=in_specs, out_specs=out_specs, check_vma=False)
```

```python
import functools
import math

import jax
import jax.numpy as jnp
from jax import lax
from jax.experimental import pallas as pl
from jax.experimental.pallas import tpu as pltpu
from jax.sharding import PartitionSpec as P

HEADS = 16
HEAD_DIM = 64


epsilon = 1e-05


def norm_rows(values, gain, offset):
    center = values - jnp.mean(values, axis=-1, keepdims=True)
    spread = jnp.mean(center * center, axis=-1, keepdims=True)
    return center * lax.rsqrt(spread + epsilon) * gain + offset


def gelu_tanh(values):
    return jax.nn.gelu(values, approximate=True)


def positions(coords, model_width):
    indices = jnp.arange(model_width // 4).astype(coords.dtype)
    freqs = jnp.exp(indices * (-4.0 * math.log(10000.0) / model_width))
    along_x = coords[0][:, None] * freqs[None, :]
    along_y = coords[1][:, None] * freqs[None, :]
    return jnp.concatenate(
        [jnp.sin(along_x), jnp.cos(along_x), jnp.sin(along_y), jnp.cos(along_y)], axis=1
    )


def slide_ids(slide_lengths, length_all):
    places = jnp.arange(length_all, dtype=jnp.int32)
    return (places >= slide_lengths[0]).astype(jnp.int32) + (
        places >= slide_lengths[0] + slide_lengths[1]
    ).astype(jnp.int32)


def product(left, right):
    return jnp.dot(left, right, preferred_element_type=jnp.float32)


def contract_rows(left, right):
    return lax.dot_general(
        left, right, (((0,), (0,)), ((), ())), preferred_element_type=jnp.float32
    )


def contract_cols(left, right):
    return lax.dot_general(
        left, right, (((1,), (1,)), ((), ())), preferred_element_type=jnp.float32
    )


def body(
    gene_counts,
    coords,
    lengths,
    enc_weight,
    dec_weight,
    attn_weight,
    up_weight,
    down_weight,
    ln_gain,
    ln_bias,
    logit_grad,
):
    model_width = enc_weight.shape[1]
    group_rows = gene_counts.shape[0]
    own_rows = coords.shape[1]
    gene_index = lax.axis_index("gene")
    score_scale = 1.0 / math.sqrt(HEAD_DIM)
    slide_all = slide_ids(lengths[0], group_rows)
    slide_own = lax.dynamic_slice_in_dim(slide_all, gene_index * own_rows, own_rows)
    live_rows = (slide_all < 2).astype(jnp.bfloat16)[:, None]
    attn_full, up_full, down_full, gain_full, bias_full = (
        lax.all_gather(attn_weight, ("dp", "gene"), axis=0, tiled=True),
        lax.all_gather(up_weight, ("dp", "gene"), axis=0, tiled=True),
        lax.all_gather(down_weight, ("dp", "gene"), axis=0, tiled=True),
        lax.all_gather(ln_gain, ("dp", "gene"), axis=0, tiled=True),
        lax.all_gather(ln_bias, ("dp", "gene"), axis=0, tiled=True),
    )
    norm_gains = gain_full.astype(jnp.float32)
    offsets = bias_full.astype(jnp.float32)
    proj_weight = attn_full[: 3 * model_width]
    out_weight = attn_full[3 * model_width :]
    embedded = lax.psum_scatter(
        product(gene_counts, enc_weight).astype(jnp.bfloat16),
        "gene",
        scatter_dimension=0,
        tiled=True,
    ).astype(jnp.float32)
    stream_in = embedded + positions(coords, model_width)
    first_normed, first_pull = jax.vjp(
        norm_rows, stream_in, norm_gains[:model_width], offsets[:model_width]
    )
    first_low = first_normed.astype(jnp.bfloat16)
    projected = contract_cols(first_low, proj_weight).astype(jnp.bfloat16)
    queries = projected[:, :model_width].reshape(own_rows, HEADS, HEAD_DIM)
    keyval_all = lax.all_gather(projected[:, model_width:], "gene", axis=0, tiled=True)
    keys_all = keyval_all[:, :model_width].reshape(group_rows, HEADS, HEAD_DIM)
    values_all = keyval_all[:, model_width:].reshape(group_rows, HEADS, HEAD_DIM)
    same_slide = (slide_own[:, None] == slide_all[None, :])[None]
    scores = (
        jnp.einsum("qhd,khd->hqk", queries, keys_all, preferred_element_type=jnp.float32)
        * score_scale
    )
    scores = jnp.where(same_slide, scores, -1e30)
    row_max = jnp.max(scores, axis=-1, keepdims=True)
    raised = jnp.exp(scores - row_max)
    soft = raised / jnp.sum(raised, axis=-1, keepdims=True)
    soft_low = soft.astype(jnp.bfloat16)
    attended = jnp.einsum("hqk,khd->qhd", soft_low, values_all, preferred_element_type=jnp.float32)
    attended = attended.reshape(own_rows, model_width).astype(jnp.bfloat16)
    stream_mid = stream_in + product(attended, out_weight)
    second_normed, second_pull = jax.vjp(
        norm_rows, stream_mid, norm_gains[model_width:], offsets[model_width:]
    )
    second_low = second_normed.astype(jnp.bfloat16)
    hidden_pre = contract_cols(second_low, up_full)
    active, gelu_pull = jax.vjp(gelu_tanh, hidden_pre)
    active_low = active.astype(jnp.bfloat16)
    stream_out = stream_mid + product(active_low, down_full)
    cells_low = stream_out.astype(jnp.bfloat16)
    cells_all = lax.all_gather(cells_low, "gene", axis=0, tiled=True)
    logits_full = product(cells_all, dec_weight)
    logits = (logits_full * live_rows.astype(jnp.float32)).astype(jnp.bfloat16)
    masked_grad = logit_grad * live_rows
    grad_out = lax.psum_scatter(
        contract_cols(masked_grad, dec_weight).astype(jnp.bfloat16),
        "gene",
        scatter_dimension=0,
        tiled=True,
    ).astype(jnp.float32)
    dec_part = contract_rows(cells_all, masked_grad)
    grad_branch = grad_out.astype(jnp.bfloat16)
    down_part = contract_rows(active_low, grad_branch)
    grad_active = contract_cols(grad_branch, down_full)
    grad_hidden = gelu_pull(grad_active)[0].astype(jnp.bfloat16)
    up_part = contract_rows(grad_hidden, second_low)
    grad_second = product(grad_hidden, up_full)
    grad_mid_norm, gain_second, bias_second = second_pull(grad_second)
    grad_mid = grad_out + grad_mid_norm
    grad_attn = grad_mid.astype(jnp.bfloat16)
    out_part = contract_rows(attended, grad_attn)
    grad_attended = (
        contract_cols(grad_attn, out_weight).astype(jnp.bfloat16).reshape(own_rows, HEADS, HEAD_DIM)
    )
    grad_soft = jnp.einsum(
        "qhd,khd->hqk", grad_attended, values_all, preferred_element_type=jnp.float32
    )
    grad_scores = soft * (grad_soft - jnp.sum(grad_soft * soft, axis=-1, keepdims=True))
    grad_scores = grad_scores.astype(jnp.bfloat16)
    grad_query = (
        jnp.einsum("hqk,khd->qhd", grad_scores, keys_all, preferred_element_type=jnp.float32)
        * score_scale
    )
    grad_query = grad_query.reshape(own_rows, model_width).astype(jnp.bfloat16)
    grad_keys = (
        jnp.einsum("hqk,qhd->khd", grad_scores, queries, preferred_element_type=jnp.float32)
        * score_scale
    )
    grad_values = jnp.einsum(
        "hqk,qhd->khd", soft_low, grad_attended, preferred_element_type=jnp.float32
    )
    keyval_part = jnp.concatenate(
        [grad_keys.reshape(group_rows, model_width), grad_values.reshape(group_rows, model_width)],
        axis=1,
    )
    grad_keyval = lax.psum_scatter(
        keyval_part.astype(jnp.bfloat16), "gene", scatter_dimension=0, tiled=True
    )
    grad_proj = jnp.concatenate([grad_query, grad_keyval], axis=1)
    proj_part = contract_rows(grad_proj, first_low)
    grad_first = product(grad_proj, proj_weight)
    grad_in_norm, gain_first, bias_first = first_pull(grad_first)
    grad_in = (grad_mid + grad_in_norm).astype(jnp.bfloat16)
    grad_in_all = lax.all_gather(grad_in, "gene", axis=0, tiled=True)
    gene_grad = contract_cols(grad_in_all, enc_weight).astype(jnp.bfloat16)
    enc_part = contract_rows(gene_counts, grad_in_all)
    enc_grad, dec_grad = (
        lax.psum_scatter(enc_part, "dp", scatter_dimension=1, tiled=True),
        lax.psum_scatter(dec_part, "dp", scatter_dimension=0, tiled=True),
    )
    attn_part = jnp.concatenate([proj_part, out_part], axis=0)
    gain_part = jnp.concatenate([gain_first, gain_second], axis=0)
    attn_grad, up_grad, down_grad, gain_grad, bias_grad, mid_bias_grad = (
        lax.psum_scatter(attn_part, ("dp", "gene"), scatter_dimension=0, tiled=True),
        lax.psum_scatter(up_part, ("dp", "gene"), scatter_dimension=0, tiled=True),
        lax.psum_scatter(down_part, ("dp", "gene"), scatter_dimension=0, tiled=True),
        lax.psum_scatter(gain_part, ("dp", "gene"), scatter_dimension=0, tiled=True),
        lax.psum_scatter(bias_first, ("dp", "gene"), scatter_dimension=0, tiled=True),
        lax.psum_scatter(bias_second, ("dp", "gene"), scatter_dimension=0, tiled=True),
    )
    return (
        logits,
        gene_grad,
        enc_grad,
        dec_grad,
        attn_grad,
        up_grad,
        down_grad,
        gain_grad,
        bias_grad,
        mid_bias_grad,
    )


MESH = pl.DeviceIdType.MESH
MIB = 2**20
VMEM = pl.BlockSpec(memory_space=pltpu.VMEM)
SMEM = pl.BlockSpec(memory_space=pltpu.SMEM)
ANY = pl.BlockSpec(memory_space=pl.ANY)
DMA = pltpu.SemaphoreType.DMA


class Place:
    def __init__(self):
        self.dp = dp = lax.axis_index("dp")
        self.z = z = lax.axis_index("gene")
        self.core = dp % 2
        self.chip = dp // 2
        self.inner = z * (3 - z) > 0
        self.outer = z * (3 - z) == 0
        self.pair = (dp, z + 1 - 2 * (z % 2))
        self.middle = (dp, 3 - z)
        self.sibling_dp = dp + 1 - 2 * (dp % 2)
        self.x_dp = dp + 2 - 4 * ((dp // 2) % 2)
        self.y_dp = dp + 4 - 8 * (dp // 4)
        self.xy_dp = self.x_dp + 4 - 8 * (dp // 4)
        self.sibling = (self.sibling_dp, z)
        self.far_dps = (self.x_dp, self.y_dp, self.xy_dp)
        self.far = tuple((d, z) for d in self.far_dps)
        self.x_side = (self.x_dp + self.sibling_dp - dp, z)
        self.y_side = (self.y_dp + self.sibling_dp - dp, z)
        self.xy_side = (self.xy_dp + self.sibling_dp - dp, z)
        self.plane = self.far + (self.sibling, self.x_side, self.y_side, self.xy_side)
        self.line = tuple((dp, (z + k) % 4) for k in (1, 2, 3))

    def meet(self, devices):
        barrier = pltpu.get_barrier_semaphore()
        for device in devices:
            pl.semaphore_signal(barrier, inc=1, device_id=device, device_id_type=MESH)
        pl.semaphore_wait(barrier, len(devices))

    def meet_line(self):
        barrier = pltpu.get_barrier_semaphore()
        pl.semaphore_signal(barrier, inc=1, device_id=self.pair, device_id_type=MESH)

        @pl.when(self.inner)
        def _():
            pl.semaphore_signal(barrier, inc=1, device_id=self.middle, device_id_type=MESH)
            pl.semaphore_wait(barrier, 2)

        @pl.when(self.outer)
        def _():
            pl.semaphore_wait(barrier, 1)


def send(src, dst, send_sem, recv_sem, device):
    return pltpu.make_async_remote_copy(
        src_ref=src,
        dst_ref=dst,
        send_sem=send_sem,
        recv_sem=recv_sem,
        device_id=device,
        device_id_type=MESH,
    )


class LineSum:
    SEMS = 6

    def __init__(self, place, part, inbox, peer, total, sems, view):
        self.place, self.part, self.inbox, self.peer, self.total = place, part, inbox, peer, total
        self.sems, self.view = sems, view

    def up(self, k):
        s, v = self.sems, self.view
        return send(v(self.part, k), v(self.inbox, k), s.at[0, k], s.at[1, k], self.place.pair)

    def across(self, k):
        s, v = self.sems, self.view
        return send(v(self.part, k), v(self.peer, k), s.at[2, k], s.at[3, k], self.place.middle)

    def down(self, k):
        s, v = self.sems, self.view
        return send(v(self.total, k), v(self.total, k), s.at[4, k], s.at[5, k], self.place.pair)

    def push(self, k):
        @pl.when(self.place.outer)
        def _():
            self.up(k).start()

    def meet_up(self, k):
        @pl.when(self.place.inner)
        def _():
            self.up(k).wait_recv()
            mine, other = self.view(self.part, k), self.view(self.inbox, k)
            mine[...] = (mine[...].astype(jnp.float32) + other[...].astype(jnp.float32)).astype(
                jnp.bfloat16
            )
            self.across(k).start()

    def meet_across(self, k):
        @pl.when(self.place.inner)
        def _():
            self.across(k).wait_recv()
            mine, other = self.view(self.part, k), self.view(self.peer, k)
            self.view(self.total, k)[...] = (
                mine[...].astype(jnp.float32) + other[...].astype(jnp.float32)
            ).astype(jnp.bfloat16)
            self.down(k).start()

    def get(self, k):
        @pl.when(self.place.outer)
        def _():
            self.down(k).wait_recv()

    def finish_part(self, count):
        @pl.when(self.place.outer)
        def _():
            for k in range(count):
                self.up(k).wait_send()

        @pl.when(self.place.inner)
        def _():
            for k in range(count):
                self.across(k).wait_send()

    def finish_total(self, count):
        @pl.when(self.place.inner)
        def _():
            for k in range(count):
                self.down(k).wait_send()


class Rows:
    def __init__(self, ref, base, group):
        self.ref, self.base, self.group = ref, base, group

    def slot(self, index):
        return self.ref.at[pl.ds(self.base + index * self.group, self.group)]


def lane_block(ref, k):
    return ref.at[:, pl.ds(k * 128, 128)]


def columns(ref, k, width):
    return ref.at[:, pl.ds(k * width, width)]


def row_live(lengths, rows):
    index = lax.broadcasted_iota(jnp.int32, (rows, 1), 0)
    return (index < lengths[0, 0] + lengths[0, 1]).astype(jnp.float32)


def exact(value):
    return value.astype(jnp.float32)


def low(value):
    return value.astype(jnp.bfloat16)


def rows_of(ref, k):
    return ref.at[pl.ds(k * 64, 64)]


def normalize(values):
    center = values - jnp.mean(values, axis=-1, keepdims=True)
    spread = jnp.mean(center * center, axis=-1, keepdims=True)
    scale = lax.rsqrt(spread + epsilon)
    return center * scale, scale


def norm_back(grad, gain, normed, scale):
    lifted = grad * gain
    return scale * (
        lifted
        - jnp.mean(lifted, axis=-1, keepdims=True)
        - normed * jnp.mean(lifted * normed, axis=-1, keepdims=True)
    )


def gelu_both(u):
    curve, factor = 0.044715, math.sqrt(2.0 / math.pi)
    square = u * u
    bent = jnp.tanh(factor * (u + curve * u * square))
    half = 0.5 * (1.0 + bent)
    slope = half + 0.5 * u * (1.0 - bent * bent) * (factor * (1.0 + 3.0 * curve * square))
    return u * half, slope


def layer_kernel(
    coords,
    lengths,
    counts,
    enc,
    slopes,
    dec,
    attn_own,
    up_own,
    down_own,
    gain_own,
    bias_own,
    cells,
    grad_in,
    cells_four,
    grad_four,
    grads,
    sums_all,
    counts_side,
    slopes_side,
    counts_far,
    slopes_far,
    weights,
    vectors,
    counts_v,
    enc_v,
    slopes_v,
    dec_v,
    work,
    places,
    qkv,
    soft,
    key_sum,
    value_sum,
    gains,
    offsets,
    part_m,
    part_o,
    part_s,
    inbox_m,
    inbox_o,
    peer_m,
    peer_o,
    peer_s,
    stream,
    total_m,
    total_o,
    total_s,
    branch_rows,
    outgoing,
    arriving,
    sums,
    sums_box,
    load_sems,
    line_sems,
    gather_sems,
    vector_sems,
    tile_sems,
    side_sems,
    far_sems,
    pair_sems,
    four_sems,
    sums_sems,
    ready_sem,
):
    place = Place()
    group, width = cells.shape
    dp, z = place.dp, place.z
    step = width // 4
    local = width // 4
    span = 128
    parts = group // span
    lane = lax.broadcasted_iota(jnp.int32, (1, span), 1)
    head_lanes = [low((lane // HEAD_DIM == h).astype(jnp.float32)) for h in range(2)]
    head_exact = [exact(h) for h in head_lanes]
    first_end, second_end = lengths[0, 0], lengths[0, 0] + lengths[0, 1]

    def slide_of(index):
        return (index >= first_end).astype(jnp.int32) + (index >= second_end).astype(jnp.int32)

    def rows(r):
        return slice(r * span, (r + 1) * span)

    def row_index(r):
        return lax.broadcasted_iota(jnp.int32, (span, 1), 0) + r * span

    def matrix(i, start, stop):
        return weights[i, start:stop].reshape((stop - start) * span, width)

    first, attn, cat = [Rows(enc_v, i * 2 * group, group) for i in range(3)]
    active, hidden, second = [Rows(dec_v, i * 2 * group, group) for i in range(3)]

    def key_masked(p):
        return counts_v.at[pl.ds(0, 2 * group), pl.ds(p * span, span)]

    def value_masked(p):
        return counts_v.at[pl.ds(0, 2 * group), pl.ds((2 + p) * span, span)]

    def staged(i, t):
        return counts_v.at[pl.ds((2 + t) * group, group), pl.ds(i * 2 * span, 2 * span)]

    def side_copy(ref, i):
        return send(
            ref.slot(0), ref.slot(1), side_sems.at[0, i], side_sems.at[1, i], place.sibling
        )

    side_active, side_hidden, side_second = [
        side_copy(ref, i) for i, ref in enumerate((active, hidden, second))
    ]
    side_cat, side_first, side_attn = [
        side_copy(ref, 4 + i) for i, ref in enumerate((cat, first, attn))
    ]
    side_branch = send(
        branch_rows.at[0], branch_rows.at[1], side_sems.at[0, 3], side_sems.at[1, 3], place.sibling
    )

    pair_far = [
        send(src, dst.at[0], pair_sems.at[0, i], pair_sems.at[1, i], device)
        for i, (src, dst, device) in enumerate(
            ((counts, counts_far, place.far[1]), (slopes, slopes_far, place.far[0]))
        )
    ]
    pair_side = [
        send(dst.at[0], dst.at[1], pair_sems.at[0, 2 + i], pair_sems.at[1, 2 + i], place.sibling)
        for i, dst in enumerate((counts_far, slopes_far))
    ]
    cells_to = (place.sibling, place.far[0], place.x_side)
    grad_to = (place.sibling, place.far[1], place.y_side)

    def other_core(d):
        return d + 1 - 2 * (d % 2)

    x_dp, y_dp, xy_dp = place.far_dps
    own_pair, x_pair, y_pair = (place.dp, y_dp), (x_dp, xy_dp), (place.dp, x_dp)
    cells_blocks = (own_pair, tuple(map(other_core, own_pair)), x_pair, tuple(map(other_core, x_pair)))
    x_row = (y_dp, xy_dp)
    grad_blocks = (y_pair, tuple(map(other_core, y_pair)), x_row, tuple(map(other_core, x_row)))

    def four_copy(i, four, devices, t, r):
        block = pl.ds(r * span, span)
        return send(
            staged(i, t).at[block],
            four.at[1 + t, block],
            four_sems.at[0, i, t, r],
            four_sems.at[1, i, t, r],
            devices[t],
        )

    def cells_copy(t, r):
        return four_copy(0, cells_four, cells_to, t, r)

    def grad_copy(t, r):
        return four_copy(1, grad_four, grad_to, t, r)

    def spread(ref, i, four, blocks, copy, r):
        for t, pair in enumerate(blocks):
            for n, d in enumerate(pair):
                block = ref[rows(r), pl.ds(pl.multiple_of(d * span, span), span)]
                at = slice(n * span, (n + 1) * span)
                if t == 0:
                    four[0, rows(r), at] = block
                else:
                    staged(i, t - 1)[rows(r), at] = block
            if t > 0:
                copy(t - 1, r).start()

    def line_sum(i, part, inbox, peer, total, view):
        return LineSum(place, part, inbox, peer, total, line_sems.at[i], view)

    sum_a = line_sum(0, part_m, inbox_m, peer_s, stream, lane_block)
    sum_b = line_sum(1, part_o, inbox_o, peer_o, branch_rows.at[0], lane_block)
    sum_m = line_sum(2, part_m, inbox_m, peer_m, total_m, rows_of)
    sum_o = line_sum(3, part_o, inbox_o, peer_o, total_o, rows_of)
    sum_s = line_sum(4, part_s, inbox_m, peer_s, total_s, rows_of)
    sum_f = line_sum(5, part_s, inbox_m, peer_m, total_s, rows_of)
    all_sums = dict(a=sum_a, b=sum_b, m=sum_m, o=sum_o, s=sum_s, f=sum_f)

    def loads_of(table, table_v, wide, wide_v, i):
        found = [pltpu.make_async_copy(table, table_v, load_sems.at[i, 0])]
        for j in range(4):
            found.append(
                pltpu.make_async_copy(
                    columns(wide, j, step), columns(wide_v, j, step), load_sems.at[i, 1 + j]
                )
            )
        return found

    loads = [
        loads_of(counts, counts_v, enc, enc_v, 0),
        loads_of(slopes, slopes_v, dec, dec_v, 1),
    ]
    for copy in loads[0] + loads[1]:
        copy.start()
    for i, ref in enumerate((attn_own, up_own, down_own)):
        weights[i, dp] = ref[...]
    tile = vectors.at[dp * 4 + z]
    tile[...] = jnp.zeros_like(tile)
    tile[0:1, 0:64] = exact(gain_own[...])
    tile[1:2, 0:64] = exact(bias_own[...])
    place.meet(place.plane + place.line)

    line_out = [
        send(tile, tile, tile_sems.at[0, i], tile_sems.at[1, i], device)
        for i, device in enumerate(place.line)
    ]
    for copy in line_out:
        copy.start()

    def weight_far(i, q, d):
        block = weights.at[i, d]
        return send(
            block, block, gather_sems.at[0, i, q], gather_sems.at[1, i, q], place.far[q]
        )

    def weight_side(i, q):
        block = weights.at[i, ((dp,) + place.far_dps)[q]]
        return send(
            block, block, gather_sems.at[2, i, q], gather_sems.at[3, i, q], place.sibling
        )

    def tiles(d):
        return vectors.at[pl.ds(d * 4, 4)]

    vec_far = [
        send(tiles(dp), tiles(dp), vector_sems.at[0, q], vector_sems.at[1, q], device)
        for q, device in enumerate(place.far)
    ]
    vec_side = [
        send(tiles(d), tiles(d), vector_sems.at[2, q], vector_sems.at[3, q], place.sibling)
        for q, d in enumerate((dp,) + place.far_dps)
    ]
    def weights_out(some):
        for i in some:
            for q in range(3):
                weight_far(i, q, dp).start()
            weight_side(i, 0).start()

    weights_out((0,))
    own_side = [
        send(src, dst, pair_sems.at[0, 4 + i], pair_sems.at[1, 4 + i], place.sibling)
        for i, (src, dst) in enumerate(((counts_v, counts_side), (slopes_v, slopes_side)))
    ]

    own_rows = coords.shape[1]
    index = lax.broadcasted_iota(jnp.int32, (1, step), 1).astype(jnp.float32)
    freqs = jnp.exp(index * (-4.0 * math.log(10000.0) / width))
    for axis in range(2):
        along = jnp.broadcast_to(coords[axis : axis + 1, :], (own_rows, own_rows)).T
        angle = along[:, 0:1] * freqs
        places[2 * axis] = jnp.sin(angle)
        places[2 * axis + 1] = jnp.cos(angle)
    own = pl.ds(pl.multiple_of(z * own_rows, own_rows), own_rows)
    sums[...] = jnp.zeros_like(sums)
    key_sum[...] = jnp.zeros_like(key_sum)
    value_sum[...] = jnp.zeros_like(value_sum)

    def vectors_on(k):
        if k == 0:
            for copy in line_out:
                copy.wait_recv()
            for copy in vec_far + vec_side[:1]:
                copy.start()
            weights_out((1, 2))
            for copy in pair_far:
                copy.start()
        if k == 1:
            for q in range(3):
                vec_far[q].wait_recv()
                vec_side[1 + q].start()
        if k == 2:
            for copy in vec_side:
                copy.wait_recv()
            for n in range(2 * width // span):
                for ref, row in ((gains, 0), (offsets, 1)):
                    ref[0:1, n * span : (n + 1) * span] = jnp.concatenate(
                        [vectors[2 * n + i, row : row + 1, 0:64] for i in range(2)], axis=1
                    )

    def weights_on(some, k):
        for i in some:
            if k == 0:
                for q, d in enumerate(place.far_dps):
                    weight_far(i, q, d).wait_recv()
                    weight_side(i, 1 + q).start()
            else:
                for q in range(4):
                    weight_side(i, q).wait_recv()

    def encode(j):
        if j == 0:
            loads[0][0].wait()
            own_side[0].start()
        loads[0][1 + j].wait()
        work[...] = contract_rows(counts_v[...], enc_v[:, j * step : (j + 1) * step])
        work[own, :] += places[j]
        part_m[:, j * step : (j + 1) * step] = low(work[...])
        for k in range(2 * j, 2 * j + 2):
            sum_a.push(k)

    def decode(j):
        if j == 0:
            loads[1][0].wait()
            own_side[1].start()
        loads[1][1 + j].wait()
        live = (lax.broadcasted_iota(jnp.int32, (group, 1), 0) < second_end).astype(jnp.float32)
        part_o[:, j * step : (j + 1) * step] = low(
            contract_rows(slopes_v[...], dec_v[:, j * step : (j + 1) * step]) * live
        )

    def project(r):
        gain_a, offset_a = gains[0:1, :width], offsets[0:1, :width]
        if r == 0:
            for k in range(8):
                sum_a.get(k)
            own_side[0].wait_send()
            pl.semaphore_signal(
                ready_sem, inc=1, device_id=place.sibling, device_id_type=MESH
            )
        normed, _ = normalize(exact(stream[rows(r), :]))
        value = low(normed * gain_a + offset_a)
        first.slot(0)[rows(r), :] = value
        qkv[rows(r), :] = low(contract_cols(value, matrix(0, 0, 6)))
        for p in range(2):
            for ref, at in ((key_masked(p), local), (value_masked(p), 2 * local)):
                block = qkv[rows(r), at + p * span : at + (p + 1) * span]
                for h in range(2):
                    ref[h * group + r * span : h * group + (r + 1) * span, :] = (
                        block * head_lanes[h]
                    )

    def attend(r):
        if r == 0:
            pl.semaphore_wait(ready_sem, 1)
            side_first.start()
            sum_a.finish_part(8)
        same = slide_of(row_index(r)) == slide_of(
            lax.broadcasted_iota(jnp.int32, (1, group), 1)
        )
        for p in range(2):
            query = qkv[rows(r), p * span : (p + 1) * span]
            scores = contract_cols(query, key_masked(p)[...]) * (1.0 / math.sqrt(HEAD_DIM))
            for h in range(2):
                own = jnp.where(same, scores[:, h * group : (h + 1) * group], -1e30)
                raised = jnp.exp(own - jnp.max(own, axis=-1, keepdims=True))
                soft[p, rows(r), h * group : (h + 1) * group] = low(
                    raised / jnp.sum(raised, axis=-1, keepdims=True)
                )
            cat.slot(0)[rows(r), 3 * local + p * span : 3 * local + (p + 1) * span] = low(
                product(soft[p, rows(r), :], value_masked(p)[...])
            )
        part_m[rows(r), :] = low(product(cat.slot(0)[rows(r), 3 * local :], matrix(0, 6, 8)))
        push(sum_m, r)

    def middle(r):
        return exact(stream[rows(r), :]) + exact(total_m[rows(r), :])

    def feed(r):
        gain_b, offset_b = gains[0:1, width:], offsets[0:1, width:]
        if r == 0:
            for k in range(8):
                sum_b.get(k)
            sum_b.finish_part(8)
        get(sum_m, r)
        normed, _ = normalize(middle(r))
        value = low(normed * gain_b + offset_b)
        second.slot(0)[rows(r), :] = value
        act, slope = gelu_both(contract_cols(value, matrix(1, 0, 8)))
        active.slot(0)[rows(r), :] = low(act)
        grad = branch_rows[0, rows(r), :]
        back = low(contract_cols(grad, matrix(2, 0, 8)) * slope)
        hidden.slot(0)[rows(r), :] = back
        part_s[rows(r), :] = low(product(back, matrix(1, 0, 8)))
        push(sum_s, r)
        part_o[rows(r), :] = low(product(active.slot(0)[rows(r), :], matrix(2, 0, 8)))

    def attend_back(r):
        gain_b = gains[0:1, width:]
        get(sum_s, r)
        normed, scale = normalize(middle(r))
        grad = exact(total_s[rows(r), :])
        sums[1:2, :] += jnp.sum(grad * normed, axis=0, keepdims=True)
        sums[3:4, :] += jnp.sum(grad, axis=0, keepdims=True)
        mid = exact(branch_rows[0, rows(r), :]) + norm_back(grad, gain_b, normed, scale)
        attn.slot(0)[rows(r), :] = low(mid)
        back = low(contract_cols(low(mid), matrix(0, 6, 8)))
        for p in range(2):
            out = back[:, p * span : (p + 1) * span]
            slopes = contract_cols(out, value_masked(p)[...])
            marks = []
            for h in range(2):
                block = exact(soft[p, rows(r), h * group : (h + 1) * group])
                slope = slopes[:, h * group : (h + 1) * group]
                inner = jnp.sum(slope * block, axis=-1, keepdims=True)
                marks.append(low(block * (slope - inner)))
            scale_q = 1.0 / math.sqrt(HEAD_DIM)
            cat.slot(0)[rows(r), p * span : (p + 1) * span] = low(
                product(jnp.concatenate(marks, axis=1), key_masked(p)[...]) * scale_q
            )
            query = qkv[rows(r), p * span : (p + 1) * span]
            at = slice(p * span, (p + 1) * span)
            key_sum[:, at] += contract_rows(
                jnp.concatenate(marks, axis=0),
                jnp.concatenate([query * lanes for lanes in head_lanes], axis=0),
            )
            value_sum[:, at] += contract_rows(
                jnp.concatenate(
                    [soft[p, rows(r), h * group : (h + 1) * group] for h in range(2)], axis=0
                ),
                jnp.concatenate([out * lanes for lanes in head_lanes], axis=0),
            )

    def project_back(r):
        if r == 0:
            sum_s.finish_part(8)
            sum_s.finish_total(8)
            cat.slot(0)[:, local : 2 * local] = low(key_sum[...] * (1.0 / math.sqrt(HEAD_DIM)))
            cat.slot(0)[:, 2 * local : 3 * local] = low(value_sum[...])
        part_s[rows(r), :] = low(product(cat.slot(0)[rows(r), : 3 * local], matrix(0, 0, 6)))
        push(sum_f, r)

    def finish_in(r):
        gain_a = gains[0:1, :width]
        get(sum_f, r)
        normed, scale = normalize(exact(stream[rows(r), :]))
        grad = exact(total_s[rows(r), :])
        sums[0:1, :] += jnp.sum(grad * normed, axis=0, keepdims=True)
        sums[2:3, :] += jnp.sum(grad, axis=0, keepdims=True)
        grad_in[rows(r), :] = low(
            exact(attn.slot(0)[rows(r), :]) + norm_back(grad, gain_a, normed, scale)
        )
        spread(grad_in, 1, grad_four, grad_blocks, grad_copy, r)

    def finish_out(r):
        get(sum_o, r)
        live = (row_index(r) < second_end).astype(jnp.float32)
        cells[rows(r), :] = low((middle(r) + exact(total_o[rows(r), :])) * live)
        spread(cells, 0, cells_four, cells_blocks, cells_copy, r)

    def push(total, r):
        total.push(2 * r)
        total.push(2 * r + 1)

    def get(total, r):
        total.get(2 * r)
        total.get(2 * r + 1)

    chips = tuple(d // 2 for d in place.far_dps) + (place.chip,)

    def lanes_of(ref, slot, chip):
        start = pl.multiple_of((chip * 2 + place.core) * span, span)
        return ref.slot(slot)[:, pl.ds(start, span)]

    def far_copy(i, q):
        return send(
            outgoing.at[i, q],
            arriving.at[i, q],
            far_sems.at[0, i, q],
            far_sems.at[1, i, q],
            place.far[q],
        )

    def keep(i, q, value):
        if q == 3:
            grads[i] = value
        else:
            outgoing[i, q] = low(value)
            far_copy(i, q).start()

    def weight_grad(i, left, right, half):
        pair = chips[2 * half : 2 * half + 2]
        got = sum(
            contract_rows(
                jnp.concatenate([lanes_of(left, slot, chip) for chip in pair], axis=1),
                right(slot),
            )
            for slot in range(2)
        )
        for k in range(2):
            keep(i, 2 * half + k, got[k * span : (k + 1) * span])

    def attn_right(kind, slot):
        start = pl.multiple_of(kind * 2 * group + slot * group, group)
        return enc_v[pl.ds(start, group), :]

    def attn_grad(q):
        kind = chips[q] // 3
        keep(
            0,
            q,
            sum(
                contract_rows(lanes_of(cat, slot, chips[q]), attn_right(kind, slot))
                for slot in range(2)
            ),
        )

    def run(word):
        name, k = word[:-1], int(word[-1])
        if name[0] in "ux":
            total = all_sums[name[1]]
            (total.meet_up if name[0] == "u" else total.meet_across)(k)
        else:
            steps[name](k)

    def start_feed_sides(_):
        for copy in (side_hidden, side_second, side_active, side_branch):
            copy.start()

    def start_attn_sides(_):
        side_cat.start()
        side_attn.start()

    def pass_on(i):
        pair_far[i].wait_recv()
        pair_side[i].start()

    def up_grad(half):
        if half == 0:
            side_hidden.wait_recv()
            side_second.wait_recv()
        weight_grad(1, hidden, lambda slot: second.slot(slot)[...], half)

    def down_grad(half):
        if half == 0:
            side_active.wait_recv()
            side_branch.wait_recv()
        weight_grad(2, active, lambda slot: branch_rows[slot], half)

    def attn_grads(half):
        if half == 0:
            side_first.wait_recv()
            side_attn.wait_recv()
            side_cat.wait_recv()
        attn_grad(2 * half)
        attn_grad(2 * half + 1)

    def push_branch(j):
        sum_b.push(2 * j)
        sum_b.push(2 * j + 1)

    steps = dict(
        N=encode,
        M=decode,
        Q=push_branch,
        V=vectors_on,
        W=functools.partial(weights_on, (0,)),
        Y=functools.partial(weights_on, (1, 2)),
        A=project,
        B=attend,
        C=feed,
        D=attend_back,
        G=project_back,
        E=finish_in,
        F=finish_out,
        P=lambda r: push(sum_o, r),
        S=start_feed_sides,
        T=start_attn_sides,
        X=pass_on,
        H=up_grad,
        L=down_grad,
        K=attn_grads,
    )
    for word in SCHEDULE:
        run(word)
    sums_out = [
        send(sums, sums_box.at[i], sums_sems.at[0, i], sums_sems.at[1, i], device)
        for i, device in enumerate(place.plane)
    ]
    for copy in sums_out:
        copy.start()
    for i in (2, 1, 0):
        for q in range(3):
            far_copy(i, q).wait_recv()
        grads[i] = grads[i] + sum(exact(arriving[i, q]) for q in range(3))
    for copy in sums_out:
        copy.wait()
    sums_all[...] = sums[...] + sum(sums_box[i] for i in range(len(sums_out)))
    for total in (sum_m, sum_o, sum_f):
        total.finish_part(8)
    for total in (sum_a, sum_b, sum_m, sum_o, sum_f):
        total.finish_total(8)
    for i in range(3):
        for q in range(3):
            weight_far(i, q, dp).wait_send()
        for q in range(4):
            weight_side(i, q).wait_send()
    for copy in line_out + vec_far + vec_side:
        copy.wait_send()
    own_side[0].wait_recv()
    own_side[1].wait()
    for i in range(3):
        for q in range(3):
            far_copy(i, q).wait_send()
    for t in range(3):
        for r in range(parts):
            cells_copy(t, r).wait()
            grad_copy(t, r).wait()
    for copy in pair_far:
        copy.wait_send()
    for copy in pair_side:
        copy.wait()
    for copy in (
        side_active,
        side_hidden,
        side_second,
        side_branch,
        side_cat,
        side_first,
        side_attn,
    ):
        copy.wait_send()


SCHEDULE = (
    "N0", "M0", "N1", "ua0", "ua1", "Q0", "M1", "xa0", "ua2", "ua3", "V0", "xa1", "N2", "ub0",
    "N3", "V1", "xa2", "ub1", "W0", "M2", "xa3", "V2", "ua4", "Q1", "xb0", "ua5", "M3", "xa4",
    "ua6", "Q2", "ua7", "xa5", "ub2", "xa6", "ub3", "xa7", "xb1", "Q3", "ub4", "xb2", "ub5",
    "xb3", "W1", "A0", "ub6", "A1", "xb4", "xb5", "A2", "ub7", "A3", "B0", "um0", "xb6", "B1",
    "um1", "xb7", "B2", "um2", "xm0", "xm1", "Y0", "um3", "B3", "xm2", "um4", "xm3", "um5", "Y1",
    "C0", "xm4", "um6", "um7", "xm5", "C1", "us0", "xm6", "us1", "xm7", "C2", "us2", "xs0", "us3",
    "xs1", "C3", "xs2", "us4", "us5", "S0", "P0", "xs3", "P1", "D0", "us6", "xs4", "D1", "xs5",
    "us7", "D2", "uo0", "xs6", "xs7", "uo1", "P2", "H0", "xo0", "uo2", "D3", "xo1", "uo3", "G0",
    "uo4", "xo2", "G1", "T0", "F0", "uo5", "xo3", "L0", "uf0", "H1", "xo4", "uf1", "xo5", "uf2",
    "P3", "xf0", "L1", "G2", "uf3", "xf1", "uo6", "G3", "xf2", "F1", "K0", "uo7", "xf3", "F2",
    "xo6", "uf4", "uf5", "xo7", "E0", "xf4", "uf6", "K1", "E1", "xf5", "uf7", "xf6", "xf7", "X0",
    "X1", "E2", "F3", "E3",
)


def layer_call(coords, lengths, counts, enc, slopes, dec, attn, up, down, gain, bias):
    genes, group = counts.shape
    width = enc.shape[1]
    half, full = jnp.bfloat16, jnp.float32
    plain = pltpu.VMEM((group, width), half)
    table, wide = pltpu.VMEM((genes, group), half), pltpu.VMEM((genes, width), half)
    return pl.pallas_call(
        layer_kernel,
        out_shape=(
            jax.ShapeDtypeStruct((group, width), half),
            jax.ShapeDtypeStruct((group, width), half),
            jax.ShapeDtypeStruct((4, group, 256), half),
            jax.ShapeDtypeStruct((4, group, 256), half),
            jax.ShapeDtypeStruct((3, 128, width), full),
            jax.ShapeDtypeStruct((8, width), full),
            jax.ShapeDtypeStruct(counts.shape, half),
            jax.ShapeDtypeStruct(slopes.shape, half),
            jax.ShapeDtypeStruct((2,) + counts.shape, half),
            jax.ShapeDtypeStruct((2,) + slopes.shape, half),
        ),
        in_specs=[VMEM, SMEM, ANY, ANY, ANY, ANY] + [VMEM] * 5,
        out_specs=(VMEM,) * 6 + (ANY,) * 4,
        scratch_shapes=[
            pltpu.VMEM((3, 8) + attn.shape, half),
            pltpu.VMEM((32, 8, 128), full),
            table,
            wide,
            table,
            wide,
            pltpu.VMEM((group, width // 4), full),
            pltpu.VMEM((4, coords.shape[1], width // 4), full),
            pltpu.VMEM((group, 3 * width // 4), half),
            pltpu.VMEM((2, group, 2 * group), half),
            pltpu.VMEM((group, width // 4), full),
            pltpu.VMEM((group, width // 4), full),
            pltpu.VMEM((1, 2 * width), full),
            pltpu.VMEM((1, 2 * width), full),
        ]
        + [plain] * 12
        + [
            pltpu.VMEM((2, group, width), half),
            pltpu.VMEM((3, 3, 128, width), half),
            pltpu.VMEM((3, 3, 128, width), half),
            pltpu.VMEM((8, width), full),
            pltpu.VMEM((7, 8, width), full),
            DMA((2, 5)),
            DMA((6, 6, 8)),
            DMA((4, 3, 4)),
            DMA((4, 4)),
            DMA((2, 3)),
            DMA((2, 7)),
            DMA((2, 3, 3)),
            DMA((2, 6)),
            DMA((2, 2, 3, 4)),
            DMA((2, 7)),
            pltpu.SemaphoreType.REGULAR,
        ],
        compiler_params=pltpu.CompilerParams(
            collective_id=1, has_side_effects=True, vmem_limit_bytes=60 * MIB
        ),
        name="layer",
    )(coords, lengths, counts, enc, slopes, dec, attn, up, down, gain, bias)


GENE_STEP = 848


def parts_kernel(own, side, far, right, kept, sent):
    lefts = (own[...], side[...], far[0], far[1])
    got = sum(product(left, right[t]) for t, left in enumerate(lefts))
    kept[...] = got[:, :128]
    sent[...] = low(got[:, 128:])


def parts_call(own, side, far, right):
    genes, group = own.shape
    flat = pl.BlockSpec((GENE_STEP, group), lambda i: (i, 0))
    pair = pl.BlockSpec((2, GENE_STEP, group), lambda i: (0, i, 0))
    four = pl.BlockSpec(right.shape, lambda i: (0, 0, 0))
    return pl.pallas_call(
        parts_kernel,
        out_shape=(
            jax.ShapeDtypeStruct((genes, 128), jnp.float32),
            jax.ShapeDtypeStruct((genes, 128), jnp.bfloat16),
        ),
        grid=(-(-genes // GENE_STEP),),
        in_specs=[flat, flat, pair, four],
        out_specs=(pl.BlockSpec((GENE_STEP, 128), lambda i: (i, 0)),) * 2,
        cost_estimate=pl.CostEstimate(
            flops=8 * genes * group * 256,
            bytes_accessed=8 * genes * group + 6 * genes * 128,
            transcendentals=0,
        ),
        compiler_params=pltpu.CompilerParams(vmem_limit_bytes=60 * MIB),
        name="parts",
    )(own, side, far, right)


def expand_kernel(enc, dec, cells, grad_in, logits, gene_grad):
    logits[...] = low(contract_cols(dec[...], cells[...]))
    gene_grad[...] = low(contract_cols(enc[...], grad_in[...]))


def expand_call(enc, dec, cells, grad_in):
    genes, width = enc.shape
    group = cells.shape[0]
    steps = -(-genes // GENE_STEP)
    half = jax.ShapeDtypeStruct((genes, group), jnp.bfloat16)
    table = pl.BlockSpec((GENE_STEP, width), lambda i: (i, 0))
    whole = pl.BlockSpec((group, width), lambda i: (0, 0))
    return pl.pallas_call(
        expand_kernel,
        out_shape=(half, half),
        grid=(steps,),
        in_specs=[table, table, whole, whole],
        out_specs=(pl.BlockSpec((GENE_STEP, group), lambda i: (i, 0)),) * 2,
        cost_estimate=pl.CostEstimate(
            flops=4 * genes * group * width,
            bytes_accessed=4 * genes * (width + group),
            transcendentals=0,
        ),
        compiler_params=pltpu.CompilerParams(vmem_limit_bytes=60 * MIB),
        name="expand",
    )(enc, dec, cells, grad_in)


def swap(values, bit):
    return lax.ppermute(values, "dp", [(d, d ^ bit) for d in range(8)])


def fast_body(
    gene_counts,
    coords,
    lengths,
    enc_weight,
    dec_weight,
    attn_weight,
    up_weight,
    down_weight,
    ln_gain,
    ln_bias,
    logit_grad,
):
    model_width = enc_weight.shape[1]
    counts, slopes, dec = gene_counts.T, logit_grad.T, dec_weight.T
    (
        cells,
        grad_in,
        cells_four,
        grad_four,
        layer_grad,
        sums,
        counts_side,
        slopes_side,
        counts_far,
        slopes_far,
    ) = layer_call(
        coords,
        lengths,
        counts,
        enc_weight,
        slopes,
        dec,
        attn_weight,
        up_weight,
        down_weight,
        ln_gain[None],
        ln_bias[None],
    )
    enc_own, enc_out = parts_call(counts, counts_side, counts_far, grad_four)
    enc_came = swap(enc_out, 2)
    cells_four, _ = lax.optimization_barrier((cells_four, enc_out))
    dec_own, dec_out = parts_call(slopes, slopes_side, slopes_far, cells_four)
    dec_came = swap(dec_out, 4)
    cells, grad_in, _ = lax.optimization_barrier((cells, grad_in, dec_out))
    logits, gene_grad = expand_call(enc_weight, dec, cells, grad_in)
    enc_grad = enc_own + enc_came.astype(jnp.float32)
    dec_grad = dec_own + dec_came.astype(jnp.float32)
    small = sums[:4].reshape(-1)
    place = lax.axis_index("dp") * 4 + lax.axis_index("gene")
    gain_grad = lax.dynamic_slice_in_dim(small[: 2 * model_width], place * 64, 64)
    bias_grad = lax.dynamic_slice_in_dim(
        small[2 * model_width : 3 * model_width], place * 32, 32
    )
    mid_bias_grad = lax.dynamic_slice_in_dim(small[3 * model_width :], place * 32, 32)
    return (
        logits.T,
        gene_grad.T,
        enc_grad,
        dec_grad.T,
        layer_grad[0],
        layer_grad[1],
        layer_grad[2],
        gain_grad,
        bias_grad,
        mid_bias_grad,
    )


def solution(mesh):
    fast = dict(mesh.shape) == {"dp": 8, "gene": 4}
    in_specs = (
        P("dp", "gene"),
        P(None, ("dp", "gene")),
        P("dp", None),
        P("gene", None),
        P(None, "gene"),
        P(("dp", "gene"), None),
        P(("dp", "gene"), None),
        P(("dp", "gene"), None),
        P(("dp", "gene")),
        P(("dp", "gene")),
        P("dp", "gene"),
    )
    out_specs = (
        P("dp", "gene"),
        P("dp", "gene"),
        P("gene", "dp"),
        P("dp", "gene"),
        P(("dp", "gene"), None),
        P(("dp", "gene"), None),
        P(("dp", "gene"), None),
        P(("dp", "gene")),
        P(("dp", "gene")),
        P(("dp", "gene")),
    )
    return jax.shard_map(
        fast_body if fast else body, mesh=mesh, in_specs=in_specs, out_specs=out_specs, check_vma=False)
```
